32 devices in a mesh: wide: 8 (over z, y), narrow: 4 (over x, core).
Axes of the slice: x: 2, y: 2, z: 4, core: 2. Of those that a mesh axis runs over, the one named last changes fastest.
Arguments:
- layer_input: bfloat16 [8, 2048, 1024], P(None, ('wide', 'narrow')), may hold values from -6 to 6
- query_weight: bfloat16 [1024, 1024], P('wide', 'narrow'), may hold values from -0.1875 to 0.1875
- key_weight: bfloat16 [1024, 1024], P('wide', 'narrow'), may hold values from -0.1875 to 0.1875
- value_weight: bfloat16 [1024, 1024], P('wide', 'narrow'), may hold values from -0.1875 to 0.1875
- modulate_weight: bfloat16 [1024, 1024], P('wide', 'narrow'), may hold values from -0.1875 to 0.1875
- output_weight: bfloat16 [1024, 1024], P('wide', 'narrow'), may hold values from -0.1875 to 0.1875
- gate_matrix: bfloat16 [1024, 2816], P(None, ('wide', 'narrow')), may hold values from -0.1875 to 0.1875
- lift_matrix: bfloat16 [1024, 2816], P(None, ('wide', 'narrow')), may hold values from -0.1875 to 0.1875
- down_matrix: bfloat16 [1024, 2816], P(None, ('wide', 'narrow')), may hold values from -0.109375 to 0.109375
- decay_factor: float32 [8], P('narrow'), may hold values from 0.96 to 1, as said below
- valid_lengths: int32 [8], replicated, may hold values from 512 to 2048, as said below
- output_cotangent: bfloat16 [8, 2048, 1024], P(None, ('wide', 'narrow')), may hold values from -6 to 6
Outputs:
- layer_output: bfloat16 [8, 2048, 1024], P(None, ('wide', 'narrow'))
- input_gradient: float32 [8, 2048, 1024], P(None, ('wide', 'narrow'))
- query_gradient: float32 [1024, 1024], P('wide', 'narrow')
- key_gradient: float32 [1024, 1024], P('wide', 'narrow')
- value_gradient: float32 [1024, 1024], P('wide', 'narrow')
- modulate_gradient: float32 [1024, 1024], P('wide', 'narrow')
- output_gradient: float32 [1024, 1024], P('wide', 'narrow')
- gate_gradient: float32 [1024, 2816], P(None, ('wide', 'narrow'))
- lift_gradient: float32 [1024, 2816], P(None, ('wide', 'narrow'))
- down_gradient: float32 [1024, 2816], P(None, ('wide', 'narrow'))
The draws below stay inside these ranges and needn't reach their ends.
Inputs may be any that keep to these rules, and one draw needn't show every extreme that they name: `decay_factor`: decay per position of each head, below one. `valid_lengths`: valid positions of each slot; in every draw one slot, drawn from the seed, is full (2048 positions).
All inputs are finite; a program needn't handle non-finite values.
Results may differ from the reference program's by a relative error of at most 0.014.
Values may be sent and summed in bfloat16 or wider, within the bound.
No kernel may reach another device: no remote copies, remote signals or barrier semaphores. Data moves between devices by JAX's collectives and lax.ppermute only.
A program may use at most 256 MiB of HBM per device.

```python
import math
import jax
import jax.numpy as jnp
from jax import lax

D = 1024
H = 8
FF = 2816
SEQS = 8
L_DEV = 256
L = 2048


def draw_decay_factor(key, part):
    key = jax.random.fold_in(key, 7)
    slow_key, fast_key, order_key = jax.random.split(key, 3)
    slow_rate = jnp.exp(jax.random.uniform(slow_key, (H,), jnp.float32, math.log(0.2 / L), math.log(2.0 / L)))
    fast_rate = jnp.exp(jax.random.uniform(fast_key, (H,), jnp.float32, math.log(1.0 / 50.0), math.log(1.0 / 30.0)))
    ranking = jax.random.permutation(order_key, H)
    slow_count = H // 2
    decay_rate = jnp.where(ranking < slow_count, slow_rate, fast_rate)
    return jnp.exp(-decay_rate).astype(jnp.float32)


def draw_valid_lengths(key, part):
    key = jax.random.fold_in(key, 11)
    length_key, full_key = jax.random.split(key)
    drawn_length = jax.random.randint(length_key, (SEQS,), L // 4, L + 1)
    chosen = jax.random.randint(full_key, (), 0, SEQS)
    return jnp.where(jnp.arange(SEQS) == chosen, L, drawn_length).astype(jnp.int32)


def levels(stream_key, extent, shards, low, high):
    def one(position, blocks):
        draws = jax.random.uniform(jax.random.fold_in(jax.random.fold_in(stream_key, 6), position), (blocks,), jnp.float32, low / len(shards), high / len(shards))
        return jnp.repeat(jnp.exp(draws), extent[position] // blocks).reshape((-1,) + (1,) * (len(extent) - position - 1))

    loudness = one(*shards[0])
    for cut in shards[1:]:
        loudness = loudness * one(*cut)
    return loudness


def scatter_about(rng, extent, scale, reach, cuts=(), kind=jnp.bfloat16):
    values = scale * jax.random.normal(rng, extent, jnp.float32)
    if cuts:
        values = values * levels(rng, extent, cuts, -0.22, 0.18)
    return jnp.clip(values, -reach, reach).astype(kind)


def setup_inputs(seed: int = 0) -> dict:
    key_list = jax.random.split(jax.random.key(seed), 13)
    return {
        "layer_input": scatter_about(key_list[0], (SEQS, L, D), 1.0, 6.0, ((1, 32),)),
        "query_weight": scatter_about(key_list[1], (D, D), D ** -0.5, 0.1875, ((0, 8), (1, 4))),
        "key_weight": scatter_about(key_list[2], (D, D), D ** -0.5, 0.1875, ((0, 8), (1, 4))),
        "value_weight": scatter_about(key_list[3], (D, D), D ** -0.5, 0.1875, ((0, 8), (1, 4))),
        "modulate_weight": scatter_about(key_list[4], (D, D), D ** -0.5, 0.1875, ((0, 8), (1, 4))),
        "output_weight": scatter_about(key_list[5], (D, D), D ** -0.5, 0.1875, ((0, 8), (1, 4))),
        "gate_matrix": scatter_about(key_list[6], (D, FF), D ** -0.5, 0.1875, ((1, 32),)),
        "lift_matrix": scatter_about(key_list[7], (D, FF), D ** -0.5, 0.1875, ((1, 32),)),
        "down_matrix": scatter_about(key_list[8], (D, FF), FF ** -0.5, 0.109375, ((1, 32),)),
        "decay_factor": draw_decay_factor(jax.random.fold_in(key_list[12], 71), 0),
        "valid_lengths": draw_valid_lengths(jax.random.fold_in(key_list[12], 71), 0),
        "output_cotangent": scatter_about(key_list[11], (SEQS, L, D), 1.0, 6.0, ((1, 32),)),
    }


EPS = 1e-06
HIGH = lax.Precision.HIGHEST

@jax.custom_vjp
def low(v):
    return lax.optimization_barrier(v.astype(jnp.bfloat16)).astype(jnp.float32)

@jax.custom_vjp
def low_back(v):
    return v

def low_keep(v):
    return (low(v), None)

def low_pass(kept, grad):
    return (grad,)

def back_keep(v):
    return (v, None)

def back_low(kept, grad):
    return (low(grad),)
low.defvjp(low_keep, low_pass)
low_back.defvjp(back_keep, back_low)

def simple_norm(values):
    return values * lax.rsqrt(lax.optimization_barrier(jnp.mean(values * values, axis=-1, keepdims=True)) + EPS)

def apply_swish(values):
    return values * jax.nn.sigmoid(values)

def rotation_tables(positions, head_size):
    half_width = head_size // 2
    frequency = jnp.exp(-math.log(10000.0) * jnp.arange(half_width, dtype=jnp.float32) / half_width)
    phase_angle = positions.astype(jnp.float32)[:, None] * frequency[None, :]
    return (jnp.cos(phase_angle)[:, None, :], jnp.sin(phase_angle)[:, None, :])

def rotate(values, cosine_table, sine_table):
    half_width = values.shape[-1] // 2
    first_half = values[..., :half_width]
    second_half = values[..., half_width:]
    return jnp.concatenate([first_half * cosine_table - second_half * sine_table, first_half * sine_table + second_half * cosine_table], axis=-1)

def decay_tables(log_decay, block_length):
    position_index = jnp.arange(block_length, dtype=jnp.float32)
    position_gap = position_index[:, None] - position_index[None, :]
    decay_grid = jnp.where(position_gap[None] >= 0.0, jnp.exp(jnp.maximum(position_gap, 0.0)[None] * log_decay[:, None, None]), 0.0)
    query_decay = jnp.exp((position_index[:, None] + 1.0) * log_decay[None, :])
    key_decay = jnp.exp((block_length - 1.0 - position_index[:, None]) * log_decay[None, :])
    block_decay = jnp.exp(block_length * log_decay)
    return (decay_grid, query_decay, key_decay, block_decay)

def layer_forward(layer_input, query_weight, key_weight, value_weight, modulate_weight, output_weight, gate_matrix, lift_matrix, down_matrix, decay_factor, valid_mask):
    batch_size, length, model_width = layer_input.shape
    head_count = decay_factor.shape[0]
    head_size = model_width // head_count
    block_count = length // L_DEV

    def split_heads(values):
        return values.reshape(batch_size, length, head_count, head_size)
    normed = low(simple_norm(layer_input))
    query_pre = low_back(jnp.einsum('bld,de->ble', normed, query_weight, precision=HIGH))
    key_pre = low_back(jnp.einsum('bld,de->ble', normed, key_weight, precision=HIGH))
    value_pre = low_back(jnp.einsum('bld,de->ble', normed, value_weight, precision=HIGH))
    modulate_pre = low_back(jnp.einsum('bld,de->ble', normed, modulate_weight, precision=HIGH))
    cosine_table, sine_table = rotation_tables(jnp.arange(length).astype(jnp.int32), head_size)
    mask_heads = valid_mask[..., None]
    queries = low(rotate(split_heads(apply_swish(query_pre)), cosine_table, sine_table))
    key_rows = low(mask_heads * rotate(split_heads(apply_swish(key_pre)), cosine_table, sine_table))
    value_rows = low(mask_heads * split_heads(value_pre))
    decay_grid, query_decay, key_decay, block_decay = decay_tables(jnp.log(decay_factor), L_DEV)

    def group_step(carried, pieces):
        query_block, key_block, value_block = pieces
        raw_scores = low_back(jnp.einsum('bihd,bjhd->bhij', query_block, key_block, precision=HIGH))
        scores = low(raw_scores * decay_grid[None])
        intra_part = jnp.einsum('bhij,bjhd->bihd', scores, value_block, precision=HIGH)
        inter_part = jnp.einsum('bihd,bhde->bihe', query_block * query_decay[None, :, :, None], carried, precision=HIGH)
        carried = block_decay[None, :, None, None] * carried + jnp.einsum('bjhd,bjhe->bhde', key_block * key_decay[None, :, :, None], value_block, precision=HIGH)
        return (carried, intra_part + inter_part)

    def to_blocks(values):
        return jnp.moveaxis(values.reshape(batch_size, block_count, L_DEV, head_count, head_size), 1, 0)
    start_state = jnp.zeros((batch_size, head_count, head_size, head_size), jnp.float32)
    final_state, outputs = lax.scan(jax.checkpoint(group_step), start_state, (to_blocks(queries), to_blocks(key_rows), to_blocks(value_rows)))
    mixed_heads = low_back(jnp.moveaxis(outputs, 0, 1).reshape(batch_size, length, head_count, head_size))
    gated_heads = low((mask_heads * simple_norm(mixed_heads) * split_heads(modulate_pre)).reshape(batch_size, length, model_width))
    attended = low_back(jnp.einsum('ble,oe->blo', gated_heads, output_weight, precision=HIGH))
    middle = layer_input + attended
    normed_two = low(simple_norm(middle))
    gate_pre = low_back(jnp.einsum('bld,df->blf', normed_two, gate_matrix, precision=HIGH))
    lift_pre = low_back(jnp.einsum('bld,df->blf', normed_two, lift_matrix, precision=HIGH))
    inner_act = low(apply_swish(gate_pre) * lift_pre)
    branch = low_back(jnp.einsum('blf,df->bld', inner_act, down_matrix, precision=HIGH))
    return middle + valid_mask * branch

def reference(layer_input, query_weight, key_weight, value_weight, modulate_weight, output_weight, gate_matrix, lift_matrix, down_matrix, decay_factor, valid_lengths, output_cotangent):
    length = layer_input.shape[1]
    position_index = jnp.arange(length).astype(jnp.int32)
    valid_mask = (position_index[None, :] < valid_lengths.astype(jnp.int32)[:, None]).astype(jnp.float32)[..., None]
    decay_float = decay_factor.astype(jnp.float32)
    floats = [array.astype(jnp.float32) for array in (layer_input, query_weight, key_weight, value_weight, modulate_weight, output_weight, gate_matrix, lift_matrix, down_matrix)]

    def forward(*weights):
        return layer_forward(*weights, decay_float, valid_mask)
    result, pullback = jax.vjp(forward, *floats)
    gradients = pullback(output_cotangent.astype(jnp.float32))
    return (result.astype(jnp.bfloat16), gradients[0], gradients[1], gradients[2], gradients[3], gradients[4], gradients[5], gradients[6], gradients[7], gradients[8])
```

```python
import math

import jax
import jax.numpy as jnp
from jax import lax
from jax.sharding import PartitionSpec as P

EPS = 1e-06
AXES = ("wide", "narrow")
BF16 = jnp.bfloat16
F32 = jnp.float32


def simple_norm(values):
    return values * lax.rsqrt(jnp.mean(values * values, axis=-1, keepdims=True) + EPS)


def norm_backward(values, cotangent):
    scale = lax.rsqrt(jnp.mean(values * values, axis=-1, keepdims=True) + EPS)
    inner = jnp.mean(values * cotangent, axis=-1, keepdims=True)
    return scale * cotangent - values * (scale * scale * scale * inner)


def apply_swish(values):
    return values * jax.nn.sigmoid(values)


def swish_slope(values):
    sigmoid_value = jax.nn.sigmoid(values)
    return sigmoid_value + values * sigmoid_value * (1.0 - sigmoid_value)


def rotation_tables(positions, head_size):
    half_width = head_size // 2
    frequency = jnp.exp(-math.log(10000.0) * jnp.arange(half_width, dtype=F32) / half_width)
    phase_angle = positions.astype(F32)[:, None] * frequency[None, :]
    return (jnp.cos(phase_angle)[:, None, :], jnp.sin(phase_angle)[:, None, :])


def rotate(values, cosine_table, sine_table):
    half_width = values.shape[-1] // 2
    first_half = values[..., :half_width]
    second_half = values[..., half_width:]
    return jnp.concatenate(
        [
            first_half * cosine_table - second_half * sine_table,
            first_half * sine_table + second_half * cosine_table,
        ],
        axis=-1,
    )


def exchange(x, mask):
    count = lax.axis_size(AXES)
    return lax.ppermute(x, AXES, [(i, i ^ mask) for i in range(count)])


def shift_z(x, step, reverse):
    count, unit = lax.axis_size(AXES), 2 * lax.axis_size("narrow")
    pairs = [(i, i + step * unit) for i in range(count - step * unit)]
    if reverse:
        pairs = [(b, a) for a, b in pairs]
    return lax.ppermute(x, AXES, pairs)


def gather_plane(x, masks):
    held = x[None]
    for mask in masks:
        held = jnp.concatenate([held, exchange(held, mask)], axis=0)
    return held


def gather_hidden(x, masks, swapped):
    held = gather_plane(x, masks)
    if swapped:
        held = jnp.swapaxes(held.reshape(2, 2, -1, *x.shape), 0, 1)
    return held.reshape(-1, x.shape[-1])


def scatter_plane(x, masks):
    for mask in reversed(masks):
        half = x.shape[0] // 2
        got = exchange(x[half:], mask)
        total = x[:half].astype(F32) + got.astype(F32)
        x = total.astype(BF16) if half > 1 else total
    return x[0]


def relative(masks, index):
    out = 0
    for k, mask in enumerate(masks):
        out ^= mask * ((index >> k) & 1)
    return out


def block_place(masks, wide_count):
    own = lax.axis_index(AXES)
    narrow_count = lax.axis_size("narrow")
    count = 1 << len(masks)
    ids = jnp.array([relative(masks, i) for i in range(count)], jnp.int32) ^ own
    return (ids // narrow_count) * (narrow_count // 2) + (ids % narrow_count) // 2


def to_canonical(blocks, masks, wide_count):
    own = lax.axis_index(AXES)
    count, rows, cols = blocks.shape
    narrow_count = lax.axis_size("narrow")
    sides = narrow_count // 2
    inverse = {relative(masks, i): i for i in range(count)}
    out = jnp.zeros((wide_count * rows, sides * cols), blocks.dtype)
    for i in range(count):
        ids = relative(masks, i) ^ own
        w, side = ids // narrow_count, (ids % narrow_count) // 2
        out = lax.dynamic_update_slice(out, blocks[i], (w * rows, side * cols))
    return out


def to_relative(full, masks, rows, cols):
    own = lax.axis_index(AXES)
    narrow_count = lax.axis_size("narrow")
    pieces = []
    for i in range(1 << len(masks)):
        ids = relative(masks, i) ^ own
        w, side = ids // narrow_count, (ids % narrow_count) // 2
        pieces.append(lax.dynamic_slice(full, (w * rows, side * cols), (rows, cols)))
    return jnp.stack(pieces)


def carried(local, block_decay, reverse):
    narrow_count = lax.axis_size("narrow")
    z_count = lax.axis_size("wide") // 2
    n, w = lax.axis_index("narrow"), lax.axis_index("wide")
    member = 2 * (w % 2) + n // 2
    masks = [0, 2, narrow_count, narrow_count + 2]
    slots = local.shape[0]
    share = slots // 4
    rank = lambda m: 3 - m if reverse else m
    log_decay = jnp.log(block_decay)
    power = lambda e: jnp.exp(e * log_decay)[None, :, None, None]

    def part(m):
        return lax.dynamic_slice_in_dim(local, m * share, share, 0)

    held = [part(member)] + [exchange(part(member ^ k), masks[k]) for k in range(1, 4)]
    held = [h.astype(F32) for h in held]
    ranks = [rank(member ^ k) for k in range(4)]
    total = sum(power((3 - ranks[k]).astype(F32)) * held[k] for k in range(4))
    before, span, step = 0.0, total, 1
    while step < z_count:
        got = shift_z(span.astype(BF16), step, reverse).astype(F32)
        before = before + power(4.0 * (step - 1)) * got
        span = span + power(4.0 * step) * got
        step *= 2
    sent = []
    for k in range(4):
        state = power(ranks[k].astype(F32)) * before
        for j in range(4):
            gap = (ranks[k] - 1 - ranks[j]).astype(F32)
            state = state + jnp.where(gap >= 0, power(jnp.maximum(gap, 0.0)), 0.0) * held[j]
        sent.append(state.astype(BF16))
    out = jnp.zeros(local.shape, BF16)
    for k in range(4):
        got = sent[0] if k == 0 else exchange(sent[k], masks[k])
        out = lax.dynamic_update_slice_in_dim(out, got, (member ^ k) * share, 0)
    return out


def on_device(
    layer_input,
    query_weight,
    key_weight,
    value_weight,
    modulate_weight,
    output_weight,
    gate_matrix,
    lift_matrix,
    down_matrix,
    decay_factor,
    valid_lengths,
    output_cotangent,
):
    narrow_count, wide_count = lax.axis_size("narrow"), lax.axis_size("wide")
    wide_index, narrow_index = lax.axis_index("wide"), lax.axis_index("narrow")
    core, side = narrow_index % 2, narrow_index // 2
    slots, quarter, width = layer_input.shape
    block = 2 * quarter
    rows, cols = query_weight.shape
    heads = 2 * decay_factor.shape[0]
    head_size = cols // decay_factor.shape[0]
    x_mask = 2
    wide_masks = []
    bit = narrow_count
    while bit < narrow_count * wide_count:
        wide_masks.append(bit)
        bit *= 2
    y_mask, z_masks = wide_masks[0], wide_masks[:0:-1]
    order_yx = z_masks + [y_mask, x_mask]
    order_xy = z_masks + [x_mask, y_mask]

    base = wide_index * (quarter * narrow_count) + side * block
    offsets = jnp.concatenate(
        [core * quarter + jnp.arange(quarter), (1 - core) * quarter + jnp.arange(quarter)]
    ).astype(jnp.int32)
    positions = base + offsets
    mask = (positions[None, :] < valid_lengths[:, None]).astype(F32)
    mask_rows = mask[:, :quarter, None]
    mask_heads = mask[:, :, None, None]

    def pair(mine):
        return jnp.concatenate([mine, exchange(mine, 1)], axis=1)

    def core_sum(partial):
        return partial[:, :quarter] + exchange(partial[:, quarter:].astype(BF16), 1).astype(F32)

    other_decay = exchange(decay_factor, x_mask)
    decay = jnp.concatenate(
        [jnp.where(side == 0, decay_factor, other_decay), jnp.where(side == 0, other_decay, decay_factor)]
    )
    log_decay = jnp.log(decay)

    def gathered(weight, masks):
        return to_canonical(gather_plane(weight, masks), masks, wide_count)

    full_key = gathered(key_weight, order_yx)
    full_value = gathered(value_weight, order_xy)
    full_query = gathered(query_weight, order_yx)
    full_modulate = gathered(modulate_weight, order_xy)
    full_output = gathered(output_weight, order_yx)
    gate_t = gather_hidden(gate_matrix.T, order_yx, False)
    lift_t = gather_hidden(lift_matrix.T, order_xy, True)
    down_t = gather_hidden(down_matrix.T, order_yx, False)

    input_rows = layer_input.astype(F32)
    normed = pair(simple_norm(input_rows).astype(BF16))

    def project(matrix):
        return jnp.einsum("bld,de->ble", normed, matrix, preferred_element_type=F32).reshape(
            slots, block, heads, head_size
        )

    cosine_table, sine_table = rotation_tables(positions, head_size)
    key_pre = project(full_key)
    value_pre = project(full_value)
    keys = (mask_heads * rotate(apply_swish(key_pre), cosine_table, sine_table)).astype(BF16)
    values = (mask_heads * value_pre).astype(BF16)
    spot = offsets.astype(F32)
    gap = spot[:, None] - spot[None, :]
    decay_grid = jnp.where(
        gap[None] >= 0.0, jnp.exp(jnp.maximum(gap, 0.0)[None] * log_decay[:, None, None]), 0.0
    )
    query_decay = jnp.exp((spot[:, None] + 1.0) * log_decay[None, :])[None, :, :, None]
    key_decay = jnp.exp((block - 1.0 - spot[:, None]) * log_decay[None, :])[None, :, :, None]
    block_decay = jnp.exp(block * log_decay)
    keys_scaled = (keys.astype(F32) * key_decay).astype(BF16)
    local_state = jnp.einsum("bjhd,bjhe->bhde", keys_scaled, values, preferred_element_type=F32)
    state = carried(local_state.astype(BF16), block_decay, False)

    query_pre = project(full_query)
    modulate_pre = project(full_modulate)
    queries = rotate(apply_swish(query_pre), cosine_table, sine_table).astype(BF16)
    scores = (
        jnp.einsum("bihd,bjhd->bhij", queries, keys, preferred_element_type=F32) * decay_grid[None]
    ).astype(BF16)
    queries_scaled = (queries.astype(F32) * query_decay).astype(BF16)
    mixed = jnp.einsum("bhij,bjhd->bihd", scores, values, preferred_element_type=F32)
    mixed = mixed + jnp.einsum("bihd,bhde->bihe", queries_scaled, state, preferred_element_type=F32)
    normed_heads = simple_norm(mixed)
    modulate_masked = modulate_pre * mask_heads
    gated = (normed_heads * modulate_masked).astype(BF16).reshape(slots, block, heads * head_size)
    attended = core_sum(jnp.einsum("ble,oe->blo", gated, full_output, preferred_element_type=F32))
    middle = input_rows + attended
    normed_two = pair(simple_norm(middle).astype(BF16))
    cotangent = output_cotangent.astype(F32)
    branch_grad = pair((mask_rows * cotangent).astype(BF16))

    def hidden(rows_in, matrix):
        return jnp.einsum("bld,fd->blf", rows_in, matrix, preferred_element_type=F32)

    def outer(a, b):
        return jnp.einsum("blf,bld->fd", a, b, preferred_element_type=F32).astype(BF16)

    gate_pre = hidden(normed_two, gate_t)
    lift_pre = hidden(normed_two, lift_t)
    inner_grad = hidden(branch_grad, down_t)
    gate_act = apply_swish(gate_pre)
    inner = (gate_act * lift_pre).astype(BF16)
    gate_grad = (inner_grad * lift_pre * swish_slope(gate_pre)).astype(BF16)
    lift_grad = (inner_grad * gate_act).astype(BF16)
    normed_grad = jnp.einsum("blf,fd->bld", gate_grad, gate_t, preferred_element_type=F32)
    normed_grad = normed_grad + jnp.einsum("blf,fd->bld", lift_grad, lift_t, preferred_element_type=F32)
    middle_grad = cotangent + norm_backward(middle, core_sum(normed_grad))
    branch = core_sum(jnp.einsum("blf,fd->bld", inner, down_t, preferred_element_type=F32))
    layer_output = (middle + mask_rows * branch).astype(BF16)

    def scattered(grad, masks, swapped):
        members = 1 << len(masks)
        if swapped:
            grad = jnp.swapaxes(grad.reshape(2, 2, -1, width), 0, 1)
        return scatter_plane(grad.reshape(members, -1, width), masks).T

    gate_gradient = scattered(outer(gate_grad, normed_two), order_yx, False)
    lift_gradient = scattered(outer(lift_grad, normed_two), order_xy, True)
    down_gradient = scattered(outer(inner, branch_grad), order_yx, False)

    attended_grad = pair(middle_grad.astype(BF16))
    gated_grad = jnp.einsum(
        "blo,oe->ble", attended_grad, full_output, preferred_element_type=F32
    ).reshape(slots, block, heads, head_size)
    modulate_grad = (gated_grad * mask_heads * normed_heads).astype(BF16)
    mixed_grad = norm_backward(mixed, gated_grad * modulate_masked).astype(BF16)
    state_grad = jnp.einsum("bihd,bihe->bhde", queries_scaled, mixed_grad, preferred_element_type=F32)
    later = carried(state_grad.astype(BF16), block_decay, True)
    score_grad = (
        jnp.einsum("bihe,bjhe->bhij", mixed_grad, values, preferred_element_type=F32)
        * decay_grid[None]
    ).astype(BF16)
    value_grad = jnp.einsum("bhij,bihe->bjhe", scores, mixed_grad, preferred_element_type=F32)
    query_grad = jnp.einsum("bhij,bjhd->bihd", score_grad, keys, preferred_element_type=F32)
    key_grad = jnp.einsum("bhij,bihd->bjhd", score_grad, queries, preferred_element_type=F32)
    query_grad = (
        query_grad
        + jnp.einsum("bihe,bhde->bihd", mixed_grad, state, preferred_element_type=F32) * query_decay
    )
    key_grad = (
        key_grad
        + jnp.einsum("bjhe,bhde->bjhd", values, later, preferred_element_type=F32) * key_decay
    )
    value_grad = value_grad + jnp.einsum(
        "bjhd,bhde->bjhe", keys_scaled, later, preferred_element_type=F32
    )
    query_pre_grad = (rotate(query_grad, cosine_table, -sine_table) * swish_slope(query_pre)).astype(BF16)
    key_pre_grad = (
        rotate(key_grad * mask_heads, cosine_table, -sine_table) * swish_slope(key_pre)
    ).astype(BF16)
    value_pre_grad = (value_grad * mask_heads).astype(BF16)
    grads = [
        g.reshape(slots, block, heads * head_size)
        for g in (query_pre_grad, key_pre_grad, value_pre_grad, modulate_grad)
    ]
    matrices = (full_query, full_key, full_value, full_modulate)
    row_grad = sum(
        jnp.einsum("ble,de->bld", g, m, preferred_element_type=F32) for g, m in zip(grads, matrices)
    )
    input_gradient = middle_grad + norm_backward(input_rows, core_sum(row_grad))

    def square(a, b, masks):
        full = jnp.einsum("bld,ble->de", a, b, preferred_element_type=F32)
        return scatter_plane(to_relative(full.astype(BF16), masks, rows, cols), masks)

    output_gradient = square(attended_grad, gated, order_yx)
    modulate_gradient = square(normed, grads[3], order_xy)
    query_gradient = square(normed, grads[0], order_yx)
    key_gradient = square(normed, grads[1], order_xy)
    value_gradient = square(normed, grads[2], order_yx)
    return (
        layer_output,
        input_gradient,
        query_gradient,
        key_gradient,
        value_gradient,
        modulate_gradient,
        output_gradient,
        gate_gradient,
        lift_gradient,
        down_gradient,
    )


def solution(mesh):
    placed = (
        P(None, ("wide", "narrow"), None),
        P("wide", "narrow"),
        P("wide", "narrow"),
        P("wide", "narrow"),
        P("wide", "narrow"),
        P("wide", "narrow"),
        P(None, ("wide", "narrow")),
        P(None, ("wide", "narrow")),
        P(None, ("wide", "narrow")),
        P("narrow"),
        P(),
        P(None, ("wide", "narrow"), None),
    )
    return jax.shard_map(
        on_device,
        mesh=mesh,
        in_specs=placed,
        out_specs=(
            P(None, ("wide", "narrow"), None),
            P(None, ("wide", "narrow"), None),
            P("wide", "narrow"),
            P("wide", "narrow"),
            P("wide", "narrow"),
            P("wide", "narrow"),
            P("wide", "narrow"),
            P(None, ("wide", "narrow")),
            P(None, ("wide", "narrow")),
            P(None, ("wide", "narrow")),
        ),
        check_vma=False,
    )
```

```python
import functools
import math

import jax
import jax.numpy as jnp
from jax import lax
from jax.experimental import pallas as pl
from jax.experimental.pallas import tpu as pltpu
from jax.sharding import PartitionSpec as P

EPS = 1e-06
AXES = ("wide", "narrow")
BF16 = jnp.bfloat16
F32 = jnp.float32


def simple_norm(values):
    return values * lax.rsqrt(jnp.mean(values * values, axis=-1, keepdims=True) + EPS)


def norm_backward(values, cotangent):
    scale = lax.rsqrt(jnp.mean(values * values, axis=-1, keepdims=True) + EPS)
    inner = jnp.mean(values * cotangent, axis=-1, keepdims=True)
    return scale * cotangent - values * (scale * scale * scale * inner)


def apply_swish(values):
    return values * jax.nn.sigmoid(values)


def swish_slope(values):
    sigmoid_value = jax.nn.sigmoid(values)
    return sigmoid_value + values * sigmoid_value * (1.0 - sigmoid_value)


def exchange(x, mask):
    count = lax.axis_size(AXES)
    return lax.ppermute(x, AXES, [(i, i ^ mask) for i in range(count)])


def shift_z(x, step, reverse):
    count, unit = lax.axis_size(AXES), 2 * lax.axis_size("narrow")
    pairs = [(i, i + step * unit) for i in range(count - step * unit)]
    if reverse:
        pairs = [(b, a) for a, b in pairs]
    return lax.ppermute(x, AXES, pairs)


def gather_plane(x, masks):
    return gather_more(x[None], masks)


def gather_more(held, masks):
    for mask in masks:
        held = jnp.concatenate([held, exchange(held, mask)], axis=0)
    return held


def gather_hidden(x, masks, swapped):
    held = gather_plane(x, masks)
    if swapped:
        held = jnp.swapaxes(held.reshape(2, 2, -1, *x.shape), 0, 1)
    return held.reshape(-1, x.shape[-1])


def scatter_plane(x, masks):
    for mask in reversed(masks):
        half = x.shape[0] // 2
        got = exchange(x[half:], mask)
        total = x[:half].astype(F32) + got.astype(F32)
        x = total.astype(BF16) if half > 1 else total
    return x[0]


def relative(masks, index):
    out = 0
    for k, mask in enumerate(masks):
        out ^= mask * ((index >> k) & 1)
    return out


NT = (((1,), (1,)), ((), ()))
NN = (((1,), (0,)), ((), ()))
TN = (((0,), (0,)), ((), ()))


def mm(a, b, dims=NN):
    return lax.dot_general(a, b, dims, preferred_element_type=F32)


def turn(v, cosine, sine):
    return v * cosine + pltpu.roll(v, v.shape[-1] // 2, 1) * sine


def block_spots(masks):
    own = lax.axis_index(AXES)
    narrow_count = lax.axis_size("narrow")
    ids = jnp.array([relative(masks, i) for i in range(1 << len(masks))], jnp.int32) ^ own
    return jnp.stack([ids // narrow_count, (ids % narrow_count) // 2], axis=1)


def block_copy(spots, which, i, rows, cols, whole, part, sem, out):
    at = (
        pl.ds(pl.multiple_of(spots[which, i, 0] * rows, rows), rows),
        pl.ds(pl.multiple_of(spots[which, i, 1] * cols, cols), cols),
    )
    if out:
        return pltpu.make_async_copy(whole.at[at], part, sem)
    return pltpu.make_async_copy(part, whole.at[at], sem)


def each_block(spots, jobs, out=False):
    def go(method):
        for order, k, near, far, whole, sems in jobs:
            half, _, rows, cols = near.shape

            def step(i, _):
                for at, part in enumerate((near, far)):
                    copy = block_copy(
                        spots, order, i + at * half, rows, cols, whole, part.at[i, k],
                        sems.at[i + at * half], out,
                    )
                    getattr(copy, method)()
                return 0

            lax.fori_loop(0, half, step, 0)

    go("start")
    go("wait")


def both(near, far):
    rows = near.shape[0] * near.shape[1]
    return jnp.concatenate([near.reshape(rows, -1), far.reshape(rows, -1)], axis=0)


def slot_rows(x, s, size, count):
    return jnp.concatenate(
        [x[s * size : (s + 1) * size], x[(count + s) * size : (count + s + 1) * size]], axis=0
    )


def slot_back(parts, size):
    return jnp.concatenate([p[:size] for p in parts] + [p[size:] for p in parts], axis=0)


def put(ref, lanes, value):
    two, count, size, _ = ref.shape
    ref[:, :, :, lanes] = value.reshape(two, count, size, -1).astype(ref.dtype)


def get(ref, lanes=slice(None)):
    two, count, size, width = ref.shape
    x = ref[:, :, :, lanes]
    return x.reshape(two * count * size, x.shape[-1])


def key_value_kernel(
    spots, near, far, mask, cosine, sine, key_decay, kw0, kw1, vw0, vw1,
    key_pre, keys, values, state, wk, wv, sems
):
    @pl.when(pl.program_id(0) == 0)
    def _():
        each_block(spots, [(0, 0, kw0, kw1, wk, sems.at[0]), (1, 0, vw0, vw1, wv, sems.at[1])])

    count, size = near.shape[0], near.shape[1]
    x = both(near[...], far[...])
    valid = get(mask)
    head = cosine.shape[-1]
    pre = mm(x, wk[...])
    val_pre = mm(x, wv[...])
    for h in range(pre.shape[-1] // head):
        lanes = slice(h * head, (h + 1) * head)
        kp = pre[:, lanes]
        put(key_pre, lanes, kp)
        key = (valid * turn(kp * jax.nn.sigmoid(kp), cosine[...], sine[...])).astype(BF16)
        val = (valid * val_pre[:, lanes]).astype(BF16)
        put(keys, lanes, key)
        put(values, lanes, val)
        scaled = (key.astype(F32) * key_decay[:, lanes]).astype(BF16)
        for s in range(count):
            state[s, h] = mm(
                slot_rows(scaled, s, size, count), slot_rows(val, s, size, count), TN
            ).astype(BF16)


def query_kernel(
    spots, near, far, mask, cosine, sine, grid, keys, values, w0, w1,
    query_pre, queries, modulate, intra, wq, wm, sems
):
    @pl.when(pl.program_id(0) == 0)
    def _():
        each_block(spots, [(0, 0, w0, w1, wq, sems.at[0]), (0, 1, w0, w1, wm, sems.at[1])])

    count, size = near.shape[0], near.shape[1]
    x = both(near[...], far[...])
    valid = get(mask)
    head = cosine.shape[-1]
    pre = mm(x, wq[...])
    mod = mm(x, wm[...])
    for h in range(pre.shape[-1] // head):
        lanes = slice(h * head, (h + 1) * head)
        qp = pre[:, lanes]
        put(query_pre, lanes, qp)
        put(modulate, lanes, mod[:, lanes] * valid)
        q = turn(qp * jax.nn.sigmoid(qp), cosine[...], sine[...]).astype(BF16)
        put(queries, lanes, q)
        k, v = get(keys, lanes), get(values, lanes)
        parts = []
        for s in range(count):
            scores = mm(slot_rows(q, s, size, count), slot_rows(k, s, size, count), NT) * grid[h]
            parts.append(mm(scores.astype(BF16), slot_rows(v, s, size, count)))
        put(intra, lanes, slot_back(parts, size))


def load_states(spots, pieces, held, sems):
    member = spots[2, 0, 0]
    copies = [
        pltpu.make_async_copy(p, held.at[member ^ k], sems.at[k]) for k, p in enumerate(pieces)
    ]
    for c in copies:
        c.start()
    for c in copies:
        c.wait()


def mixed_kernel(
    spots, queries, intra, modulate, query_decay, s0, s1, s2, s3, w0, w1,
    mixed, gated, near_out, far_out, wo, held, sems, state_sems
):
    @pl.when(pl.program_id(0) == 0)
    def _():
        load_states(spots, (s0, s1, s2, s3), held, state_sems)
        each_block(spots, [(0, 0, w0, w1, wo, sems)])

    step = pl.program_id(0)
    _, count, size, width = queries.shape
    heads = held.shape[2]
    head = width // heads
    gates = []
    for h in range(heads):
        lanes = slice(h * head, (h + 1) * head)
        q = (get(queries, lanes).astype(F32) * query_decay[:, lanes]).astype(BF16)
        parts = [mm(slot_rows(q, s, size, count), held[step, s, h]) for s in range(count)]
        mix = get(intra, lanes) + slot_back(parts, size)
        put(mixed, lanes, mix)
        scale = lax.rsqrt(jnp.mean(mix * mix, axis=-1, keepdims=True) + EPS)
        gates.append((mix * scale * get(modulate, lanes)).astype(BF16))
    gate = jnp.concatenate(gates, axis=1)
    put(gated, slice(None), gate)
    out = mm(gate, wo[...], NT)
    near_out[...] = out[: count * size].reshape(near_out.shape)
    far_out[...] = out[count * size :].astype(BF16).reshape(far_out.shape)


def mixed_back_kernel(
    spots, near, far, mixed, modulate, queries, query_pre, keys, values, mask, cosine, sine,
    query_decay, grid, s0, s1, s2, s3, w0, w1,
    modulate_grad, query_grad, key_grad, value_grad, state_grad, wo, held, sems, state_sems
):
    @pl.when(pl.program_id(0) == 0)
    def _():
        load_states(spots, (s0, s1, s2, s3), held, state_sems)
        each_block(spots, [(0, 0, w0, w1, wo, sems)])

    step = pl.program_id(0)
    _, count, size, width = queries.shape
    heads = held.shape[2]
    head = width // heads
    gate_grad = mm(both(near[...], far[...]), wo[...])
    valid = get(mask)
    for h in range(heads):
        lanes = slice(h * head, (h + 1) * head)
        mix = get(mixed, lanes)
        scale = lax.rsqrt(jnp.mean(mix * mix, axis=-1, keepdims=True) + EPS)
        gg = gate_grad[:, lanes]
        put(modulate_grad, lanes, gg * valid * (mix * scale))
        cot = gg * get(modulate, lanes)
        inner = jnp.mean(mix * cot, axis=-1, keepdims=True)
        gm = (scale * cot - mix * (scale * scale * scale * inner)).astype(BF16)
        q, k, v = get(queries, lanes), get(keys, lanes), get(values, lanes)
        qs = (q.astype(F32) * query_decay[:, lanes]).astype(BF16)
        gq, gk, gv = [], [], []
        for s in range(count):
            pick = lambda x: slot_rows(x, s, size, count)
            gms, qq, kk, vv = pick(gm), pick(q), pick(k), pick(v)
            gs = (mm(gms, vv, NT) * grid[h]).astype(BF16)
            sc = (mm(qq, kk, NT) * grid[h]).astype(BF16)
            gv.append(mm(sc, gms, TN))
            gk.append(mm(gs, qq, TN))
            decay = slot_rows(query_decay[:, lanes], s, size, count)
            gq.append(mm(gs, kk) + mm(gms, held[step, s, h], NT) * decay)
            state_grad[s, h] = mm(pick(qs), gms, TN).astype(BF16)
        put(key_grad, lanes, slot_back(gk, size))
        put(value_grad, lanes, slot_back(gv, size))
        qp = get(query_pre, lanes)
        sg = jax.nn.sigmoid(qp)
        slope = sg + qp * sg * (1.0 - sg)
        put(query_grad, lanes, turn(slot_back(gq, size), cosine[...], -sine[...]) * slope)


def rows_kernel(spots, query_grad, modulate_grad, w0, w1, out, wq, wm, sems):
    @pl.when(pl.program_id(0) == 0)
    def _():
        each_block(spots, [(0, 0, w0, w1, wq, sems.at[0]), (0, 1, w0, w1, wm, sems.at[1])])

    put(out, slice(None), mm(get(query_grad), wq[...], NT) + mm(get(modulate_grad), wm[...], NT))


def key_back_kernel(
    spots, key_grad, value_grad, keys, values, key_pre, mask, cosine, sine, key_decay, rows_in,
    g0, g1, g2, g3, kw0, kw1, vw0, vw1,
    key_out, value_out, near_out, far_out, wk, wv, held, sems, state_sems
):
    @pl.when(pl.program_id(0) == 0)
    def _():
        load_states(spots, (g0, g1, g2, g3), held, state_sems)
        each_block(spots, [(0, 0, kw0, kw1, wk, sems.at[0]), (1, 0, vw0, vw1, wv, sems.at[1])])

    step = pl.program_id(0)
    _, count, size, width = keys.shape
    heads = held.shape[2]
    head = width // heads
    valid = get(mask)
    gks, gvs = [], []
    for h in range(heads):
        lanes = slice(h * head, (h + 1) * head)
        decay = key_decay[:, lanes]
        k, v = get(keys, lanes), get(values, lanes)
        scaled = (k.astype(F32) * decay).astype(BF16)
        pk = [mm(slot_rows(v, s, size, count), held[step, s, h], NT) for s in range(count)]
        pv = [mm(slot_rows(scaled, s, size, count), held[step, s, h]) for s in range(count)]
        gk = get(key_grad, lanes) + slot_back(pk, size) * decay
        gv = get(value_grad, lanes) + slot_back(pv, size)
        kp = get(key_pre, lanes)
        sg = jax.nn.sigmoid(kp)
        slope = sg + kp * sg * (1.0 - sg)
        gks.append((turn(gk * valid, cosine[...], -sine[...]) * slope).astype(BF16))
        gvs.append((gv * valid).astype(BF16))
    gk, gv = jnp.concatenate(gks, axis=1), jnp.concatenate(gvs, axis=1)
    put(key_out, slice(None), gk)
    put(value_out, slice(None), gv)
    out = get(rows_in) + mm(gk, wk[...], NT) + mm(gv, wv[...], NT)
    near_out[...] = out[: count * size].reshape(near_out.shape)
    far_out[...] = out[count * size :].astype(BF16).reshape(far_out.shape)


def outer_kernel(order, spots, near, far, *refs):
    count = (len(refs) - 4) // 1
    grads, (keep, send, whole, sems) = refs[:count], refs[count:]
    rows = near.shape[0] * near.shape[1]
    width = near.shape[2]
    tile = 256
    for c in range(0, width, tile):
        a = near[:, :, c : c + tile].reshape(rows, tile)
        b = far[:, :, c : c + tile].reshape(rows, tile)
        for k, g in enumerate(grads):
            g0 = g[0].reshape(rows, -1)
            g1 = g[1].reshape(rows, -1)
            whole[k, c : c + tile, :] = (mm(a, g0, TN) + mm(b, g1, TN)).astype(BF16)
    each_block(
        spots, [(order, k, keep, send, whole.at[k], sems.at[k]) for k in range(count)], out=True
    )


ANY = pl.BlockSpec(memory_space=pl.ANY)
VMEM = pl.BlockSpec(memory_space=pltpu.VMEM)


def run(kernel, name, spots, inputs, outputs, scratch, steps, flops):
    def spec(shape, kind):
        if kind == "any":
            return ANY
        if kind == "rows":
            size = shape[0] // steps
            return pl.BlockSpec((size, *shape[1:]), lambda i, _: (i,) + (0,) * (len(shape) - 1))
        if kind == "pair":
            size = shape[1] // steps
            return pl.BlockSpec(
                (2, size, *shape[2:]), lambda i, _: (0, i) + (0,) * (len(shape) - 2)
            )
        return pl.BlockSpec(shape, lambda i, _: (0,) * len(shape))

    moved = sum(a.size * a.dtype.itemsize for a, _ in inputs)
    moved += sum(math.prod(s) * jnp.dtype(d).itemsize for s, d, _ in outputs)
    return pl.pallas_call(
        kernel,
        out_shape=[jax.ShapeDtypeStruct(s, d) for s, d, _ in outputs],
        grid_spec=pltpu.PrefetchScalarGridSpec(
            num_scalar_prefetch=1,
            grid=(steps,),
            in_specs=[spec(a.shape, kind) for a, kind in inputs],
            out_specs=[spec(s, kind) for s, _, kind in outputs],
            scratch_shapes=scratch,
        ),
        compiler_params=pltpu.CompilerParams(vmem_limit_bytes=40 * 2**20),
        cost_estimate=pl.CostEstimate(flops=flops, bytes_accessed=moved, transcendentals=0),
        name=name,
    )(spots, *[a for a, _ in inputs])


def carried(local, block_decay, reverse):
    narrow_count = lax.axis_size("narrow")
    z_count = lax.axis_size("wide") // 2
    n, w = lax.axis_index("narrow"), lax.axis_index("wide")
    member = 2 * (w % 2) + n // 2
    masks = [0, 2, narrow_count, narrow_count + 2]
    slots = local.shape[0]
    share = slots // 4
    rank = lambda m: 3 - m if reverse else m
    log_decay = jnp.log(block_decay)
    power = lambda e: jnp.exp(e * log_decay)[None, :, None, None]

    def part(m):
        return lax.dynamic_slice_in_dim(local, m * share, share, 0)

    held = [part(member)] + [exchange(part(member ^ k), masks[k]) for k in range(1, 4)]
    held = [h.astype(F32) for h in held]
    ranks = [rank(member ^ k) for k in range(4)]
    total = sum(power((3 - ranks[k]).astype(F32)) * held[k] for k in range(4))
    before, span, step = 0.0, total, 1
    while step < z_count:
        got = shift_z(span.astype(BF16), step, reverse).astype(F32)
        before = before + power(4.0 * (step - 1)) * got
        span = span + power(4.0 * step) * got
        step *= 2
    sent = []
    for k in range(4):
        state = power(ranks[k].astype(F32)) * before
        for j in range(4):
            gap = (ranks[k] - 1 - ranks[j]).astype(F32)
            state = state + jnp.where(gap >= 0, power(jnp.maximum(gap, 0.0)), 0.0) * held[j]
        sent.append(state.astype(BF16))
    return [sent[0]] + [exchange(sent[k], masks[k]) for k in range(1, 4)]


def on_device(
    layer_input,
    query_weight,
    key_weight,
    value_weight,
    modulate_weight,
    output_weight,
    gate_matrix,
    lift_matrix,
    down_matrix,
    decay_factor,
    valid_lengths,
    output_cotangent,
):
    narrow_count, wide_count = lax.axis_size("narrow"), lax.axis_size("wide")
    wide_index, narrow_index = lax.axis_index("wide"), lax.axis_index("narrow")
    core, side = narrow_index % 2, narrow_index // 2
    slots, quarter, width = layer_input.shape
    block = 2 * quarter
    rows, cols = query_weight.shape
    heads = 2 * decay_factor.shape[0]
    head_size = cols // decay_factor.shape[0]
    x_mask = 2
    wide_masks = []
    bit = narrow_count
    while bit < narrow_count * wide_count:
        wide_masks.append(bit)
        bit *= 2
    y_mask, z_masks = wide_masks[0], wide_masks[:0:-1]
    order_yx = z_masks + [y_mask, x_mask]
    order_xy = z_masks + [x_mask, y_mask]
    members = 1 << len(order_yx)
    half = members // 2

    base = wide_index * (quarter * narrow_count) + side * block
    offsets = jnp.stack(
        [core * quarter + jnp.arange(quarter), (1 - core) * quarter + jnp.arange(quarter)]
    ).astype(jnp.int32)
    mask = ((base + offsets)[:, None, :] < valid_lengths[None, :, None]).astype(F32)
    mask_rows = mask[0][:, :, None]
    mask_wide = jnp.broadcast_to(mask[..., None], (2, slots, quarter, head_size))
    member = 2 * (wide_index % 2) + side
    spots = jnp.concatenate(
        [
            block_spots(order_xy)[None],
            block_spots(order_yx)[None],
            jnp.broadcast_to(member, (1, members, 2)).astype(jnp.int32),
        ]
    )

    def core_sum(near, far):
        return near + exchange(far, 1).astype(F32)

    other_decay = exchange(decay_factor, x_mask)
    decay = jnp.concatenate(
        [jnp.where(side == 0, decay_factor, other_decay), jnp.where(side == 0, other_decay, decay_factor)]
    )
    log_decay = jnp.log(decay)
    block_decay = jnp.exp(block * log_decay)
    steps = 4
    count = slots // steps

    def table(values):
        lanes = values.shape[-1]
        return jnp.broadcast_to(values[:, None], (2, count, quarter, lanes)).reshape(-1, lanes)

    half_head = head_size // 2
    frequency = jnp.exp(-math.log(10000.0) * jnp.arange(half_head, dtype=F32) / half_head)
    phase = (base + offsets).astype(F32)[..., None] * frequency
    cosine, sine = jnp.cos(phase), jnp.sin(phase)
    cosine = table(jnp.concatenate([cosine, cosine], axis=-1))
    sine = table(jnp.concatenate([-sine, sine], axis=-1))
    spot = offsets.astype(F32)
    log_lanes = jnp.repeat(log_decay, head_size)
    query_decay = table(jnp.exp((spot[..., None] + 1.0) * log_lanes))
    key_decay = table(jnp.exp((block - 1.0 - spot[..., None]) * log_lanes))
    flat = spot.reshape(-1)
    gap = flat[:, None] - flat[None, :]
    decay_grid = jnp.where(
        gap[None] >= 0.0, jnp.exp(jnp.maximum(gap, 0.0)[None] * log_decay[:, None, None]), 0.0
    )

    def halves(x, masks):
        held = gather_plane(x, masks[:-1])
        return held, exchange(held, masks[-1])

    def bundle(*weights):
        return jnp.stack(weights)

    key_value = gather_plane(bundle(key_weight, value_weight), z_masks)
    key_near = gather_more(key_value[:, :1], [x_mask])
    value_near = gather_more(key_value[:, 1:], [y_mask])
    key_parts = (key_near, exchange(key_near, y_mask))
    value_parts = (value_near, exchange(value_near, x_mask))
    query_parts = halves(bundle(query_weight, modulate_weight), order_xy)
    output_parts = halves(bundle(output_weight), order_xy)
    gate_t = gather_hidden(gate_matrix.T, order_yx, False)
    lift_t = gather_hidden(lift_matrix.T, order_xy, True)
    down_t = gather_hidden(down_matrix.T, order_yx, False)

    input_rows = layer_input.astype(F32)
    normed = simple_norm(input_rows).astype(BF16)
    normed_pair = (normed, exchange(normed, 1))
    inner_width = heads * head_size
    chip_shape = (2, slots, quarter, inner_width)
    row_shape = (slots, quarter, width)
    state_shape = (slots, heads, head_size, head_size)
    square_flops = 2 * 2 * slots * quarter * width * inner_width
    wide_scratch = pltpu.VMEM((width, inner_width), BF16)
    held_scratch = pltpu.VMEM((4, slots // 4, heads, head_size, head_size), BF16)
    dma = pltpu.SemaphoreType.DMA

    key_pre, keys, values, local_state = run(
        key_value_kernel, "key_value", spots,
        [
            (normed_pair[0], "rows"), (normed_pair[1], "rows"), (mask_wide, "pair"),
            (cosine, "whole"), (sine, "whole"), (key_decay, "whole"),
            (key_parts[0], "any"), (key_parts[1], "any"),
            (value_parts[0], "any"), (value_parts[1], "any"),
        ],
        [
            (chip_shape, F32, "pair"), (chip_shape, BF16, "pair"), (chip_shape, BF16, "pair"),
            (state_shape, BF16, "rows"),
        ],
        [wide_scratch, wide_scratch, dma((2, members))],
        steps, 2 * square_flops,
    )
    state_parts = carried(local_state, block_decay, False)
    query_pre, queries, modulate, intra = run(
        query_kernel, "query", spots,
        [
            (normed_pair[0], "rows"), (normed_pair[1], "rows"), (mask_wide, "pair"),
            (cosine, "whole"), (sine, "whole"), (decay_grid, "whole"),
            (keys, "pair"), (values, "pair"), (query_parts[0], "any"), (query_parts[1], "any"),
        ],
        [
            (chip_shape, F32, "pair"), (chip_shape, BF16, "pair"), (chip_shape, F32, "pair"),
            (chip_shape, F32, "pair"),
        ],
        [wide_scratch, wide_scratch, dma((2, members))],
        steps, 2 * square_flops,
    )
    state_inputs = [(p, "any") for p in state_parts]
    output_inputs = [(p, "any") for p in output_parts]
    mixed, gated, near_att, far_att = run(
        mixed_kernel, "mixed", spots,
        [
            (queries, "pair"), (intra, "pair"), (modulate, "pair"), (query_decay, "whole"),
            *state_inputs, *output_inputs,
        ],
        [
            (chip_shape, F32, "pair"), (chip_shape, BF16, "pair"), (row_shape, F32, "rows"),
            (row_shape, BF16, "rows"),
        ],
        [wide_scratch, held_scratch, dma((members,)), dma((4,))],
        steps, square_flops,
    )
    middle = input_rows + core_sum(near_att, far_att)

    def pair(mine):
        return jnp.stack([mine, exchange(mine, 1)])

    normed_two = pair(simple_norm(middle).astype(BF16))
    cotangent = output_cotangent.astype(F32)
    branch_grad = pair((mask_rows * cotangent).astype(BF16))

    def hidden(rows_in, matrix):
        return jnp.einsum("pbld,fd->pblf", rows_in, matrix, preferred_element_type=F32)

    def outer(a, b):
        return jnp.einsum("pblf,pbld->fd", a, b, preferred_element_type=F32).astype(BF16)

    gate_pre = hidden(normed_two, gate_t)
    lift_pre = hidden(normed_two, lift_t)
    inner_grad = hidden(branch_grad, down_t)
    gate_act = apply_swish(gate_pre)
    inner = (gate_act * lift_pre).astype(BF16)
    gate_grad = (inner_grad * lift_pre * swish_slope(gate_pre)).astype(BF16)
    lift_grad = (inner_grad * gate_act).astype(BF16)
    normed_grad = jnp.einsum("pblf,fd->pbld", gate_grad, gate_t, preferred_element_type=F32)
    normed_grad = normed_grad + jnp.einsum(
        "pblf,fd->pbld", lift_grad, lift_t, preferred_element_type=F32
    )
    middle_grad = cotangent + norm_backward(
        middle, core_sum(normed_grad[0], normed_grad[1].astype(BF16))
    )
    branch = jnp.einsum("pblf,fd->pbld", inner, down_t, preferred_element_type=F32)
    branch = core_sum(branch[0], branch[1].astype(BF16))
    layer_output = (middle + mask_rows * branch).astype(BF16)

    def scattered(grad, masks, swapped):
        if swapped:
            grad = jnp.swapaxes(grad.reshape(2, 2, -1, width), 0, 1)
        return scatter_plane(grad.reshape(members, -1, width), masks).T

    gate_gradient = scattered(outer(gate_grad, normed_two), order_yx, False)
    lift_gradient = scattered(outer(lift_grad, normed_two), order_xy, True)
    down_gradient = scattered(outer(inner, branch_grad), order_yx, False)

    attended_grad = middle_grad.astype(BF16)
    attended_pair = (attended_grad, exchange(attended_grad, 1))
    modulate_grad, query_grad, key_grad, value_grad, state_grad = run(
        mixed_back_kernel, "mixed_back", spots,
        [
            (attended_pair[0], "rows"), (attended_pair[1], "rows"), (mixed, "pair"),
            (modulate, "pair"), (queries, "pair"), (query_pre, "pair"), (keys, "pair"),
            (values, "pair"), (mask_wide, "pair"), (cosine, "whole"), (sine, "whole"),
            (query_decay, "whole"), (decay_grid, "whole"), *state_inputs, *output_inputs,
        ],
        [
            (chip_shape, BF16, "pair"), (chip_shape, BF16, "pair"), (chip_shape, F32, "pair"),
            (chip_shape, F32, "pair"), (state_shape, BF16, "rows"),
        ],
        [wide_scratch, held_scratch, dma((members,)), dma((4,))],
        steps, 2 * square_flops,
    )
    later_inputs = [(p, "any") for p in carried(state_grad, block_decay, True)]
    part_shape = (half, 1, rows, cols)

    def square(name, order, a, *grads):
        shape = (half, len(grads), rows, cols)
        return run(
            functools.partial(outer_kernel, order), name, spots,
            [(a[0], "whole"), (a[1], "whole"), *[(g, "whole") for g in grads]],
            [(shape, BF16, "any"), (shape, BF16, "any")],
            [pltpu.VMEM((len(grads), width, inner_width), BF16), dma((len(grads), members))],
            1, len(grads) * square_flops,
        )

    def finish(parts, masks):
        total = (parts[0].astype(F32) + exchange(parts[1], masks[-1]).astype(F32)).astype(BF16)
        return scatter_plane(total, masks[:-1])

    output_gradient = finish(square("output_outer", 0, attended_pair, gated), order_xy)[0]
    (query_rows,) = run(
        rows_kernel, "query_rows", spots,
        [(query_grad, "pair"), (modulate_grad, "pair"), (query_parts[0], "any"), (query_parts[1], "any")],
        [((2, *row_shape), F32, "pair")],
        [wide_scratch, wide_scratch, dma((2, members))],
        steps, 2 * square_flops,
    )
    query_gradient, modulate_gradient = finish(
        square("query_outer", 0, normed_pair, query_grad, modulate_grad), order_xy
    )
    key_out, value_out, near_rows, far_rows = run(
        key_back_kernel, "key_back", spots,
        [
            (key_grad, "pair"), (value_grad, "pair"), (keys, "pair"), (values, "pair"),
            (key_pre, "pair"), (mask_wide, "pair"), (cosine, "whole"), (sine, "whole"),
            (key_decay, "whole"), (query_rows, "pair"), *later_inputs,
            (key_parts[0], "any"), (key_parts[1], "any"),
            (value_parts[0], "any"), (value_parts[1], "any"),
        ],
        [
            (chip_shape, BF16, "pair"), (chip_shape, BF16, "pair"), (row_shape, F32, "rows"),
            (row_shape, BF16, "rows"),
        ],
        [wide_scratch, wide_scratch, held_scratch, dma((2, members)), dma((4,))],
        steps, 2 * square_flops,
    )
    key_gradient = finish(square("key_outer", 0, normed_pair, key_out), order_xy)[0]
    value_gradient = finish(square("value_outer", 1, normed_pair, value_out), order_yx)[0]
    input_gradient = middle_grad + norm_backward(input_rows, core_sum(near_rows, far_rows))
    return (
        layer_output,
        input_gradient,
        query_gradient,
        key_gradient,
        value_gradient,
        modulate_gradient,
        output_gradient,
        gate_gradient,
        lift_gradient,
        down_gradient,
    )


def solution(mesh):
    placed = (
        P(None, ("wide", "narrow"), None),
        P("wide", "narrow"),
        P("wide", "narrow"),
        P("wide", "narrow"),
        P("wide", "narrow"),
        P("wide", "narrow"),
        P(None, ("wide", "narrow")),
        P(None, ("wide", "narrow")),
        P(None, ("wide", "narrow")),
        P("narrow"),
        P(),
        P(None, ("wide", "narrow"), None),
    )
    return jax.shard_map(
        on_device,
        mesh=mesh,
        in_specs=placed,
        out_specs=(
            P(None, ("wide", "narrow"), None),
            P(None, ("wide", "narrow"), None),
            P("wide", "narrow"),
            P("wide", "narrow"),
            P("wide", "narrow"),
            P("wide", "narrow"),
            P("wide", "narrow"),
            P(None, ("wide", "narrow")),
            P(None, ("wide", "narrow")),
            P(None, ("wide", "narrow")),
        ),
        check_vma=False,
    )
```

```python
import functools
import math

import jax
import jax.numpy as jnp
from jax import lax
from jax.experimental import pallas as pl
from jax.experimental.pallas import tpu as pltpu
from jax.sharding import PartitionSpec as P

EPS = 1e-06
AXES = ("wide", "narrow")
BF16 = jnp.bfloat16
F32 = jnp.float32


def simple_norm(values):
    return values * lax.rsqrt(jnp.mean(values * values, axis=-1, keepdims=True) + EPS)


def norm_backward(values, cotangent):
    scale = lax.rsqrt(jnp.mean(values * values, axis=-1, keepdims=True) + EPS)
    inner = jnp.mean(values * cotangent, axis=-1, keepdims=True)
    return scale * cotangent - values * (scale * scale * scale * inner)


def apply_swish(values):
    return values * jax.nn.sigmoid(values)


def swish_slope(values):
    sigmoid_value = jax.nn.sigmoid(values)
    return sigmoid_value + values * sigmoid_value * (1.0 - sigmoid_value)


def exchange(x, mask):
    count = lax.axis_size(AXES)
    return lax.ppermute(x, AXES, [(i, i ^ mask) for i in range(count)])


def after(x, *others):
    return lax.optimization_barrier((x, *others))[0]


def shift_z(x, step, reverse):
    count, unit = lax.axis_size(AXES), 2 * lax.axis_size("narrow")
    pairs = [(i, i + step * unit) for i in range(count - step * unit)]
    if reverse:
        pairs = [(b, a) for a, b in pairs]
    return lax.ppermute(x, AXES, pairs)


def gather_plane(x, masks):
    return gather_more(x[None], masks)


def gather_more(held, masks):
    for mask in masks:
        held = jnp.concatenate([held, exchange(held, mask)], axis=0)
    return held


def gather_hidden(x, masks, swapped):
    held = gather_plane(x, masks)
    if swapped:
        held = jnp.swapaxes(held.reshape(2, 2, -1, *x.shape), 0, 1)
    return held.reshape(-1, x.shape[-1])


def scatter_plane(x, masks):
    for mask in reversed(masks):
        half = x.shape[0] // 2
        got = exchange(x[half:], mask)
        total = x[:half].astype(F32) + got.astype(F32)
        x = total.astype(BF16) if half > 1 else total
    return x[0]


def relative(masks, index):
    out = 0
    for k, mask in enumerate(masks):
        out ^= mask * ((index >> k) & 1)
    return out


NT = (((1,), (1,)), ((), ()))
NN = (((1,), (0,)), ((), ()))
TN = (((0,), (0,)), ((), ()))


def mm(a, b, dims=NN):
    return lax.dot_general(a, b, dims, preferred_element_type=F32)


def turn(v, cosine, sine):
    return v * cosine + pltpu.roll(v, v.shape[-1] // 2, 1) * sine


def block_spots(masks):
    own = lax.axis_index(AXES)
    narrow_count = lax.axis_size("narrow")
    ids = jnp.array([relative(masks, i) for i in range(1 << len(masks))], jnp.int32) ^ own
    return jnp.stack([ids // narrow_count, (ids % narrow_count) // 2], axis=1)


def block_copy(spots, which, i, rows, cols, whole, part, sem, out):
    at = (
        pl.ds(pl.multiple_of(spots[which, i, 0] * rows, rows), rows),
        pl.ds(pl.multiple_of(spots[which, i, 1] * cols, cols), cols),
    )
    if out:
        return pltpu.make_async_copy(whole.at[at], part, sem)
    return pltpu.make_async_copy(part, whole.at[at], sem)


def each_block(spots, jobs, out=False):
    def go(method):
        for order, k, near, far, whole, sems in jobs:
            half, _, rows, cols = near.shape

            def step(i, _):
                for at, part in enumerate((near, far)):
                    copy = block_copy(
                        spots, order, i + at * half, rows, cols, whole, part.at[i, k],
                        sems.at[i + at * half], out,
                    )
                    getattr(copy, method)()
                return 0

            lax.fori_loop(0, half, step, 0)

    go("start")
    go("wait")


def both(near, far):
    rows = near.shape[0] * near.shape[1]
    return jnp.concatenate([near.reshape(rows, -1), far.reshape(rows, -1)], axis=0)


def slot_rows(x, s, size, count):
    return jnp.concatenate(
        [x[s * size : (s + 1) * size], x[(count + s) * size : (count + s + 1) * size]], axis=0
    )


def slot_back(parts, size):
    return jnp.concatenate([p[:size] for p in parts] + [p[size:] for p in parts], axis=0)


def put(ref, lanes, value):
    two, count, size, _ = ref.shape
    ref[:, :, :, lanes] = value.reshape(two, count, size, -1).astype(ref.dtype)


def get(ref, lanes=slice(None)):
    two, count, size, width = ref.shape
    x = ref[:, :, :, lanes]
    return x.reshape(two * count * size, x.shape[-1])


def key_value_kernel(
    spots, near, far, mask, cosine, sine, key_decay, kw0, kw1, vw0, vw1,
    key_pre, keys, values, state, wk, wv, sems
):
    @pl.when(pl.program_id(0) == 0)
    def _():
        each_block(spots, [(0, 0, kw0, kw1, wk, sems.at[0]), (1, 0, vw0, vw1, wv, sems.at[1])])

    count, size = near.shape[0], near.shape[1]
    x = both(near[...], far[...])
    valid = get(mask)
    head = cosine.shape[-1]
    pre = mm(x, wk[...])
    val_pre = mm(x, wv[...])
    for h in range(pre.shape[-1] // head):
        lanes = slice(h * head, (h + 1) * head)
        kp = pre[:, lanes]
        put(key_pre, lanes, kp)
        key = (valid * turn(kp * jax.nn.sigmoid(kp), cosine[...], sine[...])).astype(BF16)
        val = (valid * val_pre[:, lanes]).astype(BF16)
        put(keys, lanes, key)
        put(values, lanes, val)
        scaled = (key.astype(F32) * key_decay[:, lanes]).astype(BF16)
        for s in range(count):
            state[s, h] = mm(
                slot_rows(scaled, s, size, count), slot_rows(val, s, size, count), TN
            ).astype(BF16)


def query_kernel(
    spots, near, far, mask, cosine, sine, grid, keys, values, w0, w1,
    query_pre, queries, modulate, intra, wq, wm, sems
):
    @pl.when(pl.program_id(0) == 0)
    def _():
        each_block(spots, [(0, 0, w0, w1, wq, sems.at[0]), (0, 1, w0, w1, wm, sems.at[1])])

    count, size = near.shape[0], near.shape[1]
    x = both(near[...], far[...])
    valid = get(mask)
    head = cosine.shape[-1]
    pre = mm(x, wq[...])
    mod = mm(x, wm[...])
    for h in range(pre.shape[-1] // head):
        lanes = slice(h * head, (h + 1) * head)
        qp = pre[:, lanes]
        put(query_pre, lanes, qp)
        put(modulate, lanes, mod[:, lanes] * valid)
        q = turn(qp * jax.nn.sigmoid(qp), cosine[...], sine[...]).astype(BF16)
        put(queries, lanes, q)
        k, v = get(keys, lanes), get(values, lanes)
        parts = []
        for s in range(count):
            scores = mm(slot_rows(q, s, size, count), slot_rows(k, s, size, count), NT) * grid[h]
            parts.append(mm(scores.astype(BF16), slot_rows(v, s, size, count)))
        put(intra, lanes, slot_back(parts, size))


def load_states(spots, pieces, held, sems):
    member = spots[2, 0, 0]
    copies = [
        pltpu.make_async_copy(p, held.at[member ^ k], sems.at[k]) for k, p in enumerate(pieces)
    ]
    for c in copies:
        c.start()
    for c in copies:
        c.wait()


def mixed_kernel(
    spots, queries, intra, modulate, query_decay, s0, s1, s2, s3, w0, w1,
    mixed, gated, near_out, far_out, wo, held, sems, state_sems
):
    @pl.when(pl.program_id(0) == 0)
    def _():
        load_states(spots, (s0, s1, s2, s3), held, state_sems)
        each_block(spots, [(1, 0, w0, w1, wo, sems)])

    step = pl.program_id(0)
    _, count, size, width = queries.shape
    heads = held.shape[2]
    head = width // heads
    gates = []
    for h in range(heads):
        lanes = slice(h * head, (h + 1) * head)
        q = (get(queries, lanes).astype(F32) * query_decay[:, lanes]).astype(BF16)
        parts = [mm(slot_rows(q, s, size, count), held[step, s, h]) for s in range(count)]
        mix = get(intra, lanes) + slot_back(parts, size)
        put(mixed, lanes, mix)
        scale = lax.rsqrt(jnp.mean(mix * mix, axis=-1, keepdims=True) + EPS)
        gates.append((mix * scale * get(modulate, lanes)).astype(BF16))
    gate = jnp.concatenate(gates, axis=1)
    put(gated, slice(None), gate)
    out = mm(gate, wo[...], NT)
    near_out[...] = out[: count * size].reshape(near_out.shape)
    far_out[...] = out[count * size :].astype(BF16).reshape(far_out.shape)


def mixed_back_kernel(
    spots, near, far, mixed, modulate, queries, query_pre, keys, values, mask, cosine, sine,
    query_decay, grid, s0, s1, s2, s3, w0, w1,
    modulate_grad, query_grad, key_grad, value_grad, state_grad, wo, held, sems, state_sems
):
    @pl.when(pl.program_id(0) == 0)
    def _():
        load_states(spots, (s0, s1, s2, s3), held, state_sems)
        each_block(spots, [(1, 0, w0, w1, wo, sems)])

    step = pl.program_id(0)
    _, count, size, width = queries.shape
    heads = held.shape[2]
    head = width // heads
    gate_grad = mm(both(near[...], far[...]), wo[...])
    valid = get(mask)
    for h in range(heads):
        lanes = slice(h * head, (h + 1) * head)
        mix = get(mixed, lanes)
        scale = lax.rsqrt(jnp.mean(mix * mix, axis=-1, keepdims=True) + EPS)
        gg = gate_grad[:, lanes]
        put(modulate_grad, lanes, gg * valid * (mix * scale))
        cot = gg * get(modulate, lanes)
        inner = jnp.mean(mix * cot, axis=-1, keepdims=True)
        gm = (scale * cot - mix * (scale * scale * scale * inner)).astype(BF16)
        q, k, v = get(queries, lanes), get(keys, lanes), get(values, lanes)
        qs = (q.astype(F32) * query_decay[:, lanes]).astype(BF16)
        gq, gk, gv = [], [], []
        for s in range(count):
            pick = lambda x: slot_rows(x, s, size, count)
            gms, qq, kk, vv = pick(gm), pick(q), pick(k), pick(v)
            gs = (mm(gms, vv, NT) * grid[h]).astype(BF16)
            sc = (mm(qq, kk, NT) * grid[h]).astype(BF16)
            gv.append(mm(sc, gms, TN))
            gk.append(mm(gs, qq, TN))
            decay = slot_rows(query_decay[:, lanes], s, size, count)
            gq.append(mm(gs, kk) + mm(gms, held[step, s, h], NT) * decay)
            state_grad[s, h] = mm(pick(qs), gms, TN).astype(BF16)
        put(key_grad, lanes, slot_back(gk, size))
        put(value_grad, lanes, slot_back(gv, size))
        qp = get(query_pre, lanes)
        sg = jax.nn.sigmoid(qp)
        slope = sg + qp * sg * (1.0 - sg)
        put(query_grad, lanes, turn(slot_back(gq, size), cosine[...], -sine[...]) * slope)


def rows_kernel(spots, query_grad, modulate_grad, w0, w1, out, wq, wm, sems):
    @pl.when(pl.program_id(0) == 0)
    def _():
        each_block(spots, [(0, 0, w0, w1, wq, sems.at[0]), (0, 1, w0, w1, wm, sems.at[1])])

    put(out, slice(None), mm(get(query_grad), wq[...], NT) + mm(get(modulate_grad), wm[...], NT))


def key_back_kernel(
    spots, key_grad, value_grad, keys, values, key_pre, mask, cosine, sine, key_decay, rows_in,
    g0, g1, g2, g3, kw0, kw1, vw0, vw1,
    key_out, value_out, near_out, far_out, wk, wv, held, sems, state_sems
):
    @pl.when(pl.program_id(0) == 0)
    def _():
        load_states(spots, (g0, g1, g2, g3), held, state_sems)
        each_block(spots, [(0, 0, kw0, kw1, wk, sems.at[0]), (1, 0, vw0, vw1, wv, sems.at[1])])

    step = pl.program_id(0)
    _, count, size, width = keys.shape
    heads = held.shape[2]
    head = width // heads
    valid = get(mask)
    gks, gvs = [], []
    for h in range(heads):
        lanes = slice(h * head, (h + 1) * head)
        decay = key_decay[:, lanes]
        k, v = get(keys, lanes), get(values, lanes)
        scaled = (k.astype(F32) * decay).astype(BF16)
        pk = [mm(slot_rows(v, s, size, count), held[step, s, h], NT) for s in range(count)]
        pv = [mm(slot_rows(scaled, s, size, count), held[step, s, h]) for s in range(count)]
        gk = get(key_grad, lanes) + slot_back(pk, size) * decay
        gv = get(value_grad, lanes) + slot_back(pv, size)
        kp = get(key_pre, lanes)
        sg = jax.nn.sigmoid(kp)
        slope = sg + kp * sg * (1.0 - sg)
        gks.append((turn(gk * valid, cosine[...], -sine[...]) * slope).astype(BF16))
        gvs.append((gv * valid).astype(BF16))
    gk, gv = jnp.concatenate(gks, axis=1), jnp.concatenate(gvs, axis=1)
    put(key_out, slice(None), gk)
    put(value_out, slice(None), gv)
    out = get(rows_in) + mm(gk, wk[...], NT) + mm(gv, wv[...], NT)
    near_out[...] = out[: count * size].reshape(near_out.shape)
    far_out[...] = out[count * size :].astype(BF16).reshape(far_out.shape)


def outer_kernel(order, spots, near, far, *refs):
    count = (len(refs) - 4) // 1
    grads, (keep, send, whole, sems) = refs[:count], refs[count:]
    rows = near.shape[0] * near.shape[1]
    width = near.shape[2]
    tile = 256
    for c in range(0, width, tile):
        a = near[:, :, c : c + tile].reshape(rows, tile)
        b = far[:, :, c : c + tile].reshape(rows, tile)
        for k, g in enumerate(grads):
            g0 = g[0].reshape(rows, -1)
            g1 = g[1].reshape(rows, -1)
            whole[k, c : c + tile, :] = (mm(a, g0, TN) + mm(b, g1, TN)).astype(BF16)
    each_block(
        spots, [(order, k, keep, send, whole.at[k], sems.at[k]) for k in range(count)], out=True
    )


ANY = pl.BlockSpec(memory_space=pl.ANY)
VMEM = pl.BlockSpec(memory_space=pltpu.VMEM)


def run(kernel, name, spots, inputs, outputs, scratch, steps, flops):
    def spec(shape, kind):
        if kind == "any":
            return ANY
        if kind == "rows":
            size = shape[0] // steps
            return pl.BlockSpec((size, *shape[1:]), lambda i, _: (i,) + (0,) * (len(shape) - 1))
        if kind == "pair":
            size = shape[1] // steps
            return pl.BlockSpec(
                (2, size, *shape[2:]), lambda i, _: (0, i) + (0,) * (len(shape) - 2)
            )
        return pl.BlockSpec(shape, lambda i, _: (0,) * len(shape))

    moved = sum(a.size * a.dtype.itemsize for a, _ in inputs)
    moved += sum(math.prod(s) * jnp.dtype(d).itemsize for s, d, _ in outputs)
    return pl.pallas_call(
        kernel,
        out_shape=[jax.ShapeDtypeStruct(s, d) for s, d, _ in outputs],
        grid_spec=pltpu.PrefetchScalarGridSpec(
            num_scalar_prefetch=1,
            grid=(steps,),
            in_specs=[spec(a.shape, kind) for a, kind in inputs],
            out_specs=[spec(s, kind) for s, _, kind in outputs],
            scratch_shapes=scratch,
        ),
        compiler_params=pltpu.CompilerParams(vmem_limit_bytes=40 * 2**20),
        cost_estimate=pl.CostEstimate(flops=flops, bytes_accessed=moved, transcendentals=0),
        name=name,
    )(spots, *[a for a, _ in inputs])


class Carry:
    def __init__(self, local, block_decay, reverse):
        self.local, self.reverse = local, reverse
        narrow_count = lax.axis_size("narrow")
        self.member = 2 * (lax.axis_index("wide") % 2) + lax.axis_index("narrow") // 2
        self.masks = [0, 2, narrow_count, narrow_count + 2]
        ranks = [self.member ^ k for k in range(4)]
        self.ranks = [3 - r if reverse else r for r in ranks]
        self.log_decay = jnp.log(block_decay)

    def power(self, e):
        return jnp.exp(e * self.log_decay)[None, :, None, None]

    def spread(self):
        share = self.local.shape[0] // 4
        parts = [
            lax.dynamic_slice_in_dim(self.local, (self.member ^ k) * share, share, 0)
            for k in range(4)
        ]
        self.got = [parts[0]] + [exchange(parts[k], self.masks[k]) for k in range(1, 4)]

    def along(self):
        self.held = [h.astype(F32) for h in self.got]
        span = sum(self.power((3 - self.ranks[k]).astype(F32)) * self.held[k] for k in range(4))
        before, step = 0.0, 1
        while step < lax.axis_size("wide") // 2:
            got = shift_z(span.astype(BF16), step, self.reverse).astype(F32)
            before = before + self.power(4.0 * (step - 1)) * got
            span = span + self.power(4.0 * step) * got
            step *= 2
        self.before = before

    def back(self):
        sent = []
        for k in range(4):
            state = self.power(self.ranks[k].astype(F32)) * self.before
            for j in range(4):
                gap = (self.ranks[k] - 1 - self.ranks[j]).astype(F32)
                scale = jnp.where(gap >= 0, self.power(jnp.maximum(gap, 0.0)), 0.0)
                state = state + scale * self.held[j]
            sent.append(state.astype(BF16))
        return [sent[0]] + [exchange(sent[k], self.masks[k]) for k in range(1, 4)]


def on_device(
    layer_input,
    query_weight,
    key_weight,
    value_weight,
    modulate_weight,
    output_weight,
    gate_matrix,
    lift_matrix,
    down_matrix,
    decay_factor,
    valid_lengths,
    output_cotangent,
):
    narrow_count, wide_count = lax.axis_size("narrow"), lax.axis_size("wide")
    wide_index, narrow_index = lax.axis_index("wide"), lax.axis_index("narrow")
    core, side = narrow_index % 2, narrow_index // 2
    slots, quarter, width = layer_input.shape
    block = 2 * quarter
    rows, cols = query_weight.shape
    heads = 2 * decay_factor.shape[0]
    head_size = cols // decay_factor.shape[0]
    x_mask = 2
    wide_masks = []
    bit = narrow_count
    while bit < narrow_count * wide_count:
        wide_masks.append(bit)
        bit *= 2
    y_mask, z_masks = wide_masks[0], wide_masks[:0:-1]
    order_yx = z_masks + [y_mask, x_mask]
    order_xy = z_masks + [x_mask, y_mask]
    members = 1 << len(order_yx)
    half = members // 2

    base = wide_index * (quarter * narrow_count) + side * block
    offsets = jnp.stack(
        [core * quarter + jnp.arange(quarter), (1 - core) * quarter + jnp.arange(quarter)]
    ).astype(jnp.int32)
    mask = ((base + offsets)[:, None, :] < valid_lengths[None, :, None]).astype(F32)
    mask_rows = mask[0][:, :, None]
    mask_wide = jnp.broadcast_to(mask[..., None], (2, slots, quarter, head_size))
    member = 2 * (wide_index % 2) + side
    spots = jnp.concatenate(
        [
            block_spots(order_xy)[None],
            block_spots(order_yx)[None],
            jnp.broadcast_to(member, (1, members, 2)).astype(jnp.int32),
        ]
    )

    def core_sum(near, far):
        return near + exchange(far, 1).astype(F32)

    other_decay = exchange(decay_factor, x_mask)
    decay = jnp.concatenate(
        [jnp.where(side == 0, decay_factor, other_decay), jnp.where(side == 0, other_decay, decay_factor)]
    )
    log_decay = jnp.log(decay)
    block_decay = jnp.exp(block * log_decay)
    steps = 4
    count = slots // steps

    def table(values):
        lanes = values.shape[-1]
        return jnp.broadcast_to(values[:, None], (2, count, quarter, lanes)).reshape(-1, lanes)

    half_head = head_size // 2
    frequency = jnp.exp(-math.log(10000.0) * jnp.arange(half_head, dtype=F32) / half_head)
    phase = (base + offsets).astype(F32)[..., None] * frequency
    cosine, sine = jnp.cos(phase), jnp.sin(phase)
    cosine = table(jnp.concatenate([cosine, cosine], axis=-1))
    sine = table(jnp.concatenate([-sine, sine], axis=-1))
    spot = offsets.astype(F32)
    log_lanes = jnp.repeat(log_decay, head_size)
    query_decay = table(jnp.exp((spot[..., None] + 1.0) * log_lanes))
    key_decay = table(jnp.exp((block - 1.0 - spot[..., None]) * log_lanes))
    flat = spot.reshape(-1)
    gap = flat[:, None] - flat[None, :]
    decay_grid = jnp.where(
        gap[None] >= 0.0, jnp.exp(jnp.maximum(gap, 0.0)[None] * log_decay[:, None, None]), 0.0
    )

    def join(*parts):
        return jnp.concatenate(parts, axis=0)

    z_far, z_near = z_masks[:-1], z_masks[-1]
    swap = exchange

    def tie(*arrays):
        return lax.optimization_barrier(arrays)

    def far_steps(x):
        for m in z_far:
            x = join(x, swap(x, m))
        return x

    kv = jnp.stack([key_weight, value_weight])[None]
    dn = down_matrix.T[None]
    gl = jnp.stack([gate_matrix.T, lift_matrix.T])[None]
    qmo = jnp.stack([query_weight, modulate_weight, output_weight])[None]
    input_rows = layer_input.astype(F32)
    normed = simple_norm(input_rows).astype(BF16)
    normed_pair = (normed, swap(normed, 1))
    kv, dn_x = tie(far_steps(kv), swap(dn, x_mask))
    dn = join(dn, dn_x)
    kv_z, dn_y = tie(swap(kv, z_near), swap(dn, y_mask))
    kv, dn = join(kv, kv_z), join(dn, dn_y)
    k_half, v_half = kv[:, :1], kv[:, 1:]
    qmo, k_half, v_half = tie(qmo, k_half, v_half)
    k_x, v_y, qmo = tie(swap(k_half, x_mask), swap(v_half, y_mask), far_steps(qmo))
    k_half, v_half = join(k_half, k_x), join(v_half, v_y)
    k_far, v_far, qmo_z = tie(swap(k_half, y_mask), swap(v_half, x_mask), swap(qmo, z_near))
    key_parts, value_parts = (k_half, k_far), (v_half, v_far)
    qmo = join(qmo, qmo_z)
    qm, out_w = qmo[:, :2], qmo[:, 2:]
    gl = after(gl, qmo_z)
    qm_x, o_y = swap(qm, x_mask), swap(out_w, y_mask)
    gl = far_steps(gl)
    inner_width = heads * head_size
    chip_shape = (2, slots, quarter, inner_width)
    row_shape = (slots, quarter, width)
    state_shape = (slots, heads, head_size, head_size)
    square_flops = 2 * 2 * slots * quarter * width * inner_width
    wide_scratch = pltpu.VMEM((width, inner_width), BF16)
    held_scratch = pltpu.VMEM((4, slots // 4, heads, head_size, head_size), BF16)
    dma = pltpu.SemaphoreType.DMA

    key_pre, keys, values, local_state = run(
        key_value_kernel, "key_value", spots,
        [
            (normed_pair[0], "rows"), (normed_pair[1], "rows"), (mask_wide, "pair"),
            (cosine, "whole"), (sine, "whole"), (key_decay, "whole"),
            (key_parts[0], "any"), (key_parts[1], "any"),
            (value_parts[0], "any"), (value_parts[1], "any"),
        ],
        [
            (chip_shape, F32, "pair"), (chip_shape, BF16, "pair"), (chip_shape, BF16, "pair"),
            (state_shape, BF16, "rows"),
        ],
        [wide_scratch, wide_scratch, dma((2, members))],
        steps, 2 * square_flops,
    )
    local_state, qm_x, o_y = tie(local_state, qm_x, o_y)
    qm, out_w = join(qm, qm_x), join(out_w, o_y)
    scan = Carry(local_state, block_decay, False)
    scan.spread()
    *scan.got, gl = tie(*scan.got, gl)
    qm_y, o_x = swap(qm, y_mask), swap(out_w, x_mask)
    gl_z = swap(gl, z_near)
    scan.along()
    scan.before, qm_y, o_x, gl_z = tie(scan.before, qm_y, o_x, gl_z)
    gl = join(gl, gl_z)
    query_parts, output_parts = (qm, qm_y), (out_w, o_x)
    dn = after(dn, gl_z)
    dn = far_steps(dn)
    state_parts = scan.back()
    query_pre, queries, modulate, intra = run(
        query_kernel, "query", spots,
        [
            (normed_pair[0], "rows"), (normed_pair[1], "rows"), (mask_wide, "pair"),
            (cosine, "whole"), (sine, "whole"), (decay_grid, "whole"),
            (keys, "pair"), (values, "pair"), (query_parts[0], "any"), (query_parts[1], "any"),
        ],
        [
            (chip_shape, F32, "pair"), (chip_shape, BF16, "pair"), (chip_shape, F32, "pair"),
            (chip_shape, F32, "pair"),
        ],
        [wide_scratch, wide_scratch, dma((2, members))],
        steps, 2 * square_flops,
    )
    *state_parts, queries = tie(*state_parts, queries)
    gate_w, lift_w = after(gl, *state_parts)[:, 0], after(gl, *state_parts)[:, 1]
    gate_y, lift_x = swap(gate_w, y_mask), swap(lift_w, x_mask)
    state_inputs = [(p, "any") for p in state_parts]
    output_inputs = [(p, "any") for p in output_parts]
    mixed, gated, near_att, far_att = run(
        mixed_kernel, "mixed", spots,
        [
            (queries, "pair"), (intra, "pair"), (modulate, "pair"), (query_decay, "whole"),
            *state_inputs, *output_inputs,
        ],
        [
            (chip_shape, F32, "pair"), (chip_shape, BF16, "pair"), (row_shape, F32, "rows"),
            (row_shape, BF16, "rows"),
        ],
        [wide_scratch, held_scratch, dma((members,)), dma((4,))],
        steps, square_flops,
    )
    near_att, gate_y, lift_x, dn = tie(near_att, gate_y, lift_x, dn)
    gate_w, lift_w = join(gate_w, gate_y), join(lift_w, lift_x)
    gate_x, lift_y, dn_z = swap(gate_w, x_mask), swap(lift_w, y_mask), swap(dn, z_near)
    middle = input_rows + core_sum(near_att, far_att)
    bulk = half // 2
    gate_t = join(gate_w, gate_x).reshape(-1, width)
    lift_t = jnp.stack(
        [lift_w.reshape(2, bulk, -1, width), lift_y.reshape(2, bulk, -1, width)], axis=1
    ).reshape(-1, width)
    down_t = jnp.moveaxis(join(dn, dn_z).reshape(bulk, 4, -1, width), 0, 1)
    down_t = jnp.swapaxes(down_t.reshape(2, 2, bulk, -1, width), 0, 1).reshape(-1, width)

    def pair(mine):
        return jnp.stack([mine, exchange(mine, 1)])

    normed_two = pair(simple_norm(middle).astype(BF16))
    cotangent = output_cotangent.astype(F32)
    branch_grad = pair((mask_rows * cotangent).astype(BF16))

    def hidden(rows_in, matrix):
        return jnp.einsum("pbld,fd->pblf", rows_in, matrix, preferred_element_type=F32)

    def outer(a, b):
        return jnp.einsum("pblf,pbld->fd", a, b, preferred_element_type=F32).astype(BF16)

    gate_pre = hidden(normed_two, gate_t)
    lift_pre = hidden(normed_two, lift_t)
    inner_grad = hidden(branch_grad, down_t)
    gate_act = apply_swish(gate_pre)
    inner = (gate_act * lift_pre).astype(BF16)
    gate_grad = (inner_grad * lift_pre * swish_slope(gate_pre)).astype(BF16)
    lift_grad = (inner_grad * gate_act).astype(BF16)
    normed_grad = jnp.einsum("pblf,fd->pbld", gate_grad, gate_t, preferred_element_type=F32)
    normed_grad = normed_grad + jnp.einsum(
        "pblf,fd->pbld", lift_grad, lift_t, preferred_element_type=F32
    )
    middle_grad = cotangent + norm_backward(
        middle, core_sum(normed_grad[0], normed_grad[1].astype(BF16))
    )
    branch = jnp.einsum("pblf,fd->pbld", inner, down_t, preferred_element_type=F32)
    branch = core_sum(branch[0], branch[1].astype(BF16))
    layer_output = (middle + mask_rows * branch).astype(BF16)

    def fold(mine, got):
        return (mine.astype(F32) + got.astype(F32)).astype(BF16)

    def final(mine, got):
        return mine.astype(F32) + got.astype(F32)

    gate_g = outer(gate_grad, normed_two).reshape(2, half, -1, width)
    lift_g = outer(lift_grad, normed_two).reshape(2, 2, bulk, -1, width)
    down_g = outer(inner, branch_grad).reshape(2, 2, 2, bulk // 2, -1, width)
    gate_x = swap(gate_g[1], x_mask)
    lift_y = swap(lift_g[:, 1], y_mask)
    down_z = swap(down_g[:, :, 1], z_near)
    attended_grad = middle_grad.astype(BF16)
    attended_pair = (attended_grad, exchange(attended_grad, 1))
    modulate_grad, query_grad, key_grad, value_grad, state_grad = run(
        mixed_back_kernel, "mixed_back", spots,
        [
            (attended_pair[0], "rows"), (attended_pair[1], "rows"), (mixed, "pair"),
            (modulate, "pair"), (queries, "pair"), (query_pre, "pair"), (keys, "pair"),
            (values, "pair"), (mask_wide, "pair"), (cosine, "whole"), (sine, "whole"),
            (query_decay, "whole"), (decay_grid, "whole"), *state_inputs, *output_inputs,
        ],
        [
            (chip_shape, BF16, "pair"), (chip_shape, BF16, "pair"), (chip_shape, F32, "pair"),
            (chip_shape, F32, "pair"), (state_shape, BF16, "rows"),
        ],
        [wide_scratch, held_scratch, dma((members,)), dma((4,))],
        steps, 2 * square_flops,
    )
    state_grad, gate_x, lift_y = tie(state_grad, gate_x, lift_y)
    gate_g = fold(gate_g[0], gate_x)
    lift_g = fold(lift_g[:, 0], lift_y)
    scan = Carry(state_grad, block_decay, True)
    scan.spread()

    def square(name, order, a, *grads):
        shape = (half, len(grads), rows, cols)
        return run(
            functools.partial(outer_kernel, order), name, spots,
            [(a[0], "whole"), (a[1], "whole"), *[(g, "whole") for g in grads]],
            [(shape, BF16, "any"), (shape, BF16, "any")],
            [pltpu.VMEM((len(grads), width, inner_width), BF16), dma((len(grads), members))],
            1, len(grads) * square_flops,
        )

    output_keep, output_send = square("output_outer", 1, attended_pair, gated)
    query_keep, query_send = square("query_outer", 0, normed_pair, query_grad, modulate_grad)
    (query_rows,) = run(
        rows_kernel, "query_rows", spots,
        [(query_grad, "pair"), (modulate_grad, "pair"), (query_parts[0], "any"), (query_parts[1], "any")],
        [((2, *row_shape), F32, "pair")],
        [wide_scratch, wide_scratch, dma((2, members))],
        steps, 2 * square_flops,
    )
    *scan.got, down_z, gate_g, lift_g = tie(*scan.got, down_z, gate_g, lift_g)
    gate_y, lift_x = swap(gate_g[bulk:], y_mask), swap(lift_g[1], x_mask)
    output_x, query_y = swap(output_send, x_mask), swap(query_send, y_mask)
    down_g = fold(down_g[:, :, 0], down_z)
    scan.along()
    scan.before, gate_y, lift_x, output_x, query_y, query_rows = tie(
        scan.before, gate_y, lift_x, output_x, query_y, query_rows
    )
    later_parts = scan.back()
    gate_lift = jnp.stack([fold(gate_g[:bulk], gate_y), fold(lift_g[0], lift_x)], axis=1)
    output_g, query_g = fold(output_keep, output_x), fold(query_keep, query_y)
    near = bulk // 2
    gl_z = swap(gate_lift[near:], z_near)
    *later_parts, gl_z = tie(*later_parts, gl_z)
    gate_lift = fold(gate_lift[:near], gl_z)
    later_inputs = [(p, "any") for p in later_parts]
    quad = half // 2
    down_g, output_g, query_g = tie(down_g, output_g, query_g, *later_parts)[:3]
    output_y, query_x = swap(output_g[quad:], y_mask), swap(query_g[quad:], x_mask)

    def far_folds(x):
        for m in reversed(z_far):
            size = x.shape[0] // 2
            x = (fold if size > 1 else final)(x[:size], swap(x[size:], m))
        return x[0]

    down_far = jnp.moveaxis(down_g, 2, 0)
    for m in reversed(z_far):
        size = down_far.shape[0] // 2
        down_far = fold(down_far[:size], swap(down_far[size:], m))
    down_g = down_far[0]
    gate_lift = far_folds(gate_lift)
    key_out, value_out, near_rows, far_rows = run(
        key_back_kernel, "key_back", spots,
        [
            (key_grad, "pair"), (value_grad, "pair"), (keys, "pair"), (values, "pair"),
            (key_pre, "pair"), (mask_wide, "pair"), (cosine, "whole"), (sine, "whole"),
            (key_decay, "whole"), (query_rows, "pair"), *later_inputs,
            (key_parts[0], "any"), (key_parts[1], "any"),
            (value_parts[0], "any"), (value_parts[1], "any"),
        ],
        [
            (chip_shape, BF16, "pair"), (chip_shape, BF16, "pair"), (row_shape, F32, "rows"),
            (row_shape, BF16, "rows"),
        ],
        [wide_scratch, wide_scratch, held_scratch, dma((2, members)), dma((4,))],
        steps, 2 * square_flops,
    )
    key_out, value_out, output_y, query_x = tie(key_out, value_out, output_y, query_x)
    key_keep, key_send = square("key_outer", 0, normed_pair, key_out)
    value_keep, value_send = square("value_outer", 1, normed_pair, value_out)
    key_y, value_x = swap(key_send, y_mask), swap(value_send, x_mask)
    qmo_g = jnp.concatenate(
        [fold(query_g[:quad], query_x), fold(output_g[:quad], output_y)], axis=1
    )
    qmo_z = swap(qmo_g[near:], z_near)
    down_y = swap(down_g[:, 1], y_mask)
    key_g, value_g = fold(key_keep, key_y), fold(value_keep, value_x)
    down_g = fold(down_g[:, 0], down_y)
    qmo_g = fold(qmo_g[:near], qmo_z)
    key_x, value_y = swap(key_g[quad:], x_mask), swap(value_g[quad:], y_mask)
    down_x = swap(down_g[1], x_mask)
    query_gradient, modulate_gradient, output_gradient = far_folds(qmo_g)
    down_gradient = final(down_g[0], down_x).T
    gate_gradient, lift_gradient = gate_lift[0].T, gate_lift[1].T
    kv_g = jnp.concatenate([fold(key_g[:quad], key_x), fold(value_g[:quad], value_y)], axis=1)
    kv_z = swap(kv_g[near:], z_near)
    key_gradient, value_gradient = far_folds(fold(kv_g[:near], kv_z))
    input_gradient = middle_grad + norm_backward(input_rows, core_sum(near_rows, far_rows))
    return (
        layer_output,
        input_gradient,
        query_gradient,
        key_gradient,
        value_gradient,
        modulate_gradient,
        output_gradient,
        gate_gradient,
        lift_gradient,
        down_gradient,
    )


def solution(mesh):
    placed = (
        P(None, ("wide", "narrow"), None),
        P("wide", "narrow"),
        P("wide", "narrow"),
        P("wide", "narrow"),
        P("wide", "narrow"),
        P("wide", "narrow"),
        P(None, ("wide", "narrow")),
        P(None, ("wide", "narrow")),
        P(None, ("wide", "narrow")),
        P("narrow"),
        P(),
        P(None, ("wide", "narrow"), None),
    )
    return jax.shard_map(
        on_device,
        mesh=mesh,
        in_specs=placed,
        out_specs=(
            P(None, ("wide", "narrow"), None),
            P(None, ("wide", "narrow"), None),
            P("wide", "narrow"),
            P("wide", "narrow"),
            P("wide", "narrow"),
            P("wide", "narrow"),
            P("wide", "narrow"),
            P(None, ("wide", "narrow")),
            P(None, ("wide", "narrow")),
            P(None, ("wide", "narrow")),
        ),
        check_vma=False,
    )
```

```python
import functools
import math

import jax
import jax.numpy as jnp
from jax import lax
from jax.experimental import pallas as pl
from jax.experimental.pallas import tpu as pltpu
from jax.sharding import PartitionSpec as P

EPS = 1e-06
AXES = ("wide", "narrow")
BF16 = jnp.bfloat16
F32 = jnp.float32


def simple_norm(values):
    return values * lax.rsqrt(jnp.mean(values * values, axis=-1, keepdims=True) + EPS)


def norm_backward(values, cotangent):
    scale = lax.rsqrt(jnp.mean(values * values, axis=-1, keepdims=True) + EPS)
    inner = jnp.mean(values * cotangent, axis=-1, keepdims=True)
    return scale * cotangent - values * (scale * scale * scale * inner)


def apply_swish(values):
    return values * jax.nn.sigmoid(values)


def swish_slope(values):
    sigmoid_value = jax.nn.sigmoid(values)
    return sigmoid_value + values * sigmoid_value * (1.0 - sigmoid_value)


def exchange(x, mask):
    count = lax.axis_size(AXES)
    return lax.ppermute(x, AXES, [(i, i ^ mask) for i in range(count)])


def after(x, *others):
    return lax.optimization_barrier((x, *others))[0]


def shift_z(x, step, reverse):
    count, unit = lax.axis_size(AXES), 2 * lax.axis_size("narrow")
    pairs = [(i, i + step * unit) for i in range(count - step * unit)]
    if reverse:
        pairs = [(b, a) for a, b in pairs]
    return lax.ppermute(x, AXES, pairs)


def gather_plane(x, masks):
    return gather_more(x[None], masks)


def gather_more(held, masks):
    for mask in masks:
        held = jnp.concatenate([held, exchange(held, mask)], axis=0)
    return held


def gather_hidden(x, masks, swapped):
    held = gather_plane(x, masks)
    if swapped:
        held = jnp.swapaxes(held.reshape(2, 2, -1, *x.shape), 0, 1)
    return held.reshape(-1, x.shape[-1])


def scatter_plane(x, masks):
    for mask in reversed(masks):
        half = x.shape[0] // 2
        got = exchange(x[half:], mask)
        total = x[:half].astype(F32) + got.astype(F32)
        x = total.astype(BF16) if half > 1 else total
    return x[0]


def fold(mine, got, dtype=BF16):
    return (mine.astype(F32) + got.astype(F32)).astype(dtype)


def final(mine, got):
    return fold(mine, got, F32)


def relative(masks, index):
    out = 0
    for k, mask in enumerate(masks):
        out ^= mask * ((index >> k) & 1)
    return out


NT = (((1,), (1,)), ((), ()))
NN = (((1,), (0,)), ((), ()))
TN = (((0,), (0,)), ((), ()))


def mm(a, b, dims=NN):
    return lax.dot_general(a, b, dims, preferred_element_type=F32)


def turn(v, cosine, sine):
    return v * cosine + pltpu.roll(v, v.shape[-1] // 2, 1) * sine


def block_spots(masks):
    own = lax.axis_index(AXES)
    narrow_count = lax.axis_size("narrow")
    ids = jnp.array([relative(masks, i) for i in range(1 << len(masks))], jnp.int32) ^ own
    return jnp.stack([ids // narrow_count, (ids % narrow_count) // 2], axis=1)


def block_copy(spots, which, i, rows, cols, whole, part, sem, out):
    at = (
        pl.ds(pl.multiple_of(spots[which, i, 0] * rows, rows), rows),
        pl.ds(pl.multiple_of(spots[which, i, 1] * cols, cols), cols),
    )
    if out:
        return pltpu.make_async_copy(whole.at[at], part, sem)
    return pltpu.make_async_copy(part, whole.at[at], sem)


def each_block(spots, jobs, out=False):
    def go(method):
        for order, k, near, far, whole, sems in jobs:
            half, _, rows, cols = near.shape

            def step(i, _):
                for at, part in enumerate((near, far)):
                    copy = block_copy(
                        spots, order, i + at * half, rows, cols, whole, part.at[i, k],
                        sems.at[i + at * half], out,
                    )
                    getattr(copy, method)()
                return 0

            lax.fori_loop(0, half, step, 0)

    go("start")
    go("wait")


def both(near, far):
    rows = near.shape[0] * near.shape[1]
    return jnp.concatenate([near.reshape(rows, -1), far.reshape(rows, -1)], axis=0)


def slot_rows(x, s, size, count):
    return jnp.concatenate(
        [x[s * size : (s + 1) * size], x[(count + s) * size : (count + s + 1) * size]], axis=0
    )


def slot_back(parts, size):
    return jnp.concatenate([p[:size] for p in parts] + [p[size:] for p in parts], axis=0)


def put(ref, lanes, value):
    two, count, size, _ = ref.shape
    ref[:, :, :, lanes] = value.reshape(two, count, size, -1).astype(ref.dtype)


def get(ref, lanes=slice(None)):
    two, count, size, width = ref.shape
    x = ref[:, :, :, lanes]
    return x.reshape(two * count * size, x.shape[-1])


def key_value_kernel(
    spots, near, far, mask, cosine, sine, key_decay, kw0, kw1, vw0, vw1,
    key_pre, keys, values, state, wk, wv, sems
):
    @pl.when(pl.program_id(0) == 0)
    def _():
        each_block(spots, [(0, 0, kw0, kw1, wk, sems.at[0]), (2, 0, vw0, vw1, wv, sems.at[1])])

    count, size = near.shape[0], near.shape[1]
    x = both(near[...], far[...])
    valid = get(mask).astype(F32)
    head = cosine.shape[-1]
    pre = mm(x, wk[...])
    val_pre = mm(x, wv[...])
    for h in range(pre.shape[-1] // head):
        lanes = slice(h * head, (h + 1) * head)
        kp = pre[:, lanes]
        put(key_pre, lanes, kp)
        key = (valid * turn(kp * jax.nn.sigmoid(kp), cosine[...], sine[...])).astype(BF16)
        val = (valid * val_pre[:, lanes]).astype(BF16)
        put(keys, lanes, key)
        put(values, lanes, val)
        scaled = (key.astype(F32) * key_decay[:, lanes]).astype(BF16)
        for s in range(count):
            state[s, h] = mm(
                slot_rows(scaled, s, size, count), slot_rows(val, s, size, count), TN
            ).astype(BF16)


def query_kernel(
    spots, near, far, mask, cosine, sine, grid, keys, values, w0, w1,
    query_pre, queries, modulate, intra, wq, wm, sems
):
    @pl.when(pl.program_id(0) == 0)
    def _():
        each_block(spots, [(0, 0, w0, w1, wq, sems.at[0]), (0, 1, w0, w1, wm, sems.at[1])])

    count, size = near.shape[0], near.shape[1]
    x = both(near[...], far[...])
    valid = get(mask).astype(F32)
    head = cosine.shape[-1]
    pre = mm(x, wq[...])
    mod = mm(x, wm[...])
    for h in range(pre.shape[-1] // head):
        lanes = slice(h * head, (h + 1) * head)
        qp = pre[:, lanes]
        put(query_pre, lanes, qp)
        put(modulate, lanes, mod[:, lanes] * valid)
        q = turn(qp * jax.nn.sigmoid(qp), cosine[...], sine[...]).astype(BF16)
        put(queries, lanes, q)
        k, v = get(keys, lanes), get(values, lanes)
        scores = (mm(q, k, NT) * grid[h]).astype(BF16)
        put(intra, lanes, mm(scores, v))


def load_states(spots, pieces, held, sems):
    member = spots[3, 0, 0]
    copies = [
        pltpu.make_async_copy(p, held.at[member ^ k], sems.at[k]) for k, p in enumerate(pieces)
    ]
    for c in copies:
        c.start()
    for c in copies:
        c.wait()


def mixed_kernel(
    spots, queries, intra, modulate, query_decay, s0, s1, s2, s3, w0, w1,
    mixed, gated, near_out, far_out, wo, held, sems, state_sems
):
    @pl.when(pl.program_id(0) == 0)
    def _():
        load_states(spots, (s0, s1, s2, s3), held, state_sems)
        each_block(spots, [(1, 0, w0, w1, wo, sems)])

    step = pl.program_id(0)
    _, count, size, width = queries.shape
    heads = held.shape[2]
    head = width // heads
    gates = []
    for h in range(heads):
        lanes = slice(h * head, (h + 1) * head)
        q = (get(queries, lanes).astype(F32) * query_decay[:, lanes]).astype(BF16)
        parts = [mm(slot_rows(q, s, size, count), held[step, s, h]) for s in range(count)]
        mix = get(intra, lanes).astype(F32) + slot_back(parts, size)
        put(mixed, lanes, mix)
        scale = lax.rsqrt(jnp.mean(mix * mix, axis=-1, keepdims=True) + EPS)
        gates.append((mix * scale * get(modulate, lanes).astype(F32)).astype(BF16))
    gate = jnp.concatenate(gates, axis=1)
    put(gated, slice(None), gate)
    out = mm(gate, wo[...], NT)
    near_out[...] = out[: count * size].reshape(near_out.shape)
    far_out[...] = out[count * size :].astype(BF16).reshape(far_out.shape)


def mixed_back_kernel(
    spots, near, far, mixed, modulate, queries, query_pre, keys, values, mask, cosine, sine,
    query_decay, grid, grid_t, s0, s1, s2, s3, w0, w1,
    modulate_grad, query_grad, key_grad, value_grad, state_grad, wo, held, sems, state_sems
):
    @pl.when(pl.program_id(0) == 0)
    def _():
        load_states(spots, (s0, s1, s2, s3), held, state_sems)
        each_block(spots, [(1, 0, w0, w1, wo, sems)])

    step = pl.program_id(0)
    _, count, size, width = queries.shape
    heads = held.shape[2]
    head = width // heads
    gate_grad = mm(both(near[...], far[...]), wo[...])
    valid = get(mask).astype(F32)
    for h in range(heads):
        lanes = slice(h * head, (h + 1) * head)
        mix = get(mixed, lanes).astype(F32)
        scale = lax.rsqrt(jnp.mean(mix * mix, axis=-1, keepdims=True) + EPS)
        gg = gate_grad[:, lanes]
        put(modulate_grad, lanes, gg * valid * (mix * scale))
        cot = gg * get(modulate, lanes).astype(F32)
        inner = jnp.mean(mix * cot, axis=-1, keepdims=True)
        gm = (scale * cot - mix * (scale * scale * scale * inner)).astype(BF16)
        q, k, v = get(queries, lanes), get(keys, lanes), get(values, lanes)
        qs = (q.astype(F32) * query_decay[:, lanes]).astype(BF16)
        gst = (mm(v, gm, NT) * grid_t[h]).astype(BF16)
        gs = (mm(gm, v, NT) * grid[h]).astype(BF16)
        sct = (mm(k, q, NT) * grid_t[h]).astype(BF16)
        put(value_grad, lanes, mm(sct, gm))
        put(key_grad, lanes, mm(gst, q))
        gq = []
        for s in range(count):
            pick = lambda x: slot_rows(x, s, size, count)
            gms = pick(gm)
            gq.append(mm(gms, held[step, s, h], NT))
            state_grad[s, h] = mm(pick(qs), gms, TN).astype(BF16)
        gq = mm(gs, k) + slot_back(gq, size) * query_decay[:, lanes]
        qp = get(query_pre, lanes).astype(F32)
        sg = jax.nn.sigmoid(qp)
        slope = sg + qp * sg * (1.0 - sg)
        put(query_grad, lanes, turn(gq, cosine[...], -sine[...]) * slope)


def rows_kernel(spots, query_grad, modulate_grad, w0, w1, out, wq, wm, sems):
    @pl.when(pl.program_id(0) == 0)
    def _():
        each_block(spots, [(0, 0, w0, w1, wq, sems.at[0]), (0, 1, w0, w1, wm, sems.at[1])])

    put(out, slice(None), mm(get(query_grad), wq[...], NT) + mm(get(modulate_grad), wm[...], NT))


def key_back_kernel(
    spots, key_grad, value_grad, keys, values, key_pre, mask, cosine, sine, key_decay, rows_in,
    g0, g1, g2, g3, kw0, kw1, vw0, vw1,
    key_out, value_out, near_out, far_out, wk, wv, held, sems, state_sems
):
    @pl.when(pl.program_id(0) == 0)
    def _():
        load_states(spots, (g0, g1, g2, g3), held, state_sems)
        each_block(spots, [(0, 0, kw0, kw1, wk, sems.at[0]), (2, 0, vw0, vw1, wv, sems.at[1])])

    step = pl.program_id(0)
    _, count, size, width = keys.shape
    heads = held.shape[2]
    head = width // heads
    valid = get(mask).astype(F32)
    gks, gvs = [], []
    for h in range(heads):
        lanes = slice(h * head, (h + 1) * head)
        decay = key_decay[:, lanes]
        k, v = get(keys, lanes), get(values, lanes)
        scaled = (k.astype(F32) * decay).astype(BF16)
        pk = [mm(slot_rows(v, s, size, count), held[step, s, h], NT) for s in range(count)]
        pv = [mm(slot_rows(scaled, s, size, count), held[step, s, h]) for s in range(count)]
        gk = get(key_grad, lanes).astype(F32) + slot_back(pk, size) * decay
        gv = get(value_grad, lanes).astype(F32) + slot_back(pv, size)
        kp = get(key_pre, lanes).astype(F32)
        sg = jax.nn.sigmoid(kp)
        slope = sg + kp * sg * (1.0 - sg)
        gks.append((turn(gk * valid, cosine[...], -sine[...]) * slope).astype(BF16))
        gvs.append((gv * valid).astype(BF16))
    gk, gv = jnp.concatenate(gks, axis=1), jnp.concatenate(gvs, axis=1)
    put(key_out, slice(None), gk)
    put(value_out, slice(None), gv)
    out = get(rows_in).astype(F32) + mm(gk, wk[...], NT) + mm(gv, wv[...], NT)
    near_out[...] = out[: count * size].reshape(near_out.shape)
    far_out[...] = out[count * size :].astype(BF16).reshape(far_out.shape)


def outer_kernel(order, spots, near, far, *refs):
    count = (len(refs) - 4) // 1
    grads, (keep, send, whole, sems) = refs[:count], refs[count:]
    rows = near.shape[0] * near.shape[1]
    width = near.shape[2]
    tile = 256
    for c in range(0, width, tile):
        a = near[:, :, c : c + tile].reshape(rows, tile)
        b = far[:, :, c : c + tile].reshape(rows, tile)
        for k, g in enumerate(grads):
            g0 = g[0].reshape(rows, -1)
            g1 = g[1].reshape(rows, -1)
            whole[k, c : c + tile, :] = (mm(a, g0, TN) + mm(b, g1, TN)).astype(BF16)
    each_block(
        spots, [(order, k, keep, send, whole.at[k], sems.at[k]) for k in range(count)], out=True
    )


ANY = pl.BlockSpec(memory_space=pltpu.HBM)
VMEM = pl.BlockSpec(memory_space=pltpu.VMEM)


def run(kernel, name, spots, inputs, outputs, scratch, steps, flops):
    def spec(shape, kind):
        if kind == "any":
            return ANY
        if kind == "rows":
            size = shape[0] // steps
            return pl.BlockSpec((size, *shape[1:]), lambda i, _: (i,) + (0,) * (len(shape) - 1))
        if kind == "pair":
            size = shape[1] // steps
            return pl.BlockSpec(
                (2, size, *shape[2:]), lambda i, _: (0, i) + (0,) * (len(shape) - 2)
            )
        return pl.BlockSpec(shape, lambda i, _: (0,) * len(shape))

    moved = sum(a.size * a.dtype.itemsize for a, _ in inputs)
    moved += sum(math.prod(s) * jnp.dtype(d).itemsize for s, d, _ in outputs)
    return pl.pallas_call(
        kernel,
        out_shape=[jax.ShapeDtypeStruct(s, d) for s, d, _ in outputs],
        grid_spec=pltpu.PrefetchScalarGridSpec(
            num_scalar_prefetch=1,
            grid=(steps,),
            in_specs=[spec(a.shape, kind) for a, kind in inputs],
            out_specs=[spec(s, kind) for s, _, kind in outputs],
            scratch_shapes=scratch,
        ),
        compiler_params=pltpu.CompilerParams(vmem_limit_bytes=40 * 2**20),
        cost_estimate=pl.CostEstimate(flops=flops, bytes_accessed=moved, transcendentals=0),
        name=name,
    )(spots, *[a for a, _ in inputs])


class Carry:
    def __init__(self, local, block_decay, reverse):
        self.local, self.reverse = local, reverse
        narrow_count = lax.axis_size("narrow")
        self.member = 2 * (lax.axis_index("wide") % 2) + lax.axis_index("narrow") // 2
        self.masks = [0, 2, narrow_count, narrow_count + 2]
        ranks = [self.member ^ k for k in range(4)]
        self.ranks = [3 - r if reverse else r for r in ranks]
        self.log_decay = jnp.log(block_decay)

    def power(self, e):
        return jnp.exp(e * self.log_decay)[None, :, None, None]

    def spread(self):
        share = self.local.shape[0] // 4
        parts = [
            lax.dynamic_slice_in_dim(self.local, (self.member ^ k) * share, share, 0)
            for k in range(4)
        ]
        self.got = [parts[0]] + [exchange(parts[k], self.masks[k]) for k in range(1, 4)]

    def along(self, between=lambda step, got: got):
        self.held = [h.astype(F32) for h in self.got]
        span = sum(self.power((3 - self.ranks[k]).astype(F32)) * self.held[k] for k in range(4))
        before, step = 0.0, 1
        while step < lax.axis_size("wide") // 2:
            got = between(step, shift_z(span.astype(BF16), step, self.reverse)).astype(F32)
            before = before + self.power(4.0 * (step - 1)) * got
            span = span + self.power(4.0 * step) * got
            step *= 2
        self.before = before

    def back(self):
        sent = []
        for k in range(4):
            state = self.power(self.ranks[k].astype(F32)) * self.before
            for j in range(4):
                gap = (self.ranks[k] - 1 - self.ranks[j]).astype(F32)
                scale = jnp.where(gap >= 0, self.power(jnp.maximum(gap, 0.0)), 0.0)
                state = state + scale * self.held[j]
            sent.append(state.astype(BF16))
        return [sent[0]] + [exchange(sent[k], self.masks[k]) for k in range(1, 4)]


def on_device(
    layer_input,
    query_weight,
    key_weight,
    value_weight,
    modulate_weight,
    output_weight,
    gate_matrix,
    lift_matrix,
    down_matrix,
    decay_factor,
    valid_lengths,
    output_cotangent,
):
    narrow_count, wide_count = lax.axis_size("narrow"), lax.axis_size("wide")
    wide_index, narrow_index = lax.axis_index("wide"), lax.axis_index("narrow")
    core, side = narrow_index % 2, narrow_index // 2
    slots, quarter, width = layer_input.shape
    block = 2 * quarter
    rows, cols = query_weight.shape
    heads = 2 * decay_factor.shape[0]
    head_size = cols // decay_factor.shape[0]
    x_mask = 2
    wide_masks = []
    bit = narrow_count
    while bit < narrow_count * wide_count:
        wide_masks.append(bit)
        bit *= 2
    y_mask, z_masks = wide_masks[0], wide_masks[:0:-1]
    order_yx = z_masks + [y_mask, x_mask]
    order_xy = z_masks + [x_mask, y_mask]
    order_v = [y_mask] + z_masks + [x_mask]
    members = 1 << len(order_yx)
    half = members // 2

    base = wide_index * (quarter * narrow_count) + side * block
    offsets = jnp.stack(
        [core * quarter + jnp.arange(quarter), (1 - core) * quarter + jnp.arange(quarter)]
    ).astype(jnp.int32)
    mask = ((base + offsets)[:, None, :] < valid_lengths[None, :, None]).astype(F32)
    mask_rows = mask[0][:, :, None]
    mask_wide = jnp.broadcast_to(mask[..., None], (2, slots, quarter, head_size)).astype(BF16)
    member = 2 * (wide_index % 2) + side
    spots = jnp.concatenate(
        [
            block_spots(order_xy)[None],
            block_spots(order_yx)[None],
            block_spots(order_v)[None],
            jnp.broadcast_to(member, (1, members, 2)).astype(jnp.int32),
        ]
    )

    def core_sum(near, far):
        return near + exchange(far, 1).astype(F32)

    other_decay = exchange(decay_factor, x_mask)
    decay = jnp.concatenate(
        [jnp.where(side == 0, decay_factor, other_decay), jnp.where(side == 0, other_decay, decay_factor)]
    )
    log_decay = jnp.log(decay)
    block_decay = jnp.exp(block * log_decay)
    steps = 4
    count = slots // steps

    def table(values):
        lanes = values.shape[-1]
        return jnp.broadcast_to(values[:, None], (2, count, quarter, lanes)).reshape(-1, lanes)

    half_head = head_size // 2
    frequency = jnp.exp(-math.log(10000.0) * jnp.arange(half_head, dtype=F32) / half_head)
    phase = (base + offsets).astype(F32)[..., None] * frequency
    cosine, sine = jnp.cos(phase), jnp.sin(phase)
    cosine = table(jnp.concatenate([cosine, cosine], axis=-1))
    sine = table(jnp.concatenate([-sine, sine], axis=-1))
    spot = offsets.astype(F32)
    log_lanes = jnp.repeat(log_decay, head_size)
    query_decay = table(jnp.exp((spot[..., None] + 1.0) * log_lanes))
    key_decay = table(jnp.exp((block - 1.0 - spot[..., None]) * log_lanes))
    flat = jnp.broadcast_to(spot[:, None], (2, count, quarter)).reshape(-1)
    slot_of = jnp.broadcast_to(jnp.arange(count)[None, :, None], (2, count, quarter)).reshape(-1)
    gap = flat[:, None] - flat[None, :]
    seen = (gap >= 0.0) & (slot_of[:, None] == slot_of[None, :])
    decay_grid = jnp.where(
        seen[None], jnp.exp(jnp.maximum(gap, 0.0)[None] * log_decay[:, None, None]), 0.0
    )
    decay_grid_t = jnp.swapaxes(decay_grid, 1, 2)

    def join(*parts):
        return jnp.concatenate(parts, axis=0)

    z_far, z_near = z_masks[:-1], z_masks[-1]
    swap = exchange

    def tie(*arrays):
        return lax.optimization_barrier(arrays)

    def far_open(x):
        for m in z_far[:-1]:
            x = join(x, swap(x, m))
        return x, swap(x, z_far[-1])

    key_w, value_w = key_weight[None, None], value_weight[None, None]
    dn = down_matrix.T[None]
    gl = jnp.stack([gate_matrix.T, lift_matrix.T])[None]
    qmo = jnp.stack([query_weight, modulate_weight, output_weight])[None]
    input_rows = layer_input.astype(F32)
    normed = simple_norm(input_rows).astype(BF16)
    cotangent = output_cotangent.astype(F32)
    cotangent_x = [swap(output_cotangent[: slots // 2], x_mask)]
    key_w, k_got = far_open(key_w)
    k_got, v_got = tie(k_got, swap(value_w, y_mask))
    key_w, value_w = join(key_w, k_got), join(value_w, v_got)
    value_w, v_got = far_open(value_w)
    k_got, v_got, dn_y, cotangent_x[0] = tie(
        swap(key_w, z_near), v_got, swap(dn, y_mask), cotangent_x[0]
    )
    key_w, value_w, dn = join(key_w, k_got), join(value_w, v_got), join(dn, dn_y)
    normed_pair = (normed, swap(normed, 1))
    k_got, v_got = tie(swap(key_w, x_mask), swap(value_w, z_near))
    key_w, value_w, qmo = join(key_w, k_got), join(value_w, v_got), tie(qmo, k_got)[0]
    qmo, q_got = far_open(qmo)
    k_got, v_got, q_got = tie(swap(key_w, y_mask), swap(value_w, x_mask), q_got)
    key_parts, value_parts = (key_w, k_got), (value_w, v_got)
    qmo = join(qmo, q_got)
    qmo_z = swap(qmo, z_near)
    inner_width = heads * head_size
    chip_shape = (2, slots, quarter, inner_width)
    row_shape = (slots, quarter, width)
    state_shape = (slots, heads, head_size, head_size)
    square_flops = 2 * 2 * slots * quarter * width * inner_width
    wide_scratch = pltpu.VMEM((width, inner_width), BF16)
    held_scratch = pltpu.VMEM((4, slots // 4, heads, head_size, head_size), BF16)
    dma = pltpu.SemaphoreType.DMA

    key_pre, keys, values, local_state = run(
        key_value_kernel, "key_value", spots,
        [
            (normed_pair[0], "rows"), (normed_pair[1], "rows"), (mask_wide, "pair"),
            (cosine, "whole"), (sine, "whole"), (key_decay, "whole"),
            (key_parts[0], "any"), (key_parts[1], "any"),
            (value_parts[0], "any"), (value_parts[1], "any"),
        ],
        [
            (chip_shape, BF16, "pair"), (chip_shape, BF16, "pair"), (chip_shape, BF16, "pair"),
            (state_shape, BF16, "rows"),
        ],
        [wide_scratch, wide_scratch, dma((2, members))],
        steps, 2 * square_flops,
    )
    local_state, qmo_z = tie(local_state, qmo_z)
    qmo = join(qmo, qmo_z)
    qm, out_w = qmo[:, :2], qmo[:, 2:]
    scan = Carry(local_state, block_decay, False)
    scan.spread()
    gl, gl_got = far_open(tie(gl, qmo_z)[0])
    scan.got[1], scan.got[2], scan.got[3], qm, out_w = tie(*scan.got[1:], qm, out_w)
    qm_x, o_y = swap(qm, x_mask), swap(out_w, y_mask)
    held = {}

    def forward_step(step, got):
        if step == 1:
            got, qx, oy, held["gl"] = tie(got, qm_x, o_y, gl_got)
            held["qm"], held["out"] = join(qm, qx), join(out_w, oy)
            held["gl"] = join(gl, held["gl"])
            held["more"] = [
                swap(held["qm"], y_mask), swap(held["out"], x_mask), swap(held["gl"], z_near),
                swap(tie(output_cotangent[slots // 2 :], oy)[0], x_mask),
            ]
        if step == 2:
            got, *held["more"] = tie(got, *held["more"])
        return got

    scan.along(forward_step)
    qm_y, o_x, gl_z, more_x = held["more"]
    cotangent_x.append(more_x)
    gl = join(held["gl"], gl_z)
    query_parts, output_parts = (held["qm"], qm_y), (held["out"], o_x)
    dn, dn_got = far_open(tie(dn, gl_z)[0])
    state_parts = scan.back()
    query_pre, queries, modulate, intra = run(
        query_kernel, "query", spots,
        [
            (normed_pair[0], "rows"), (normed_pair[1], "rows"), (mask_wide, "pair"),
            (cosine, "whole"), (sine, "whole"), (decay_grid, "whole"),
            (keys, "pair"), (values, "pair"), (query_parts[0], "any"), (query_parts[1], "any"),
        ],
        [
            (chip_shape, BF16, "pair"), (chip_shape, BF16, "pair"), (chip_shape, BF16, "pair"),
            (chip_shape, BF16, "pair"),
        ],
        [wide_scratch, wide_scratch, dma((2, members))],
        steps, 2 * square_flops,
    )
    *state_parts, queries, dn_got = tie(*state_parts, queries, dn_got)
    dn = join(dn, dn_got)
    state_inputs = [(p, "any") for p in state_parts]
    output_inputs = [(p, "any") for p in output_parts]
    mixed, gated, near_att, far_att = run(
        mixed_kernel, "mixed", spots,
        [
            (queries, "pair"), (intra, "pair"), (modulate, "pair"), (query_decay, "whole"),
            *state_inputs, *output_inputs,
        ],
        [
            (chip_shape, BF16, "pair"), (chip_shape, BF16, "pair"), (row_shape, F32, "rows"),
            (row_shape, BF16, "rows"),
        ],
        [wide_scratch, held_scratch, dma((members,)), dma((4,))],
        steps, square_flops,
    )
    middle = input_rows + core_sum(near_att, far_att)
    two = simple_norm(middle).astype(BF16)
    two_x, gl_y = tie(swap(two, x_mask), swap(gl, y_mask))
    dn_z = swap(dn, z_near)

    def quarters(mine, got_x):
        return jnp.stack([mine, got_x, swap(mine, 1), swap(got_x, 1)])

    def core_part(parts):
        parts = parts.astype(BF16)
        got = swap(parts[2:], 1)
        return fold(parts[0], got[0], F32), fold(parts[1], got[1])

    normed_two = quarters(two, two_x)
    row_starts = (narrow_index ^ jnp.array([0, x_mask, 1, 1 + x_mask], jnp.int32)) * quarter
    row_spots = wide_index * (quarter * narrow_count) + row_starts[:, None] + jnp.arange(quarter)
    row_mask = (row_spots[:, None, :] < valid_lengths[None, :, None]).astype(F32)[..., None]
    branch_rows = quarters(output_cotangent, jnp.concatenate(cotangent_x))
    branch_rows = (row_mask * branch_rows.astype(F32)).astype(BF16)
    gate_t = join(gl[:, 0], gl_y[:, 0]).reshape(-1, width)
    lift_t = join(gl[:, 1], gl_y[:, 1]).reshape(-1, width)
    bulk = half // 2
    down_t = jnp.swapaxes(join(dn, dn_z).reshape(bulk, 2, -1, width), 0, 1).reshape(-1, width)

    def hidden(rows_in, matrix):
        return jnp.einsum("pbld,fd->pblf", rows_in, matrix, preferred_element_type=F32)

    def outer(a, b):
        return jnp.einsum("pblf,pbld->fd", a, b, preferred_element_type=F32).astype(BF16)

    gate_pre = hidden(normed_two, gate_t)
    lift_pre = hidden(normed_two, lift_t)
    inner_grad = hidden(branch_rows, down_t)
    gate_act = apply_swish(gate_pre)
    inner = (gate_act * lift_pre).astype(BF16)
    gate_grad = (inner_grad * lift_pre * swish_slope(gate_pre)).astype(BF16)
    lift_grad = (inner_grad * gate_act).astype(BF16)
    normed_grad = jnp.einsum("pblf,fd->pbld", gate_grad, gate_t, preferred_element_type=F32)
    normed_grad = normed_grad + jnp.einsum(
        "pblf,fd->pbld", lift_grad, lift_t, preferred_element_type=F32
    )
    row_mine, row_send = core_part(normed_grad)
    row_got = swap(row_send, x_mask)
    gate_grad, lift_grad, inner, row_send = tie(gate_grad, lift_grad, inner, row_send)
    gate_g = outer(gate_grad, normed_two).reshape(2, bulk, -1, width)
    gate_y = swap(gate_g[1], y_mask)
    lift_grad, inner, gate_g = tie(lift_grad, inner, gate_g)
    lift_g = outer(lift_grad, normed_two).reshape(2, bulk, -1, width)
    down_g = outer(inner, branch_rows).reshape(2, 2, bulk // 2, -1, width)
    down_z = swap(down_g[:, 1], z_near)
    row_got, gate_y = tie(row_got, gate_y)
    lift_y = swap(tie(lift_g, gate_y)[0][1], y_mask)
    middle_grad = cotangent + norm_backward(middle, row_mine + row_got.astype(F32))

    attended_grad = middle_grad.astype(BF16)
    attended_pair = (attended_grad, exchange(attended_grad, 1))
    modulate_grad, query_grad, key_grad, value_grad, state_grad = run(
        mixed_back_kernel, "mixed_back", spots,
        [
            (attended_pair[0], "rows"), (attended_pair[1], "rows"), (mixed, "pair"),
            (modulate, "pair"), (queries, "pair"), (query_pre, "pair"), (keys, "pair"),
            (values, "pair"), (mask_wide, "pair"), (cosine, "whole"), (sine, "whole"),
            (query_decay, "whole"), (decay_grid, "whole"), (decay_grid_t, "whole"),
            *state_inputs, *output_inputs,
        ],
        [
            (chip_shape, BF16, "pair"), (chip_shape, BF16, "pair"), (chip_shape, BF16, "pair"),
            (chip_shape, BF16, "pair"), (state_shape, BF16, "rows"),
        ],
        [wide_scratch, held_scratch, dma((members,)), dma((4,))],
        steps, 2 * square_flops,
    )
    state_grad, lift_y, down_z, gated = tie(state_grad, lift_y, down_z, gated)
    near = bulk // 2
    down_g = jnp.moveaxis(fold(down_g[:, 0], down_z), 1, 0)
    for m in z_far[:0:-1]:
        size = down_g.shape[0] // 2
        down_g = fold(down_g[:size], swap(down_g[size:], m))
    down_far = swap(down_g[1], z_far[0])
    scan = Carry(state_grad, block_decay, True)
    scan.spread()

    def square(name, order, a, *grads):
        shape = (half, len(grads), rows, cols)
        return run(
            functools.partial(outer_kernel, order), name, spots,
            [(a[0], "whole"), (a[1], "whole"), *[(g, "whole") for g in grads]],
            [(shape, BF16, "any"), (shape, BF16, "any")],
            [pltpu.VMEM((len(grads), width, inner_width), BF16), dma((len(grads), members))],
            1, len(grads) * square_flops,
        )

    output_keep, output_send = square("output_outer", 1, attended_pair, gated)
    query_keep, query_send = square("query_outer", 0, normed_pair, query_grad, modulate_grad)
    (query_rows,) = run(
        rows_kernel, "query_rows", spots,
        [(query_grad, "pair"), (modulate_grad, "pair"), (query_parts[0], "any"), (query_parts[1], "any")],
        [((2, *row_shape), BF16, "pair")],
        [wide_scratch, wide_scratch, dma((2, members))],
        steps, 2 * square_flops,
    )
    *scan.got, down_far, query_keep, query_send, output_keep, output_send, inner = tie(
        *scan.got, down_far, query_keep, query_send, output_keep, output_send, inner
    )
    branch = jnp.einsum("pblf,fd->pbld", inner, down_t, preferred_element_type=F32)
    branch_mine, branch_send = core_part(branch)
    down_g = fold(down_g[0], down_far)
    gl_g = jnp.stack([fold(gate_g[0], gate_y), fold(lift_g[0], lift_y)], axis=1)

    query_y, output_x = swap(query_send[:, :1], y_mask), swap(output_send, x_mask)

    def backward_step(step, got):
        if step == 1:
            got, held["y"], mod_send = tie(got, query_y, query_send[:, 1:])
            held["more"] = swap(mod_send, y_mask)
        if step == 2:
            got, held["more"], held["x"] = tie(got, held["more"], output_x)
        return got

    scan.along(backward_step)
    query_y = jnp.concatenate([held["y"], held["more"]], axis=1)
    scan.before, query_rows, branch_send = tie(scan.before, query_rows, branch_send)
    later_parts = list(tie(*scan.back()))
    gl_g, query_keep, output_keep, branch_send = tie(
        gl_g, query_keep, output_keep, branch_send, *later_parts
    )[:4]
    query_g, output_g = fold(query_keep, query_y), fold(output_keep, held["x"])
    quad = half // 2
    gl_z = swap(gl_g[near:], z_near)
    query_x, output_y = swap(query_g[quad:], x_mask), swap(output_g[quad:], y_mask)
    branch_got = swap(branch_send, x_mask)
    later_inputs = [(p, "any") for p in later_parts]
    quad = half // 2
    def far_pairs(x):
        x = x.reshape(-1, 2, *x.shape[1:])
        for m in reversed(z_far):
            size = x.shape[0] // 2
            x = fold(x[:size], swap(x[size:], m))
        return x[0]

    def far_folds(x):
        for m in reversed(z_far):
            size = x.shape[0] // 2
            x = (fold if size > 1 else final)(x[:size], swap(x[size:], m))
        return x

    key_out, value_out, near_rows, far_rows = run(
        key_back_kernel, "key_back", spots,
        [
            (key_grad, "pair"), (value_grad, "pair"), (keys, "pair"), (values, "pair"),
            (key_pre, "pair"), (mask_wide, "pair"), (cosine, "whole"), (sine, "whole"),
            (key_decay, "whole"), (query_rows, "pair"), *later_inputs,
            (key_parts[0], "any"), (key_parts[1], "any"),
            (value_parts[0], "any"), (value_parts[1], "any"),
        ],
        [
            (chip_shape, BF16, "pair"), (chip_shape, BF16, "pair"), (row_shape, F32, "rows"),
            (row_shape, BF16, "rows"),
        ],
        [wide_scratch, wide_scratch, held_scratch, dma((2, members)), dma((4,))],
        steps, 2 * square_flops,
    )
    key_keep, key_send = square("key_outer", 0, normed_pair, key_out)
    value_keep, value_send = square("value_outer", 2, normed_pair, value_out)
    key_send, value_send, gl_z, query_x, output_y = tie(
        key_send, value_send, gl_z, query_x, output_y
    )
    gl_g = fold(gl_g[:near], gl_z)
    for m in z_far[:0:-1]:
        size = gl_g.shape[0] // 2
        gl_g = fold(gl_g[:size], swap(gl_g[size:], m))
    gl_far = swap(gl_g[1], z_far[0])
    key_y, value_x = swap(key_send, y_mask), swap(value_send, x_mask)
    key_y, value_x, gl_far = tie(key_y, value_x, gl_far)
    down_y = swap(down_g[1], y_mask)
    gate_lift = final(gl_g[0], gl_far)
    key_g, value_g = fold(key_keep, key_y), fold(value_keep, value_x)
    key_x, value_z = swap(key_g[quad:], x_mask), swap(value_g[quad:], z_near)
    qmo_g = jnp.concatenate(
        [fold(query_g[:quad], query_x), fold(output_g[:quad], output_y)], axis=1
    )
    qmo_z = swap(qmo_g[near:], z_near)
    key_x, value_z, down_y, qmo_z, branch_got = tie(key_x, value_z, down_y, qmo_z, branch_got)
    layer_output = (middle + mask_rows * (branch_mine + branch_got.astype(F32))).astype(BF16)
    key_g, value_g = fold(key_g[:quad], key_x), fold(value_g[:quad], value_z)
    key_z, value_far = swap(key_g[near:], z_near), far_pairs(value_g)
    qmo_g = far_folds(fold(qmo_g[:near], qmo_z))[0]
    key_gradient = far_folds(fold(key_g[:near], key_z))[0][0]
    value_y = swap(value_far[1], y_mask)
    value_gradient = final(value_far[0], value_y)[0]
    query_gradient, modulate_gradient, output_gradient = qmo_g
    down_gradient = final(down_g[0], down_y).T
    gate_gradient, lift_gradient = gate_lift[0].T, gate_lift[1].T
    input_gradient = middle_grad + norm_backward(input_rows, core_sum(near_rows, far_rows))
    return (
        layer_output,
        input_gradient,
        query_gradient,
        key_gradient,
        value_gradient,
        modulate_gradient,
        output_gradient,
        gate_gradient,
        lift_gradient,
        down_gradient,
    )


def solution(mesh):
    placed = (
        P(None, ("wide", "narrow"), None),
        P("wide", "narrow"),
        P("wide", "narrow"),
        P("wide", "narrow"),
        P("wide", "narrow"),
        P("wide", "narrow"),
        P(None, ("wide", "narrow")),
        P(None, ("wide", "narrow")),
        P(None, ("wide", "narrow")),
        P("narrow"),
        P(),
        P(None, ("wide", "narrow"), None),
    )
    return jax.shard_map(
        on_device,
        mesh=mesh,
        in_specs=placed,
        out_specs=(
            P(None, ("wide", "narrow"), None),
            P(None, ("wide", "narrow"), None),
            P("wide", "narrow"),
            P("wide", "narrow"),
            P("wide", "narrow"),
            P("wide", "narrow"),
            P("wide", "narrow"),
            P(None, ("wide", "narrow")),
            P(None, ("wide", "narrow")),
            P(None, ("wide", "narrow")),
        ),
        check_vma=False,
    )
```

```python
import functools
import math

import jax
import jax.numpy as jnp
from jax import lax
from jax.experimental import pallas as pl
from jax.experimental.pallas import tpu as pltpu
from jax.sharding import PartitionSpec as P

EPS = 1e-06
AXES = ("wide", "narrow")
BF16 = jnp.bfloat16
F32 = jnp.float32


def simple_norm(values):
    return values * lax.rsqrt(jnp.mean(values * values, axis=-1, keepdims=True) + EPS)


def norm_backward(values, cotangent):
    scale = lax.rsqrt(jnp.mean(values * values, axis=-1, keepdims=True) + EPS)
    inner = jnp.mean(values * cotangent, axis=-1, keepdims=True)
    return scale * cotangent - values * (scale * scale * scale * inner)


def apply_swish(values):
    return values * jax.nn.sigmoid(values)


def swish_slope(values):
    sigmoid_value = jax.nn.sigmoid(values)
    return sigmoid_value + values * sigmoid_value * (1.0 - sigmoid_value)


def exchange(x, mask):
    count = lax.axis_size(AXES)
    return lax.ppermute(x, AXES, [(i, i ^ mask) for i in range(count)])


def after(x, *others):
    return lax.optimization_barrier((x, *others))[0]


def shift_z(x, step, reverse):
    count, unit = lax.axis_size(AXES), 2 * lax.axis_size("narrow")
    pairs = [(i, i + step * unit) for i in range(count - step * unit)]
    if reverse:
        pairs = [(b, a) for a, b in pairs]
    return lax.ppermute(x, AXES, pairs)


def gather_plane(x, masks):
    return gather_more(x[None], masks)


def gather_more(held, masks):
    for mask in masks:
        held = jnp.concatenate([held, exchange(held, mask)], axis=0)
    return held


def gather_hidden(x, masks, swapped):
    held = gather_plane(x, masks)
    if swapped:
        held = jnp.swapaxes(held.reshape(2, 2, -1, *x.shape), 0, 1)
    return held.reshape(-1, x.shape[-1])


def scatter_plane(x, masks):
    for mask in reversed(masks):
        half = x.shape[0] // 2
        got = exchange(x[half:], mask)
        total = x[:half].astype(F32) + got.astype(F32)
        x = total.astype(BF16) if half > 1 else total
    return x[0]


def fold(mine, got, dtype=BF16):
    return (mine.astype(F32) + got.astype(F32)).astype(dtype)


def final(mine, got):
    return fold(mine, got, F32)


def relative(masks, index):
    out = 0
    for k, mask in enumerate(masks):
        out ^= mask * ((index >> k) & 1)
    return out


NT = (((1,), (1,)), ((), ()))
NN = (((1,), (0,)), ((), ()))
TN = (((0,), (0,)), ((), ()))


def mm(a, b, dims=NN):
    return lax.dot_general(a, b, dims, preferred_element_type=F32)


def turn(v, cosine, sine):
    return v * cosine + pltpu.roll(v, v.shape[-1] // 2, 1) * sine


def block_spots(masks):
    own = lax.axis_index(AXES)
    narrow_count = lax.axis_size("narrow")
    ids = jnp.array([relative(masks, i) for i in range(1 << len(masks))], jnp.int32) ^ own
    return jnp.stack([ids // narrow_count, (ids % narrow_count) // 2], axis=1)


def block_copy(spots, which, i, rows, cols, whole, part, sem, out):
    at = (
        pl.ds(pl.multiple_of(spots[which, i, 0] * rows, rows), rows),
        pl.ds(pl.multiple_of(spots[which, i, 1] * cols, cols), cols),
    )
    if out:
        return pltpu.make_async_copy(whole.at[at], part, sem)
    return pltpu.make_async_copy(part, whole.at[at], sem)


def each_block(spots, jobs, out=False):
    def go(method):
        for order, k, near, far, whole, sems in jobs:
            half, _, rows, cols = near.shape

            def step(i, _):
                for at, part in enumerate((near, far)):
                    copy = block_copy(
                        spots, order, i + at * half, rows, cols, whole, part.at[i, k],
                        sems.at[i + at * half], out,
                    )
                    getattr(copy, method)()
                return 0

            lax.fori_loop(0, half, step, 0)

    go("start")
    go("wait")


def both(near, far):
    rows = near.shape[0] * near.shape[1]
    return jnp.concatenate([near.reshape(rows, -1), far.reshape(rows, -1)], axis=0)


def slot_rows(x, s, size, count):
    return jnp.concatenate(
        [x[s * size : (s + 1) * size], x[(count + s) * size : (count + s + 1) * size]], axis=0
    )


def slot_back(parts, size):
    return jnp.concatenate([p[:size] for p in parts] + [p[size:] for p in parts], axis=0)


def put(ref, lanes, value):
    two, count, size, _ = ref.shape
    ref[:, :, :, lanes] = value.reshape(two, count, size, -1).astype(ref.dtype)


def get(ref, lanes=slice(None)):
    two, count, size, width = ref.shape
    x = ref[:, :, :, lanes]
    return x.reshape(two * count * size, x.shape[-1])


def key_value_kernel(
    spots, near, far, mask, cosine, sine, key_decay, kw0, kw1, vw0, vw1,
    key_pre, keys, values, state, wk, wv, sems
):
    @pl.when(pl.program_id(0) == 0)
    def _():
        each_block(spots, [(0, 0, kw0, kw1, wk, sems.at[0]), (2, 0, vw0, vw1, wv, sems.at[1])])

    count, size = near.shape[0], near.shape[1]
    x = both(near[...], far[...])
    valid = get(mask).astype(F32)
    head = cosine.shape[-1]
    pre = mm(x, wk[...])
    val_pre = mm(x, wv[...])
    for h in range(pre.shape[-1] // head):
        lanes = slice(h * head, (h + 1) * head)
        kp = pre[:, lanes]
        put(key_pre, lanes, kp)
        key = (valid * turn(kp * jax.nn.sigmoid(kp), cosine[...], sine[...])).astype(BF16)
        val = (valid * val_pre[:, lanes]).astype(BF16)
        put(keys, lanes, key)
        put(values, lanes, val)
        scaled = (key.astype(F32) * key_decay[:, lanes]).astype(BF16)
        for s in range(count):
            state[s, h] = mm(
                slot_rows(scaled, s, size, count), slot_rows(val, s, size, count), TN
            ).astype(BF16)


def query_kernel(
    spots, near, far, mask, cosine, sine, grid, keys, values, w0, w1,
    query_pre, queries, modulate, intra, wq, wm, sems
):
    @pl.when(pl.program_id(0) == 0)
    def _():
        each_block(spots, [(0, 0, w0, w1, wq, sems.at[0]), (0, 1, w0, w1, wm, sems.at[1])])

    count, size = near.shape[0], near.shape[1]
    x = both(near[...], far[...])
    valid = get(mask).astype(F32)
    head = cosine.shape[-1]
    pre = mm(x, wq[...])
    mod = mm(x, wm[...])
    for h in range(pre.shape[-1] // head):
        lanes = slice(h * head, (h + 1) * head)
        qp = pre[:, lanes]
        put(query_pre, lanes, qp)
        put(modulate, lanes, mod[:, lanes] * valid)
        q = turn(qp * jax.nn.sigmoid(qp), cosine[...], sine[...]).astype(BF16)
        put(queries, lanes, q)
        k, v = get(keys, lanes), get(values, lanes)
        scores = (mm(q, k, NT) * grid[h]).astype(BF16)
        put(intra, lanes, mm(scores, v))


def load_states(spots, pieces, held, sems):
    member = spots[3, 0, 0]
    copies = [
        pltpu.make_async_copy(p, held.at[member ^ k], sems.at[k]) for k, p in enumerate(pieces)
    ]
    for c in copies:
        c.start()
    for c in copies:
        c.wait()


def mixed_kernel(
    spots, queries, intra, modulate, query_decay, s0, s1, s2, s3, w0, w1,
    mixed, gated, near_out, far_out, wo, held, sems, state_sems
):
    @pl.when(pl.program_id(0) == 0)
    def _():
        load_states(spots, (s0, s1, s2, s3), held, state_sems)
        each_block(spots, [(1, 0, w0, w1, wo, sems)])

    step = pl.program_id(0)
    _, count, size, width = queries.shape
    heads = held.shape[2]
    head = width // heads
    gates = []
    for h in range(heads):
        lanes = slice(h * head, (h + 1) * head)
        q = (get(queries, lanes).astype(F32) * query_decay[:, lanes]).astype(BF16)
        parts = [mm(slot_rows(q, s, size, count), held[step, s, h]) for s in range(count)]
        mix = get(intra, lanes).astype(F32) + slot_back(parts, size)
        put(mixed, lanes, mix)
        scale = lax.rsqrt(jnp.mean(mix * mix, axis=-1, keepdims=True) + EPS)
        gates.append((mix * scale * get(modulate, lanes).astype(F32)).astype(BF16))
    gate = jnp.concatenate(gates, axis=1)
    put(gated, slice(None), gate)
    out = mm(gate, wo[...], NT)
    near_out[...] = out[: count * size].reshape(near_out.shape)
    far_out[...] = out[count * size :].astype(BF16).reshape(far_out.shape)


def mixed_back_kernel(
    spots, near, far, mixed, modulate, queries, query_pre, keys, values, mask, cosine, sine,
    query_decay, grid, grid_t, s0, s1, s2, s3, w0, w1,
    modulate_grad, query_grad, key_grad, value_grad, state_grad, wo, held, sems, state_sems
):
    @pl.when(pl.program_id(0) == 0)
    def _():
        load_states(spots, (s0, s1, s2, s3), held, state_sems)
        each_block(spots, [(1, 0, w0, w1, wo, sems)])

    step = pl.program_id(0)
    _, count, size, width = queries.shape
    heads = held.shape[2]
    head = width // heads
    gate_grad = mm(both(near[...], far[...]), wo[...])
    valid = get(mask).astype(F32)
    for h in range(heads):
        lanes = slice(h * head, (h + 1) * head)
        mix = get(mixed, lanes).astype(F32)
        scale = lax.rsqrt(jnp.mean(mix * mix, axis=-1, keepdims=True) + EPS)
        gg = gate_grad[:, lanes]
        put(modulate_grad, lanes, gg * valid * (mix * scale))
        cot = gg * get(modulate, lanes).astype(F32)
        inner = jnp.mean(mix * cot, axis=-1, keepdims=True)
        gm = (scale * cot - mix * (scale * scale * scale * inner)).astype(BF16)
        q, k, v = get(queries, lanes), get(keys, lanes), get(values, lanes)
        qs = (q.astype(F32) * query_decay[:, lanes]).astype(BF16)
        gst = (mm(v, gm, NT) * grid_t[h]).astype(BF16)
        gs = (mm(gm, v, NT) * grid[h]).astype(BF16)
        sct = (mm(k, q, NT) * grid_t[h]).astype(BF16)
        put(value_grad, lanes, mm(sct, gm))
        put(key_grad, lanes, mm(gst, q))
        gq = []
        for s in range(count):
            pick = lambda x: slot_rows(x, s, size, count)
            gms = pick(gm)
            gq.append(mm(gms, held[step, s, h], NT))
            state_grad[s, h] = mm(pick(qs), gms, TN).astype(BF16)
        gq = mm(gs, k) + slot_back(gq, size) * query_decay[:, lanes]
        qp = get(query_pre, lanes).astype(F32)
        sg = jax.nn.sigmoid(qp)
        slope = sg + qp * sg * (1.0 - sg)
        put(query_grad, lanes, turn(gq, cosine[...], -sine[...]) * slope)


def rows_kernel(spots, query_grad, modulate_grad, w0, w1, out, wq, wm, sems):
    @pl.when(pl.program_id(0) == 0)
    def _():
        each_block(spots, [(0, 0, w0, w1, wq, sems.at[0]), (0, 1, w0, w1, wm, sems.at[1])])

    put(out, slice(None), mm(get(query_grad), wq[...], NT) + mm(get(modulate_grad), wm[...], NT))


def key_back_kernel(
    spots, key_grad, value_grad, keys, values, key_pre, mask, cosine, sine, key_decay, rows_in,
    g0, g1, g2, g3, kw0, kw1, vw0, vw1,
    key_out, value_out, near_out, far_out, wk, wv, held, sems, state_sems
):
    @pl.when(pl.program_id(0) == 0)
    def _():
        load_states(spots, (g0, g1, g2, g3), held, state_sems)
        each_block(spots, [(0, 0, kw0, kw1, wk, sems.at[0]), (2, 0, vw0, vw1, wv, sems.at[1])])

    step = pl.program_id(0)
    _, count, size, width = keys.shape
    heads = held.shape[2]
    head = width // heads
    valid = get(mask).astype(F32)
    gks, gvs = [], []
    for h in range(heads):
        lanes = slice(h * head, (h + 1) * head)
        decay = key_decay[:, lanes]
        k, v = get(keys, lanes), get(values, lanes)
        scaled = (k.astype(F32) * decay).astype(BF16)
        pk = [mm(slot_rows(v, s, size, count), held[step, s, h], NT) for s in range(count)]
        pv = [mm(slot_rows(scaled, s, size, count), held[step, s, h]) for s in range(count)]
        gk = get(key_grad, lanes).astype(F32) + slot_back(pk, size) * decay
        gv = get(value_grad, lanes).astype(F32) + slot_back(pv, size)
        kp = get(key_pre, lanes).astype(F32)
        sg = jax.nn.sigmoid(kp)
        slope = sg + kp * sg * (1.0 - sg)
        gks.append((turn(gk * valid, cosine[...], -sine[...]) * slope).astype(BF16))
        gvs.append((gv * valid).astype(BF16))
    gk, gv = jnp.concatenate(gks, axis=1), jnp.concatenate(gvs, axis=1)
    put(key_out, slice(None), gk)
    put(value_out, slice(None), gv)
    out = get(rows_in).astype(F32) + mm(gk, wk[...], NT) + mm(gv, wv[...], NT)
    near_out[...] = out[: count * size].reshape(near_out.shape)
    far_out[...] = out[count * size :].astype(BF16).reshape(far_out.shape)


def hidden_kernel(
    spots, n0, n1, n2, n3, branch_rows, gate_w, lift_w, down_w,
    inner_out, gate_out, lift_out, keep, send, branch_keep, branch_send
):
    x, b = [], get(branch_rows)
    for n in (n0, n1, n2, n3):
        x.append(n[...].reshape(-1, n.shape[-1]))
    x = jnp.concatenate(x, axis=0)
    gate, lift, down = gate_w[...], lift_w[...], down_w[...]
    parts = []
    for r in range(0, x.shape[0], 256):
        rows = slice(r, r + 256)
        gate_pre = mm(x[rows], gate, NT)
        lift_pre = mm(x[rows], lift, NT)
        inner_grad = mm(b[rows], down, NT)
        q = jax.nn.sigmoid(gate_pre)
        act = gate_pre * q
        gate_grad = (inner_grad * lift_pre * (q + act * (1.0 - q))).astype(BF16)
        lift_grad = (inner_grad * act).astype(BF16)
        inner = (act * lift_pre).astype(BF16)
        total = (mm(gate_grad, gate) + mm(lift_grad, lift)).astype(BF16)
        parts.append((inner, gate_grad, lift_grad, total, mm(inner, down).astype(BF16)))
    inner, gate_grad, lift_grad, total, branch = (jnp.concatenate(p, axis=0) for p in zip(*parts))
    put(inner_out, slice(None), inner)
    put(gate_out, slice(None), gate_grad)
    put(lift_out, slice(None), lift_grad)
    half = total.shape[0] // 2
    for near, far, value in ((keep, send, total), (branch_keep, branch_send, branch)):
        near[...] = value[:half].reshape(near.shape)
        far[...] = value[half:].reshape(far.shape)


def outer_kernel(order, spots, near, far, *refs):
    count = (len(refs) - 4) // 1
    grads, (keep, send, whole, sems) = refs[:count], refs[count:]
    rows = near.shape[0] * near.shape[1]
    width = near.shape[2]
    tile = 256
    for c in range(0, width, tile):
        a = near[:, :, c : c + tile].reshape(rows, tile)
        b = far[:, :, c : c + tile].reshape(rows, tile)
        for k, g in enumerate(grads):
            g0 = g[0].reshape(rows, -1)
            g1 = g[1].reshape(rows, -1)
            whole[k, c : c + tile, :] = (mm(a, g0, TN) + mm(b, g1, TN)).astype(BF16)
    each_block(
        spots, [(order, k, keep, send, whole.at[k], sems.at[k]) for k in range(count)], out=True
    )


ANY = pl.BlockSpec(memory_space=pltpu.HBM)
VMEM = pl.BlockSpec(memory_space=pltpu.VMEM)


def run(kernel, name, spots, inputs, outputs, scratch, steps, flops):
    def spec(shape, kind):
        if kind == "any":
            return ANY
        if kind == "rows":
            size = shape[0] // steps
            return pl.BlockSpec((size, *shape[1:]), lambda i, _: (i,) + (0,) * (len(shape) - 1))
        if kind == "pair":
            size = shape[1] // steps
            return pl.BlockSpec(
                (shape[0], size, *shape[2:]), lambda i, _: (0, i) + (0,) * (len(shape) - 2)
            )
        return pl.BlockSpec(shape, lambda i, _: (0,) * len(shape))

    moved = sum(a.size * a.dtype.itemsize for a, _ in inputs)
    moved += sum(math.prod(s) * jnp.dtype(d).itemsize for s, d, _ in outputs)
    return pl.pallas_call(
        kernel,
        out_shape=[jax.ShapeDtypeStruct(s, d) for s, d, _ in outputs],
        grid_spec=pltpu.PrefetchScalarGridSpec(
            num_scalar_prefetch=1,
            grid=(steps,),
            in_specs=[spec(a.shape, kind) for a, kind in inputs],
            out_specs=[spec(s, kind) for s, _, kind in outputs],
            scratch_shapes=scratch,
        ),
        compiler_params=pltpu.CompilerParams(vmem_limit_bytes=44 * 2**20),
        cost_estimate=pl.CostEstimate(flops=flops, bytes_accessed=moved, transcendentals=0),
        name=name,
    )(spots, *[a for a, _ in inputs])


class Carry:
    def __init__(self, local, block_decay, reverse):
        self.local, self.reverse = local, reverse
        narrow_count = lax.axis_size("narrow")
        self.member = 2 * (lax.axis_index("wide") % 2) + lax.axis_index("narrow") // 2
        self.masks = [0, 2, narrow_count, narrow_count + 2]
        ranks = [self.member ^ k for k in range(4)]
        self.ranks = [3 - r if reverse else r for r in ranks]
        self.log_decay = jnp.log(block_decay)

    def power(self, e):
        return jnp.exp(e * self.log_decay)[None, :, None, None]

    def spread(self):
        share = self.local.shape[0] // 4
        parts = [
            lax.dynamic_slice_in_dim(self.local, (self.member ^ k) * share, share, 0)
            for k in range(4)
        ]
        self.got = [parts[0]] + [exchange(parts[k], self.masks[k]) for k in range(1, 4)]

    def along(self, between=lambda step, got: got):
        self.held = [h.astype(F32) for h in self.got]
        span = sum(self.power((3 - self.ranks[k]).astype(F32)) * self.held[k] for k in range(4))
        before, step = 0.0, 1
        while step < lax.axis_size("wide") // 2:
            got = between(step, shift_z(span.astype(BF16), step, self.reverse)).astype(F32)
            before = before + self.power(4.0 * (step - 1)) * got
            span = span + self.power(4.0 * step) * got
            step *= 2
        self.before = before

    def back(self):
        sent = []
        for k in range(4):
            state = self.power(self.ranks[k].astype(F32)) * self.before
            for j in range(4):
                gap = (self.ranks[k] - 1 - self.ranks[j]).astype(F32)
                scale = jnp.where(gap >= 0, self.power(jnp.maximum(gap, 0.0)), 0.0)
                state = state + scale * self.held[j]
            sent.append(state.astype(BF16))
        return [sent[0]] + [exchange(sent[k], self.masks[k]) for k in range(1, 4)]


def on_device(
    layer_input,
    query_weight,
    key_weight,
    value_weight,
    modulate_weight,
    output_weight,
    gate_matrix,
    lift_matrix,
    down_matrix,
    decay_factor,
    valid_lengths,
    output_cotangent,
):
    narrow_count, wide_count = lax.axis_size("narrow"), lax.axis_size("wide")
    wide_index, narrow_index = lax.axis_index("wide"), lax.axis_index("narrow")
    core, side = narrow_index % 2, narrow_index // 2
    slots, quarter, width = layer_input.shape
    block = 2 * quarter
    rows, cols = query_weight.shape
    heads = 2 * decay_factor.shape[0]
    head_size = cols // decay_factor.shape[0]
    x_mask = 2
    wide_masks = []
    bit = narrow_count
    while bit < narrow_count * wide_count:
        wide_masks.append(bit)
        bit *= 2
    y_mask, z_masks = wide_masks[0], wide_masks[:0:-1]
    order_yx = z_masks + [y_mask, x_mask]
    order_xy = z_masks + [x_mask, y_mask]
    order_v = [y_mask] + z_masks + [x_mask]
    members = 1 << len(order_yx)
    half = members // 2

    base = wide_index * (quarter * narrow_count) + side * block
    offsets = jnp.stack(
        [core * quarter + jnp.arange(quarter), (1 - core) * quarter + jnp.arange(quarter)]
    ).astype(jnp.int32)
    mask = ((base + offsets)[:, None, :] < valid_lengths[None, :, None]).astype(F32)
    mask_rows = mask[0][:, :, None]
    mask_wide = jnp.broadcast_to(mask[..., None], (2, slots, quarter, head_size)).astype(BF16)
    member = 2 * (wide_index % 2) + side
    spots = jnp.concatenate(
        [
            block_spots(order_xy)[None],
            block_spots(order_yx)[None],
            block_spots(order_v)[None],
            jnp.broadcast_to(member, (1, members, 2)).astype(jnp.int32),
        ]
    )

    def core_sum(near, far):
        return near + exchange(far, 1).astype(F32)

    other_decay = exchange(decay_factor, x_mask)
    decay = jnp.concatenate(
        [jnp.where(side == 0, decay_factor, other_decay), jnp.where(side == 0, other_decay, decay_factor)]
    )
    log_decay = jnp.log(decay)
    block_decay = jnp.exp(block * log_decay)
    steps = 4
    count = slots // steps

    def table(values):
        lanes = values.shape[-1]
        return jnp.broadcast_to(values[:, None], (2, count, quarter, lanes)).reshape(-1, lanes)

    half_head = head_size // 2
    frequency = jnp.exp(-math.log(10000.0) * jnp.arange(half_head, dtype=F32) / half_head)
    phase = (base + offsets).astype(F32)[..., None] * frequency
    cosine, sine = jnp.cos(phase), jnp.sin(phase)
    cosine = table(jnp.concatenate([cosine, cosine], axis=-1))
    sine = table(jnp.concatenate([-sine, sine], axis=-1))
    spot = offsets.astype(F32)
    log_lanes = jnp.repeat(log_decay, head_size)
    query_decay = table(jnp.exp((spot[..., None] + 1.0) * log_lanes))
    key_decay = table(jnp.exp((block - 1.0 - spot[..., None]) * log_lanes))
    flat = jnp.broadcast_to(spot[:, None], (2, count, quarter)).reshape(-1)
    slot_of = jnp.broadcast_to(jnp.arange(count)[None, :, None], (2, count, quarter)).reshape(-1)
    gap = flat[:, None] - flat[None, :]
    seen = (gap >= 0.0) & (slot_of[:, None] == slot_of[None, :])
    decay_grid = jnp.where(
        seen[None], jnp.exp(jnp.maximum(gap, 0.0)[None] * log_decay[:, None, None]), 0.0
    )
    decay_grid_t = jnp.swapaxes(decay_grid, 1, 2)

    def join(*parts):
        return jnp.concatenate(parts, axis=0)

    z_far, z_near = z_masks[:-1], z_masks[-1]
    swap = exchange

    def tie(*arrays):
        return lax.optimization_barrier(arrays)

    def far_open(x):
        for m in z_far[:-1]:
            x = join(x, swap(x, m))
        return x, swap(x, z_far[-1])

    key_w, value_w = key_weight[None, None], value_weight[None, None]
    dn = down_matrix.T[None]
    gl = jnp.stack([gate_matrix.T, lift_matrix.T])[None]
    qmo = jnp.stack([query_weight, modulate_weight, output_weight])[None]
    input_rows = layer_input.astype(F32)
    normed = simple_norm(input_rows).astype(BF16)
    cotangent = output_cotangent.astype(F32)
    cotangent_x = [swap(output_cotangent[: slots // 2], x_mask)]
    key_w, k_got = far_open(key_w)
    k_got, v_got = tie(k_got, swap(value_w, y_mask))
    key_w, value_w = join(key_w, k_got), join(value_w, v_got)
    value_w, v_got = far_open(value_w)
    k_got, v_got, dn_y, cotangent_x[0] = tie(
        swap(key_w, z_near), v_got, swap(dn, y_mask), cotangent_x[0]
    )
    key_w, value_w, dn = join(key_w, k_got), join(value_w, v_got), join(dn, dn_y)
    normed_pair = (normed, swap(normed, 1))
    k_got, v_got = tie(swap(key_w, x_mask), swap(value_w, z_near))
    key_w, value_w, qmo = join(key_w, k_got), join(value_w, v_got), tie(qmo, k_got)[0]
    qmo, q_got = far_open(qmo)
    k_got, v_got, q_got = tie(swap(key_w, y_mask), swap(value_w, x_mask), q_got)
    key_parts, value_parts = (key_w, k_got), (value_w, v_got)
    qmo = join(qmo, q_got)
    qmo_z = swap(qmo, z_near)
    inner_width = heads * head_size
    chip_shape = (2, slots, quarter, inner_width)
    row_shape = (slots, quarter, width)
    state_shape = (slots, heads, head_size, head_size)
    square_flops = 2 * 2 * slots * quarter * width * inner_width
    wide_scratch = pltpu.VMEM((width, inner_width), BF16)
    held_scratch = pltpu.VMEM((4, slots // 4, heads, head_size, head_size), BF16)
    dma = pltpu.SemaphoreType.DMA

    key_pre, keys, values, local_state = run(
        key_value_kernel, "key_value", spots,
        [
            (normed_pair[0], "rows"), (normed_pair[1], "rows"), (mask_wide, "pair"),
            (cosine, "whole"), (sine, "whole"), (key_decay, "whole"),
            (key_parts[0], "any"), (key_parts[1], "any"),
            (value_parts[0], "any"), (value_parts[1], "any"),
        ],
        [
            (chip_shape, BF16, "pair"), (chip_shape, BF16, "pair"), (chip_shape, BF16, "pair"),
            (state_shape, BF16, "rows"),
        ],
        [wide_scratch, wide_scratch, dma((2, members))],
        steps, 2 * square_flops,
    )
    local_state, qmo_z = tie(local_state, qmo_z)
    qmo = join(qmo, qmo_z)
    qm, out_w = qmo[:, :2], qmo[:, 2:]
    scan = Carry(local_state, block_decay, False)
    scan.spread()
    gl, gl_got = far_open(tie(gl, qmo_z)[0])
    scan.got[1], scan.got[2], scan.got[3], qm, out_w = tie(*scan.got[1:], qm, out_w)
    qm_x, o_y = swap(qm, x_mask), swap(out_w, y_mask)
    held = {}

    def forward_step(step, got):
        if step == 1:
            got, qx, oy, held["gl"] = tie(got, qm_x, o_y, gl_got)
            held["qm"], held["out"] = join(qm, qx), join(out_w, oy)
            held["gl"] = join(gl, held["gl"])
            held["more"] = [
                swap(held["qm"], y_mask), swap(held["out"], x_mask), swap(held["gl"], z_near),
                swap(tie(output_cotangent[slots // 2 :], oy)[0], x_mask),
            ]
        if step == 2:
            got, *held["more"] = tie(got, *held["more"])
        return got

    scan.along(forward_step)
    qm_y, o_x, gl_z, more_x = held["more"]
    cotangent_x.append(more_x)
    gl = join(held["gl"], gl_z)
    query_parts, output_parts = (held["qm"], qm_y), (held["out"], o_x)
    dn, dn_got = far_open(tie(dn, gl_z)[0])
    state_parts = scan.back()
    query_pre, queries, modulate, intra = run(
        query_kernel, "query", spots,
        [
            (normed_pair[0], "rows"), (normed_pair[1], "rows"), (mask_wide, "pair"),
            (cosine, "whole"), (sine, "whole"), (decay_grid, "whole"),
            (keys, "pair"), (values, "pair"), (query_parts[0], "any"), (query_parts[1], "any"),
        ],
        [
            (chip_shape, BF16, "pair"), (chip_shape, BF16, "pair"), (chip_shape, BF16, "pair"),
            (chip_shape, BF16, "pair"),
        ],
        [wide_scratch, wide_scratch, dma((2, members))],
        steps, 2 * square_flops,
    )
    *state_parts, queries, dn_got = tie(*state_parts, queries, dn_got)
    dn = join(dn, dn_got)
    state_inputs = [(p, "any") for p in state_parts]
    output_inputs = [(p, "any") for p in output_parts]
    mixed, gated, near_att, far_att = run(
        mixed_kernel, "mixed", spots,
        [
            (queries, "pair"), (intra, "pair"), (modulate, "pair"), (query_decay, "whole"),
            *state_inputs, *output_inputs,
        ],
        [
            (chip_shape, BF16, "pair"), (chip_shape, BF16, "pair"), (row_shape, F32, "rows"),
            (row_shape, BF16, "rows"),
        ],
        [wide_scratch, held_scratch, dma((members,)), dma((4,))],
        steps, square_flops,
    )
    middle = input_rows + core_sum(near_att, far_att)
    two = simple_norm(middle).astype(BF16)
    two_x, gl_y = tie(swap(two, x_mask), swap(gl, y_mask))
    dn_z = swap(dn, z_near)

    def quarters(mine, got_x):
        return [mine, got_x, swap(mine, 1), swap(got_x, 1)]

    def core_part(keep, send):
        got = swap(send, 1)
        return fold(keep[0], got[0], F32), fold(keep[1], got[1])

    two_pieces = quarters(two, two_x)
    normed_two = jnp.stack(two_pieces)
    row_starts = (narrow_index ^ jnp.array([0, x_mask, 1, 1 + x_mask], jnp.int32)) * quarter
    row_spots = wide_index * (quarter * narrow_count) + row_starts[:, None] + jnp.arange(quarter)
    row_mask = (row_spots[:, None, :] < valid_lengths[None, :, None]).astype(F32)[..., None]
    branch_rows = jnp.stack(quarters(output_cotangent, jnp.concatenate(cotangent_x)))
    branch_rows = (row_mask * branch_rows.astype(F32)).astype(BF16)
    gate_t = join(gl[:, 0], gl_y[:, 0]).reshape(-1, width)
    lift_t = join(gl[:, 1], gl_y[:, 1]).reshape(-1, width)
    bulk = half // 2
    down_t = jnp.swapaxes(join(dn, dn_z).reshape(bulk, 2, -1, width), 0, 1).reshape(-1, width)

    def outer(a, b):
        return jnp.einsum("pblf,pbld->fd", a, b, preferred_element_type=F32).astype(BF16)

    hidden_shape = (4, slots, quarter, gate_t.shape[0])
    sum_shape = (2, slots, quarter, width)
    hidden_flops = 2 * 4 * slots * quarter * width * gate_t.shape[0]
    inner, gate_grad, lift_grad, row_keep, row_send, branch_keep, branch_send = run(
        hidden_kernel, "hidden", spots,
        [
            *[(p, "rows") for p in two_pieces], (branch_rows, "pair"), (gate_t, "whole"),
            (lift_t, "whole"), (down_t, "whole"),
        ],
        [(hidden_shape, BF16, "pair")] * 3 + [(sum_shape, BF16, "pair")] * 4,
        [], steps, 6 * hidden_flops,
    )
    row_mine, row_send = core_part(row_keep, row_send)
    row_got = swap(row_send, x_mask)
    gate_grad, lift_grad, inner, row_send = tie(gate_grad, lift_grad, inner, row_send)
    gate_g = outer(gate_grad, normed_two).reshape(2, bulk, -1, width)
    gate_y = swap(gate_g[1], y_mask)
    lift_grad, inner, gate_g = tie(lift_grad, inner, gate_g)
    lift_g = outer(lift_grad, normed_two).reshape(2, bulk, -1, width)
    down_g = outer(inner, branch_rows).reshape(2, 2, bulk // 2, -1, width)
    branch_mine, branch_send = core_part(branch_keep, branch_send)
    row_got, gate_y, lift_g, down_z_send, branch_send = tie(
        row_got, gate_y, lift_g, down_g[:, 1], branch_send
    )
    lift_y = swap(lift_g[1], y_mask)
    branch_got = swap(branch_send, x_mask)
    down_z = swap(down_z_send, z_near)
    middle_grad = cotangent + norm_backward(middle, row_mine + row_got.astype(F32))

    attended_grad = middle_grad.astype(BF16)
    attended_pair = (attended_grad, exchange(attended_grad, 1))
    modulate_grad, query_grad, key_grad, value_grad, state_grad = run(
        mixed_back_kernel, "mixed_back", spots,
        [
            (attended_pair[0], "rows"), (attended_pair[1], "rows"), (mixed, "pair"),
            (modulate, "pair"), (queries, "pair"), (query_pre, "pair"), (keys, "pair"),
            (values, "pair"), (mask_wide, "pair"), (cosine, "whole"), (sine, "whole"),
            (query_decay, "whole"), (decay_grid, "whole"), (decay_grid_t, "whole"),
            *state_inputs, *output_inputs,
        ],
        [
            (chip_shape, BF16, "pair"), (chip_shape, BF16, "pair"), (chip_shape, BF16, "pair"),
            (chip_shape, BF16, "pair"), (state_shape, BF16, "rows"),
        ],
        [wide_scratch, held_scratch, dma((members,)), dma((4,))],
        steps, 2 * square_flops,
    )
    state_grad, lift_y, branch_got, gated = tie(state_grad, lift_y, branch_got, gated)
    near = bulk // 2
    scan = Carry(state_grad, block_decay, True)
    scan.spread()

    def square(name, order, a, *grads):
        shape = (half, len(grads), rows, cols)
        return run(
            functools.partial(outer_kernel, order), name, spots,
            [(a[0], "whole"), (a[1], "whole"), *[(g, "whole") for g in grads]],
            [(shape, BF16, "any"), (shape, BF16, "any")],
            [pltpu.VMEM((len(grads), width, inner_width), BF16), dma((len(grads), members))],
            1, len(grads) * square_flops,
        )

    output_keep, output_send = square("output_outer", 1, attended_pair, gated)
    query_keep, query_send = square("query_outer", 0, normed_pair, query_grad, modulate_grad)
    (query_rows,) = run(
        rows_kernel, "query_rows", spots,
        [(query_grad, "pair"), (modulate_grad, "pair"), (query_parts[0], "any"), (query_parts[1], "any")],
        [((2, *row_shape), BF16, "pair")],
        [wide_scratch, wide_scratch, dma((2, members))],
        steps, 2 * square_flops,
    )
    *scan.got, down_z, query_keep, query_send, output_keep, output_send = tie(
        *scan.got, down_z, query_keep, query_send, output_keep, output_send
    )
    layer_output = (middle + mask_rows * (branch_mine + branch_got.astype(F32))).astype(BF16)
    down_g = jnp.moveaxis(fold(down_g[:, 0], down_z), 1, 0)
    for m in z_far[:0:-1]:
        size = down_g.shape[0] // 2
        down_g = fold(down_g[:size], swap(down_g[size:], m))
    gl_g = jnp.stack([fold(gate_g[0], gate_y), fold(lift_g[0], lift_y)], axis=1)

    query_y, output_x = swap(query_send[:, :1], y_mask), swap(output_send, x_mask)

    def backward_step(step, got):
        if step == 1:
            got, held["y"], mod_send = tie(got, query_y, query_send[:, 1:])
            held["more"] = swap(mod_send, y_mask)
        if step == 2:
            got, held["more"], held["x"] = tie(got, held["more"], output_x)
        return got

    scan.along(backward_step)
    query_y = jnp.concatenate([held["y"], held["more"]], axis=1)
    scan.before, query_rows, down_g, gl_g = tie(scan.before, query_rows, down_g, gl_g)
    down_far = swap(down_g[1], z_far[0])
    gl_z = swap(gl_g[near:], z_near)
    later_parts = list(tie(*scan.back()))
    query_keep, output_keep = tie(query_keep, output_keep, *later_parts)[:2]
    query_g, output_g = fold(query_keep, query_y), fold(output_keep, held["x"])
    quad = half // 2
    query_x, output_y = swap(query_g[quad:], x_mask), swap(output_g[quad:], y_mask)
    later_inputs = [(p, "any") for p in later_parts]
    quad = half // 2
    def far_pairs(x):
        x = x.reshape(-1, 2, *x.shape[1:])
        for m in reversed(z_far):
            size = x.shape[0] // 2
            x = fold(x[:size], swap(x[size:], m))
        return x[0]

    def far_folds(x):
        for m in reversed(z_far):
            size = x.shape[0] // 2
            x = (fold if size > 1 else final)(x[:size], swap(x[size:], m))
        return x

    key_out, value_out, near_rows, far_rows = run(
        key_back_kernel, "key_back", spots,
        [
            (key_grad, "pair"), (value_grad, "pair"), (keys, "pair"), (values, "pair"),
            (key_pre, "pair"), (mask_wide, "pair"), (cosine, "whole"), (sine, "whole"),
            (key_decay, "whole"), (query_rows, "pair"), *later_inputs,
            (key_parts[0], "any"), (key_parts[1], "any"),
            (value_parts[0], "any"), (value_parts[1], "any"),
        ],
        [
            (chip_shape, BF16, "pair"), (chip_shape, BF16, "pair"), (row_shape, F32, "rows"),
            (row_shape, BF16, "rows"),
        ],
        [wide_scratch, wide_scratch, held_scratch, dma((2, members)), dma((4,))],
        steps, 2 * square_flops,
    )
    key_keep, key_send = square("key_outer", 0, normed_pair, key_out)
    value_keep, value_send = square("value_outer", 2, normed_pair, value_out)
    key_send, value_send, gl_z, down_far, query_x, output_y = tie(
        key_send, value_send, gl_z, down_far, query_x, output_y
    )
    down_g = fold(down_g[0], down_far)
    gl_g = fold(gl_g[:near], gl_z)
    for m in z_far[:0:-1]:
        size = gl_g.shape[0] // 2
        gl_g = fold(gl_g[:size], swap(gl_g[size:], m))
    gl_far = swap(gl_g[1], z_far[0])
    key_y, value_x = swap(key_send, y_mask), swap(value_send, x_mask)
    key_y, value_x, gl_far = tie(key_y, value_x, gl_far)
    down_y = swap(down_g[1], y_mask)
    gate_lift = final(gl_g[0], gl_far)
    key_g, value_g = fold(key_keep, key_y), fold(value_keep, value_x)
    key_x, value_z = swap(key_g[quad:], x_mask), swap(value_g[quad:], z_near)
    qmo_g = jnp.concatenate(
        [fold(query_g[:quad], query_x), fold(output_g[:quad], output_y)], axis=1
    )
    qmo_z = swap(qmo_g[near:], z_near)
    key_x, value_z, down_y, qmo_z = tie(key_x, value_z, down_y, qmo_z)
    key_g, value_g = fold(key_g[:quad], key_x), fold(value_g[:quad], value_z)
    key_z, value_far = swap(key_g[near:], z_near), far_pairs(value_g)
    qmo_g = far_folds(fold(qmo_g[:near], qmo_z))[0]
    key_gradient = far_folds(fold(key_g[:near], key_z))[0][0]
    value_y = swap(value_far[1], y_mask)
    value_gradient = final(value_far[0], value_y)[0]
    query_gradient, modulate_gradient, output_gradient = qmo_g
    down_gradient = final(down_g[0], down_y).T
    gate_gradient, lift_gradient = gate_lift[0].T, gate_lift[1].T
    input_gradient = middle_grad + norm_backward(input_rows, core_sum(near_rows, far_rows))
    return (
        layer_output,
        input_gradient,
        query_gradient,
        key_gradient,
        value_gradient,
        modulate_gradient,
        output_gradient,
        gate_gradient,
        lift_gradient,
        down_gradient,
    )


def solution(mesh):
    placed = (
        P(None, ("wide", "narrow"), None),
        P("wide", "narrow"),
        P("wide", "narrow"),
        P("wide", "narrow"),
        P("wide", "narrow"),
        P("wide", "narrow"),
        P(None, ("wide", "narrow")),
        P(None, ("wide", "narrow")),
        P(None, ("wide", "narrow")),
        P("narrow"),
        P(),
        P(None, ("wide", "narrow"), None),
    )
    return jax.shard_map(
        on_device,
        mesh=mesh,
        in_specs=placed,
        out_specs=(
            P(None, ("wide", "narrow"), None),
            P(None, ("wide", "narrow"), None),
            P("wide", "narrow"),
            P("wide", "narrow"),
            P("wide", "narrow"),
            P("wide", "narrow"),
            P("wide", "narrow"),
            P(None, ("wide", "narrow")),
            P(None, ("wide", "narrow")),
            P(None, ("wide", "narrow")),
        ),
        check_vma=False,
    )
```

```python
import functools
import math

import jax
import jax.numpy as jnp
from jax import lax
from jax.experimental import pallas as pl
from jax.experimental.pallas import tpu as pltpu
from jax.sharding import PartitionSpec as P

EPS = 1e-06
AXES = ("wide", "narrow")
BF16 = jnp.bfloat16
F32 = jnp.float32


def simple_norm(values):
    return values * lax.rsqrt(jnp.mean(values * values, axis=-1, keepdims=True) + EPS)


def norm_backward(values, cotangent):
    scale = lax.rsqrt(jnp.mean(values * values, axis=-1, keepdims=True) + EPS)
    inner = jnp.mean(values * cotangent, axis=-1, keepdims=True)
    return scale * cotangent - values * (scale * scale * scale * inner)


def apply_swish(values):
    return values * jax.nn.sigmoid(values)


def swish_slope(values):
    sigmoid_value = jax.nn.sigmoid(values)
    return sigmoid_value + values * sigmoid_value * (1.0 - sigmoid_value)


def exchange(x, mask):
    count = lax.axis_size(AXES)
    return lax.ppermute(x, AXES, [(i, i ^ mask) for i in range(count)])


def after(x, *others):
    return lax.optimization_barrier((x, *others))[0]


def shift_z(x, step, reverse):
    count, unit = lax.axis_size(AXES), 2 * lax.axis_size("narrow")
    pairs = [(i, i + step * unit) for i in range(count - step * unit)]
    if reverse:
        pairs = [(b, a) for a, b in pairs]
    return lax.ppermute(x, AXES, pairs)


def gather_plane(x, masks):
    return gather_more(x[None], masks)


def gather_more(held, masks):
    for mask in masks:
        held = jnp.concatenate([held, exchange(held, mask)], axis=0)
    return held


def gather_hidden(x, masks, swapped):
    held = gather_plane(x, masks)
    if swapped:
        held = jnp.swapaxes(held.reshape(2, 2, -1, *x.shape), 0, 1)
    return held.reshape(-1, x.shape[-1])


def scatter_plane(x, masks):
    for mask in reversed(masks):
        half = x.shape[0] // 2
        got = exchange(x[half:], mask)
        total = x[:half].astype(F32) + got.astype(F32)
        x = total.astype(BF16) if half > 1 else total
    return x[0]


def fold(mine, got, dtype=BF16):
    return (mine.astype(F32) + got.astype(F32)).astype(dtype)


def final(mine, got):
    return fold(mine, got, F32)


def relative(masks, index):
    out = 0
    for k, mask in enumerate(masks):
        out ^= mask * ((index >> k) & 1)
    return out


NT = (((1,), (1,)), ((), ()))
NN = (((1,), (0,)), ((), ()))
TN = (((0,), (0,)), ((), ()))


def mm(a, b, dims=NN):
    return lax.dot_general(a, b, dims, preferred_element_type=F32)


def turn(v, cosine, sine):
    return v * cosine + pltpu.roll(v, v.shape[-1] // 2, 1) * sine


def block_spots(masks):
    own = lax.axis_index(AXES)
    narrow_count = lax.axis_size("narrow")
    ids = jnp.array([relative(masks, i) for i in range(1 << len(masks))], jnp.int32) ^ own
    return jnp.stack([ids // narrow_count, (ids % narrow_count) // 2], axis=1)


def block_copy(spots, which, i, rows, cols, whole, part, sem, out):
    at = (
        pl.ds(pl.multiple_of(spots[which, i, 0] * rows, rows), rows),
        pl.ds(pl.multiple_of(spots[which, i, 1] * cols, cols), cols),
    )
    if out:
        return pltpu.make_async_copy(whole.at[at], part, sem)
    return pltpu.make_async_copy(part, whole.at[at], sem)


def each_block(spots, jobs, out=False):
    def go(method):
        for order, k, near, far, whole, sems in jobs:
            half, _, rows, cols = near.shape

            def step(i, _):
                for at, part in enumerate((near, far)):
                    copy = block_copy(
                        spots, order, i + at * half, rows, cols, whole, part.at[i, k],
                        sems.at[i + at * half], out,
                    )
                    getattr(copy, method)()
                return 0

            lax.fori_loop(0, half, step, 0)

    go("start")
    go("wait")


def both(near, far):
    rows = near.shape[0] * near.shape[1]
    return jnp.concatenate([near.reshape(rows, -1), far.reshape(rows, -1)], axis=0)


def slot_rows(x, s, size, count):
    return jnp.concatenate(
        [x[s * size : (s + 1) * size], x[(count + s) * size : (count + s + 1) * size]], axis=0
    )


def slot_back(parts, size):
    return jnp.concatenate([p[:size] for p in parts] + [p[size:] for p in parts], axis=0)


def put(ref, lanes, value):
    two, count, size, _ = ref.shape
    ref[:, :, :, lanes] = value.reshape(two, count, size, -1).astype(ref.dtype)


def get(ref, lanes=slice(None)):
    two, count, size, width = ref.shape
    x = ref[:, :, :, lanes]
    return x.reshape(two * count * size, x.shape[-1])


def key_value_kernel(
    spots, near, far, mask, cosine, sine, key_decay, kw0, kw1, vw0, vw1,
    key_pre, keys, values, state, wk, wv, sems
):
    @pl.when(pl.program_id(0) == 0)
    def _():
        each_block(spots, [(0, 0, kw0, kw1, wk, sems.at[0]), (2, 0, vw0, vw1, wv, sems.at[1])])

    count, size = near.shape[0], near.shape[1]
    x = both(near[...], far[...])
    valid = get(mask).astype(F32)
    head = cosine.shape[-1]
    pre = mm(x, wk[...])
    val_pre = mm(x, wv[...])
    for h in range(pre.shape[-1] // head):
        lanes = slice(h * head, (h + 1) * head)
        kp = pre[:, lanes]
        put(key_pre, lanes, kp)
        key = (valid * turn(kp * jax.nn.sigmoid(kp), cosine[...], sine[...])).astype(BF16)
        val = (valid * val_pre[:, lanes]).astype(BF16)
        put(keys, lanes, key)
        put(values, lanes, val)
        scaled = (key.astype(F32) * key_decay[:, lanes]).astype(BF16)
        for s in range(count):
            state[s, h] = mm(
                slot_rows(scaled, s, size, count), slot_rows(val, s, size, count), TN
            ).astype(BF16)


def query_kernel(
    spots, near, far, mask, cosine, sine, grid, keys, values, w0, w1,
    query_pre, queries, modulate, intra, wq, wm, sems
):
    @pl.when(pl.program_id(0) == 0)
    def _():
        each_block(spots, [(0, 0, w0, w1, wq, sems.at[0]), (0, 1, w0, w1, wm, sems.at[1])])

    count, size = near.shape[0], near.shape[1]
    x = both(near[...], far[...])
    valid = get(mask).astype(F32)
    head = cosine.shape[-1]
    pre = mm(x, wq[...])
    mod = mm(x, wm[...])
    for h in range(pre.shape[-1] // head):
        lanes = slice(h * head, (h + 1) * head)
        qp = pre[:, lanes]
        put(query_pre, lanes, qp)
        put(modulate, lanes, mod[:, lanes] * valid)
        q = turn(qp * jax.nn.sigmoid(qp), cosine[...], sine[...]).astype(BF16)
        put(queries, lanes, q)
        k, v = get(keys, lanes), get(values, lanes)
        scores = (mm(q, k, NT) * grid[h]).astype(BF16)
        put(intra, lanes, mm(scores, v))


def load_states(spots, pieces, held, sems):
    member = spots[3, 0, 0]
    copies = [
        pltpu.make_async_copy(p, held.at[member ^ k], sems.at[k]) for k, p in enumerate(pieces)
    ]
    for c in copies:
        c.start()
    for c in copies:
        c.wait()


def mixed_kernel(
    spots, queries, intra, modulate, query_decay, s0, s1, s2, s3, w0, w1,
    mixed, gated, near_out, far_out, wo, held, sems, state_sems
):
    @pl.when(pl.program_id(0) == 0)
    def _():
        load_states(spots, (s0, s1, s2, s3), held, state_sems)
        each_block(spots, [(1, 0, w0, w1, wo, sems)])

    step = pl.program_id(0)
    _, count, size, width = queries.shape
    heads = held.shape[2]
    head = width // heads
    gates = []
    for h in range(heads):
        lanes = slice(h * head, (h + 1) * head)
        q = (get(queries, lanes).astype(F32) * query_decay[:, lanes]).astype(BF16)
        parts = [mm(slot_rows(q, s, size, count), held[step, s, h]) for s in range(count)]
        mix = get(intra, lanes).astype(F32) + slot_back(parts, size)
        put(mixed, lanes, mix)
        scale = lax.rsqrt(jnp.mean(mix * mix, axis=-1, keepdims=True) + EPS)
        gates.append((mix * scale * get(modulate, lanes).astype(F32)).astype(BF16))
    gate = jnp.concatenate(gates, axis=1)
    put(gated, slice(None), gate)
    out = mm(gate, wo[...], NT)
    near_out[...] = out[: count * size].reshape(near_out.shape)
    far_out[...] = out[count * size :].astype(BF16).reshape(far_out.shape)


def mixed_back_kernel(
    spots, near, far, mixed, modulate, queries, query_pre, keys, values, mask, cosine, sine,
    query_decay, grid, grid_t, s0, s1, s2, s3, w0, w1,
    modulate_grad, query_grad, key_grad, value_grad, state_grad, wo, held, sems, state_sems
):
    @pl.when(pl.program_id(0) == 0)
    def _():
        load_states(spots, (s0, s1, s2, s3), held, state_sems)
        each_block(spots, [(1, 0, w0, w1, wo, sems)])

    step = pl.program_id(0)
    _, count, size, width = queries.shape
    heads = held.shape[2]
    head = width // heads
    gate_grad = mm(both(near[...], far[...]), wo[...])
    valid = get(mask).astype(F32)
    for h in range(heads):
        lanes = slice(h * head, (h + 1) * head)
        mix = get(mixed, lanes).astype(F32)
        scale = lax.rsqrt(jnp.mean(mix * mix, axis=-1, keepdims=True) + EPS)
        gg = gate_grad[:, lanes]
        put(modulate_grad, lanes, gg * valid * (mix * scale))
        cot = gg * get(modulate, lanes).astype(F32)
        inner = jnp.mean(mix * cot, axis=-1, keepdims=True)
        gm = (scale * cot - mix * (scale * scale * scale * inner)).astype(BF16)
        q, k, v = get(queries, lanes), get(keys, lanes), get(values, lanes)
        qs = (q.astype(F32) * query_decay[:, lanes]).astype(BF16)
        gst = (mm(v, gm, NT) * grid_t[h]).astype(BF16)
        gs = (mm(gm, v, NT) * grid[h]).astype(BF16)
        sct = (mm(k, q, NT) * grid_t[h]).astype(BF16)
        put(value_grad, lanes, mm(sct, gm))
        put(key_grad, lanes, mm(gst, q))
        gq = []
        for s in range(count):
            pick = lambda x: slot_rows(x, s, size, count)
            gms = pick(gm)
            gq.append(mm(gms, held[step, s, h], NT))
            state_grad[s, h] = mm(pick(qs), gms, TN).astype(BF16)
        gq = mm(gs, k) + slot_back(gq, size) * query_decay[:, lanes]
        qp = get(query_pre, lanes).astype(F32)
        sg = jax.nn.sigmoid(qp)
        slope = sg + qp * sg * (1.0 - sg)
        put(query_grad, lanes, turn(gq, cosine[...], -sine[...]) * slope)


def rows_kernel(
    spots, query_grad, modulate_grad, key_grad, value_grad, w0, w1, kw0, kw1, vw0, vw1,
    near_out, far_out, wq, wm, wk, wv, sems
):
    @pl.when(pl.program_id(0) == 0)
    def _():
        each_block(
            spots,
            [
                (0, 0, w0, w1, wq, sems.at[0]), (0, 1, w0, w1, wm, sems.at[1]),
                (0, 0, kw0, kw1, wk, sems.at[2]), (2, 0, vw0, vw1, wv, sems.at[3]),
            ],
        )

    out = mm(get(query_grad), wq[...], NT) + mm(get(modulate_grad), wm[...], NT)
    out = out + mm(get(key_grad), wk[...], NT) + mm(get(value_grad), wv[...], NT)
    half = out.shape[0] // 2
    near_out[...] = out[:half].reshape(near_out.shape)
    far_out[...] = out[half:].astype(BF16).reshape(far_out.shape)


def key_back_kernel(
    spots, key_grad, value_grad, keys, values, key_pre, mask, cosine, sine, key_decay,
    g0, g1, g2, g3, key_out, value_out, held, state_sems
):
    @pl.when(pl.program_id(0) == 0)
    def _():
        load_states(spots, (g0, g1, g2, g3), held, state_sems)

    step = pl.program_id(0)
    _, count, size, width = keys.shape
    heads = held.shape[2]
    head = width // heads
    valid = get(mask).astype(F32)
    for h in range(heads):
        lanes = slice(h * head, (h + 1) * head)
        decay = key_decay[:, lanes]
        k, v = get(keys, lanes), get(values, lanes)
        scaled = (k.astype(F32) * decay).astype(BF16)
        pk = [mm(slot_rows(v, s, size, count), held[step, s, h], NT) for s in range(count)]
        pv = [mm(slot_rows(scaled, s, size, count), held[step, s, h]) for s in range(count)]
        gk = get(key_grad, lanes).astype(F32) + slot_back(pk, size) * decay
        gv = get(value_grad, lanes).astype(F32) + slot_back(pv, size)
        kp = get(key_pre, lanes).astype(F32)
        sg = jax.nn.sigmoid(kp)
        slope = sg + kp * sg * (1.0 - sg)
        put(key_out, lanes, turn(gk * valid, cosine[...], -sine[...]) * slope)
        put(value_out, lanes, gv * valid)


def hidden_kernel(
    spots, n0, n1, n2, n3, b0, b1, b2, b3, mask, gate_w, lift_w, down_w,
    inner_out, gate_out, lift_out, keep, send, branch_keep, branch_send
):
    flat = lambda refs: jnp.concatenate([r[...].reshape(-1, r.shape[-1]) for r in refs], axis=0)
    x, b = flat((n0, n1, n2, n3)), flat((b0, b1, b2, b3))
    valid = get(mask)[:, :1].astype(F32)
    gate, lift, down = gate_w[...], lift_w[...], down_w[...]
    parts = []
    for r in range(0, x.shape[0], 256):
        rows = slice(r, r + 256)
        gate_pre = mm(x[rows], gate, NT)
        lift_pre = mm(x[rows], lift, NT)
        inner_grad = mm(b[rows], down, NT) * valid[rows]
        q = jax.nn.sigmoid(gate_pre)
        act = gate_pre * q
        gate_grad = (inner_grad * lift_pre * (q + act * (1.0 - q))).astype(BF16)
        lift_grad = (inner_grad * act).astype(BF16)
        inner = (act * lift_pre).astype(BF16)
        total = (mm(gate_grad, gate) + mm(lift_grad, lift)).astype(BF16)
        parts.append((inner, gate_grad, lift_grad, total, mm(inner, down).astype(BF16)))
    inner, gate_grad, lift_grad, total, branch = (jnp.concatenate(p, axis=0) for p in zip(*parts))
    put(inner_out, slice(None), inner)
    put(gate_out, slice(None), gate_grad)
    put(lift_out, slice(None), lift_grad)
    half = total.shape[0] // 2
    for near, far, value in ((keep, send, total), (branch_keep, branch_send, branch)):
        near[...] = value[:half].reshape(near.shape)
        far[...] = value[half:].reshape(far.shape)


def outer_kernel(order, spots, near, far, *refs):
    count = (len(refs) - 4) // 1
    grads, (keep, send, whole, sems) = refs[:count], refs[count:]
    rows = near.shape[0] * near.shape[1]
    width = near.shape[2]
    tile = 256
    for c in range(0, width, tile):
        a = near[:, :, c : c + tile].reshape(rows, tile)
        b = far[:, :, c : c + tile].reshape(rows, tile)
        for k, g in enumerate(grads):
            g0 = g[0].reshape(rows, -1)
            g1 = g[1].reshape(rows, -1)
            whole[k, c : c + tile, :] = (mm(a, g0, TN) + mm(b, g1, TN)).astype(BF16)
    each_block(
        spots, [(order, k, keep, send, whole.at[k], sems.at[k]) for k in range(count)], out=True
    )


ANY = pl.BlockSpec(memory_space=pltpu.HBM)
VMEM = pl.BlockSpec(memory_space=pltpu.VMEM)


def run(kernel, name, spots, inputs, outputs, scratch, steps, flops):
    def spec(shape, kind):
        if kind == "any":
            return ANY
        if kind == "rows":
            size = shape[0] // steps
            return pl.BlockSpec((size, *shape[1:]), lambda i, _: (i,) + (0,) * (len(shape) - 1))
        if kind == "pair":
            size = shape[1] // steps
            return pl.BlockSpec(
                (shape[0], size, *shape[2:]), lambda i, _: (0, i) + (0,) * (len(shape) - 2)
            )
        return pl.BlockSpec(shape, lambda i, _: (0,) * len(shape))

    moved = sum(a.size * a.dtype.itemsize for a, _ in inputs)
    moved += sum(math.prod(s) * jnp.dtype(d).itemsize for s, d, _ in outputs)
    return pl.pallas_call(
        kernel,
        out_shape=[jax.ShapeDtypeStruct(s, d) for s, d, _ in outputs],
        grid_spec=pltpu.PrefetchScalarGridSpec(
            num_scalar_prefetch=1,
            grid=(steps,),
            in_specs=[spec(a.shape, kind) for a, kind in inputs],
            out_specs=[spec(s, kind) for s, _, kind in outputs],
            scratch_shapes=scratch,
        ),
        compiler_params=pltpu.CompilerParams(vmem_limit_bytes=40 * 2**20),
        cost_estimate=pl.CostEstimate(flops=int(flops * 2), bytes_accessed=int(moved * 2), transcendentals=0),
        name=name,
    )(spots, *[a for a, _ in inputs])


class Carry:
    def __init__(self, local, block_decay, reverse):
        self.local, self.reverse = local, reverse
        narrow_count = lax.axis_size("narrow")
        self.member = 2 * (lax.axis_index("wide") % 2) + lax.axis_index("narrow") // 2
        self.masks = [0, 2, narrow_count, narrow_count + 2]
        ranks = [self.member ^ k for k in range(4)]
        self.ranks = [3 - r if reverse else r for r in ranks]
        self.log_decay = jnp.log(block_decay)

    def power(self, e):
        return jnp.exp(e * self.log_decay)[None, :, None, None]

    def spread(self):
        share = self.local.shape[0] // 4
        parts = [
            lax.dynamic_slice_in_dim(self.local, (self.member ^ k) * share, share, 0)
            for k in range(4)
        ]
        self.got = [parts[0]] + [exchange(parts[k], self.masks[k]) for k in range(1, 4)]

    def along(self, between=lambda step, got: got):
        self.held = [h.astype(F32) for h in self.got]
        span = sum(self.power((3 - self.ranks[k]).astype(F32)) * self.held[k] for k in range(4))
        before, step = 0.0, 1
        while step < lax.axis_size("wide") // 2:
            got = between(step, shift_z(span.astype(BF16), step, self.reverse)).astype(F32)
            before = before + self.power(4.0 * (step - 1)) * got
            span = span + self.power(4.0 * step) * got
            step *= 2
        self.before = before

    def back(self):
        sent = []
        for k in range(4):
            state = self.power(self.ranks[k].astype(F32)) * self.before
            for j in range(4):
                gap = (self.ranks[k] - 1 - self.ranks[j]).astype(F32)
                scale = jnp.where(gap >= 0, self.power(jnp.maximum(gap, 0.0)), 0.0)
                state = state + scale * self.held[j]
            sent.append(state.astype(BF16))
        return [sent[0]] + [exchange(sent[k], self.masks[k]) for k in range(1, 4)]


def on_device(
    layer_input,
    query_weight,
    key_weight,
    value_weight,
    modulate_weight,
    output_weight,
    gate_matrix,
    lift_matrix,
    down_matrix,
    decay_factor,
    valid_lengths,
    output_cotangent,
):
    narrow_count, wide_count = lax.axis_size("narrow"), lax.axis_size("wide")
    wide_index, narrow_index = lax.axis_index("wide"), lax.axis_index("narrow")
    core, side = narrow_index % 2, narrow_index // 2
    slots, quarter, width = layer_input.shape
    block = 2 * quarter
    rows, cols = query_weight.shape
    heads = 2 * decay_factor.shape[0]
    head_size = cols // decay_factor.shape[0]
    x_mask = 2
    wide_masks = []
    bit = narrow_count
    while bit < narrow_count * wide_count:
        wide_masks.append(bit)
        bit *= 2
    y_mask, z_masks = wide_masks[0], wide_masks[:0:-1]
    order_yx = z_masks + [y_mask, x_mask]
    order_xy = z_masks + [x_mask, y_mask]
    order_v = [y_mask] + z_masks + [x_mask]
    members = 1 << len(order_yx)
    half = members // 2

    base = wide_index * (quarter * narrow_count) + side * block
    offsets = jnp.stack(
        [core * quarter + jnp.arange(quarter), (1 - core) * quarter + jnp.arange(quarter)]
    ).astype(jnp.int32)
    mask = ((base + offsets)[:, None, :] < valid_lengths[None, :, None]).astype(F32)
    mask_rows = mask[0][:, :, None]
    mask_wide = jnp.broadcast_to(mask[..., None], (2, slots, quarter, head_size)).astype(BF16)
    member = 2 * (wide_index % 2) + side
    spots = jnp.concatenate(
        [
            block_spots(order_xy)[None],
            block_spots(order_yx)[None],
            block_spots(order_v)[None],
            jnp.broadcast_to(member, (1, members, 2)).astype(jnp.int32),
        ]
    )

    def core_sum(near, far):
        return near + exchange(far, 1).astype(F32)

    other_decay = exchange(decay_factor, x_mask)
    decay = jnp.concatenate(
        [jnp.where(side == 0, decay_factor, other_decay), jnp.where(side == 0, other_decay, decay_factor)]
    )
    log_decay = jnp.log(decay)
    block_decay = jnp.exp(block * log_decay)
    steps = 4
    count = slots // steps

    def table(values):
        lanes = values.shape[-1]
        return jnp.broadcast_to(values[:, None], (2, count, quarter, lanes)).reshape(-1, lanes)

    half_head = head_size // 2
    frequency = jnp.exp(-math.log(10000.0) * jnp.arange(half_head, dtype=F32) / half_head)
    phase = (base + offsets).astype(F32)[..., None] * frequency
    cosine, sine = jnp.cos(phase), jnp.sin(phase)
    cosine = table(jnp.concatenate([cosine, cosine], axis=-1))
    sine = table(jnp.concatenate([-sine, sine], axis=-1))
    spot = offsets.astype(F32)
    log_lanes = jnp.repeat(log_decay, head_size)
    query_decay = table(jnp.exp((spot[..., None] + 1.0) * log_lanes))
    key_decay = table(jnp.exp((block - 1.0 - spot[..., None]) * log_lanes))
    flat = jnp.broadcast_to(spot[:, None], (2, count, quarter)).reshape(-1)
    slot_of = jnp.broadcast_to(jnp.arange(count)[None, :, None], (2, count, quarter)).reshape(-1)
    gap = flat[:, None] - flat[None, :]
    seen = (gap >= 0.0) & (slot_of[:, None] == slot_of[None, :])
    decay_grid = jnp.where(
        seen[None], jnp.exp(jnp.maximum(gap, 0.0)[None] * log_decay[:, None, None]), 0.0
    )
    decay_grid_t = jnp.swapaxes(decay_grid, 1, 2)

    def join(*parts):
        return jnp.concatenate(parts, axis=0)

    z_far, z_near = z_masks[:-1], z_masks[-1]
    swap = exchange

    def tie(*arrays):
        return lax.optimization_barrier(arrays)

    def far_open(x):
        for m in z_far[:-1]:
            x = join(x, swap(x, m))
        return x, swap(x, z_far[-1])

    key_w, value_w = key_weight[None, None], value_weight[None, None]
    dn = down_matrix.T[None]
    gl = jnp.stack([gate_matrix.T, lift_matrix.T])[None]
    qmo = jnp.stack([query_weight, modulate_weight, output_weight])[None]
    input_rows = layer_input.astype(F32)
    normed = simple_norm(input_rows).astype(BF16)
    cotangent = output_cotangent.astype(F32)
    cotangent_x = [swap(output_cotangent[: slots // 2], x_mask)]
    key_w, k_got = far_open(key_w)
    k_got, v_got = tie(k_got, swap(value_w, y_mask))
    key_w, value_w = join(key_w, k_got), join(value_w, v_got)
    value_w, v_got = far_open(value_w)
    k_got, v_got, dn_y, cotangent_x[0] = tie(
        swap(key_w, z_near), v_got, swap(dn, y_mask), cotangent_x[0]
    )
    key_w, value_w, dn = join(key_w, k_got), join(value_w, v_got), join(dn, dn_y)
    normed_pair = (normed, swap(normed, 1))
    k_got, v_got = tie(swap(key_w, x_mask), swap(value_w, z_near))
    key_w, value_w, qmo = join(key_w, k_got), join(value_w, v_got), tie(qmo, k_got)[0]
    qmo, q_got = far_open(qmo)
    k_got, v_got, q_got = tie(swap(key_w, y_mask), swap(value_w, x_mask), q_got)
    key_parts, value_parts = (key_w, k_got), (value_w, v_got)
    qmo = join(qmo, q_got)
    qmo_z = swap(qmo, z_near)
    inner_width = heads * head_size
    chip_shape = (2, slots, quarter, inner_width)
    row_shape = (slots, quarter, width)
    state_shape = (slots, heads, head_size, head_size)
    square_flops = 2 * 2 * slots * quarter * width * inner_width
    wide_scratch = pltpu.VMEM((width, inner_width), BF16)
    held_scratch = pltpu.VMEM((4, slots // 4, heads, head_size, head_size), BF16)
    dma = pltpu.SemaphoreType.DMA

    key_pre, keys, values, local_state = run(
        key_value_kernel, "key_value", spots,
        [
            (normed_pair[0], "rows"), (normed_pair[1], "rows"), (mask_wide, "pair"),
            (cosine, "whole"), (sine, "whole"), (key_decay, "whole"),
            (key_parts[0], "any"), (key_parts[1], "any"),
            (value_parts[0], "any"), (value_parts[1], "any"),
        ],
        [
            (chip_shape, BF16, "pair"), (chip_shape, BF16, "pair"), (chip_shape, BF16, "pair"),
            (state_shape, BF16, "rows"),
        ],
        [wide_scratch, wide_scratch, dma((2, members))],
        steps, 2 * square_flops,
    )
    local_state, qmo_z = tie(local_state, qmo_z)
    qmo = join(qmo, qmo_z)
    qm, out_w = qmo[:, :2], qmo[:, 2:]
    scan = Carry(local_state, block_decay, False)
    scan.spread()
    gl, gl_got = far_open(tie(gl, qmo_z)[0])
    scan.got[1], scan.got[2], scan.got[3], qm, out_w = tie(*scan.got[1:], qm, out_w)
    qm_x, o_y = swap(qm, x_mask), swap(out_w, y_mask)
    held = {}

    def forward_step(step, got):
        if step == 1:
            got, qx, oy, held["gl"] = tie(got, qm_x, o_y, gl_got)
            held["qm"], held["out"] = join(qm, qx), join(out_w, oy)
            held["gl"] = join(gl, held["gl"])
            held["more"] = [
                swap(held["qm"], y_mask), swap(held["out"], x_mask), swap(held["gl"], z_near),
                swap(tie(output_cotangent[slots // 2 :], oy)[0], x_mask),
            ]
        if step == 2:
            got, *held["more"] = tie(got, *held["more"])
        return got

    scan.along(forward_step)
    qm_y, o_x, gl_z, more_x = held["more"]
    cotangent_x.append(more_x)
    gl = join(held["gl"], gl_z)
    query_parts, output_parts = (held["qm"], qm_y), (held["out"], o_x)
    dn, dn_got = far_open(tie(dn, gl_z)[0])
    state_parts = scan.back()
    query_pre, queries, modulate, intra = run(
        query_kernel, "query", spots,
        [
            (normed_pair[0], "rows"), (normed_pair[1], "rows"), (mask_wide, "pair"),
            (cosine, "whole"), (sine, "whole"), (decay_grid, "whole"),
            (keys, "pair"), (values, "pair"), (query_parts[0], "any"), (query_parts[1], "any"),
        ],
        [
            (chip_shape, BF16, "pair"), (chip_shape, BF16, "pair"), (chip_shape, BF16, "pair"),
            (chip_shape, BF16, "pair"),
        ],
        [wide_scratch, wide_scratch, dma((2, members))],
        steps, 2 * square_flops,
    )
    *state_parts, queries, dn_got = tie(*state_parts, queries, dn_got)
    dn = join(dn, dn_got)
    state_inputs = [(p, "any") for p in state_parts]
    output_inputs = [(p, "any") for p in output_parts]
    mixed, gated, near_att, far_att = run(
        mixed_kernel, "mixed", spots,
        [
            (queries, "pair"), (intra, "pair"), (modulate, "pair"), (query_decay, "whole"),
            *state_inputs, *output_inputs,
        ],
        [
            (chip_shape, BF16, "pair"), (chip_shape, BF16, "pair"), (row_shape, F32, "rows"),
            (row_shape, BF16, "rows"),
        ],
        [wide_scratch, held_scratch, dma((members,)), dma((4,))],
        steps, square_flops,
    )
    middle = input_rows + core_sum(near_att, far_att)
    two = simple_norm(middle).astype(BF16)
    two_x, gl_y = tie(swap(two, x_mask), swap(gl, y_mask))
    dn_z = swap(dn, z_near)

    def quarters(mine, got_x):
        return [mine, got_x, swap(mine, 1), swap(got_x, 1)]

    def core_part(keep, send):
        got = swap(send, 1)
        return fold(keep[0], got[0], F32), fold(keep[1], got[1])

    two_pieces = quarters(two, two_x)
    normed_two = jnp.stack(two_pieces)
    row_starts = (narrow_index ^ jnp.array([0, x_mask, 1, 1 + x_mask], jnp.int32)) * quarter
    row_spots = wide_index * (quarter * narrow_count) + row_starts[:, None] + jnp.arange(quarter)
    row_mask = (row_spots[:, None, :] < valid_lengths[None, :, None]).astype(F32)[..., None]
    branch_pieces = quarters(output_cotangent, jnp.concatenate(cotangent_x))
    row_mask_wide = jnp.broadcast_to(row_mask, (4, slots, quarter, head_size)).astype(BF16)
    gate_t = join(gl[:, 0], gl_y[:, 0]).reshape(-1, width)
    lift_t = join(gl[:, 1], gl_y[:, 1]).reshape(-1, width)
    bulk = half // 2
    down_t = jnp.swapaxes(join(dn, dn_z).reshape(bulk, 2, -1, width), 0, 1).reshape(-1, width)

    def outer(a, b):
        return jnp.einsum("pblf,pbld->fd", a, b, preferred_element_type=F32).astype(BF16)

    hidden_shape = (4, slots, quarter, gate_t.shape[0])
    sum_shape = (2, slots, quarter, width)
    hidden_flops = 2 * 4 * slots * quarter * width * gate_t.shape[0]
    inner, gate_grad, lift_grad, row_keep, row_send, branch_keep, branch_send = run(
        hidden_kernel, "hidden", spots,
        [
            *[(p, "rows") for p in two_pieces], *[(p, "rows") for p in branch_pieces],
            (row_mask_wide, "pair"), (gate_t, "whole"),
            (lift_t, "whole"), (down_t, "whole"),
        ],
        [(hidden_shape, BF16, "pair")] * 3 + [(sum_shape, BF16, "pair")] * 4,
        [], steps, 6 * hidden_flops,
    )
    row_mine, row_send = core_part(row_keep, row_send)
    row_got = swap(row_send, x_mask)
    branch_rows = jnp.stack(branch_pieces).astype(F32)
    branch_rows = (tie(row_mask, row_send)[0] * branch_rows).astype(BF16)
    gate_grad, lift_grad, inner, row_send = tie(gate_grad, lift_grad, inner, row_send)
    gate_g = outer(gate_grad, normed_two).reshape(2, bulk, -1, width)
    gate_y = swap(gate_g[1], y_mask)
    lift_grad, inner, gate_g = tie(lift_grad, inner, gate_g)
    lift_g = outer(lift_grad, normed_two).reshape(2, bulk, -1, width)
    down_g = outer(inner, branch_rows).reshape(2, 2, bulk // 2, -1, width)
    branch_mine, branch_send = core_part(branch_keep, branch_send)
    row_got, gate_y, lift_g, down_z_send, branch_send = tie(
        row_got, gate_y, lift_g, down_g[:, 1], branch_send
    )
    lift_y = swap(lift_g[1], y_mask)
    branch_got = swap(branch_send, x_mask)
    down_z = swap(down_z_send, z_near)
    middle_grad = cotangent + norm_backward(middle, row_mine + row_got.astype(F32))

    attended_grad = middle_grad.astype(BF16)
    attended_pair = (attended_grad, exchange(attended_grad, 1))
    modulate_grad, query_grad, key_grad, value_grad, state_grad = run(
        mixed_back_kernel, "mixed_back", spots,
        [
            (attended_pair[0], "rows"), (attended_pair[1], "rows"), (mixed, "pair"),
            (modulate, "pair"), (queries, "pair"), (query_pre, "pair"), (keys, "pair"),
            (values, "pair"), (mask_wide, "pair"), (cosine, "whole"), (sine, "whole"),
            (query_decay, "whole"), (decay_grid, "whole"), (decay_grid_t, "whole"),
            *state_inputs, *output_inputs,
        ],
        [
            (chip_shape, BF16, "pair"), (chip_shape, BF16, "pair"), (chip_shape, BF16, "pair"),
            (chip_shape, BF16, "pair"), (state_shape, BF16, "rows"),
        ],
        [wide_scratch, held_scratch, dma((members,)), dma((4,))],
        steps, 2 * square_flops,
    )
    state_grad, lift_y, gated = tie(state_grad, lift_y, gated)
    near = bulk // 2
    scan = Carry(state_grad, block_decay, True)
    scan.spread()

    def square(name, order, a, *grads):
        shape = (half, len(grads), rows, cols)
        return run(
            functools.partial(outer_kernel, order), name, spots,
            [(a[0], "whole"), (a[1], "whole"), *[(g, "whole") for g in grads]],
            [(shape, BF16, "any"), (shape, BF16, "any")],
            [pltpu.VMEM((len(grads), width, inner_width), BF16), dma((len(grads), members))],
            1, len(grads) * square_flops,
        )

    output_keep, output_send = square("output_outer", 1, attended_pair, gated)
    query_keep, query_send = square("query_outer", 0, normed_pair, query_grad, modulate_grad)
    *scan.got, down_z, branch_got, query_keep, query_send, output_keep, output_send = tie(
        *scan.got, down_z, branch_got, query_keep, query_send, output_keep, output_send
    )
    layer_output = (middle + mask_rows * (branch_mine + branch_got.astype(F32))).astype(BF16)
    down_g = jnp.moveaxis(fold(down_g[:, 0], down_z), 1, 0)
    for m in z_far[:0:-1]:
        size = down_g.shape[0] // 2
        down_g = fold(down_g[:size], swap(down_g[size:], m))
    gl_g = jnp.stack([fold(gate_g[0], gate_y), fold(lift_g[0], lift_y)], axis=1)

    query_y, output_x = swap(query_send[:, :1], y_mask), swap(output_send, x_mask)

    def backward_step(step, got):
        if step == 1:
            got, held["y"], mod_send = tie(got, query_y, query_send[:, 1:])
            held["more"] = swap(mod_send, y_mask)
        if step == 2:
            got, held["more"], held["x"] = tie(got, held["more"], output_x)
        return got

    scan.along(backward_step)
    query_y = jnp.concatenate([held["y"], held["more"]], axis=1)
    scan.before, down_g, gl_g = tie(scan.before, down_g, gl_g)
    down_far = swap(down_g[1], z_far[0])
    gl_z = swap(gl_g[near:], z_near)
    later_parts = list(tie(*scan.back()))
    query_keep, output_keep = tie(query_keep, output_keep, *later_parts)[:2]
    query_g, output_g = fold(query_keep, query_y), fold(output_keep, held["x"])
    quad = half // 2
    query_x, output_y = swap(query_g[quad:], x_mask), swap(output_g[quad:], y_mask)
    later_inputs = [(p, "any") for p in later_parts]
    quad = half // 2
    def far_pairs(x):
        x = x.reshape(-1, 2, *x.shape[1:])
        for m in reversed(z_far):
            size = x.shape[0] // 2
            x = fold(x[:size], swap(x[size:], m))
        return x[0]

    def far_folds(x):
        for m in reversed(z_far):
            size = x.shape[0] // 2
            x = (fold if size > 1 else final)(x[:size], swap(x[size:], m))
        return x

    key_out, value_out = run(
        key_back_kernel, "key_back", spots,
        [
            (key_grad, "pair"), (value_grad, "pair"), (keys, "pair"), (values, "pair"),
            (key_pre, "pair"), (mask_wide, "pair"), (cosine, "whole"), (sine, "whole"),
            (key_decay, "whole"), *later_inputs,
        ],
        [(chip_shape, BF16, "pair"), (chip_shape, BF16, "pair")],
        [held_scratch, dma((4,))],
        steps, square_flops // 2,
    )
    key_keep, key_send = square("key_outer", 0, normed_pair, key_out)
    value_keep, value_send = square("value_outer", 2, normed_pair, value_out)
    key_send, value_send, gl_z, down_far, query_x, output_y = tie(
        key_send, value_send, gl_z, down_far, query_x, output_y
    )
    down_g = fold(down_g[0], down_far)
    gl_g = fold(gl_g[:near], gl_z)
    for m in z_far[:0:-1]:
        size = gl_g.shape[0] // 2
        gl_g = fold(gl_g[:size], swap(gl_g[size:], m))
    gl_far = swap(gl_g[1], z_far[0])
    key_y, value_x = swap(key_send, y_mask), swap(value_send, x_mask)
    key_out, value_out = tie(key_out, value_out, key_send, value_send)[:2]
    near_rows, far_rows = run(
        rows_kernel, "rows", spots,
        [
            (query_grad, "pair"), (modulate_grad, "pair"), (key_out, "pair"),
            (value_out, "pair"), (query_parts[0], "any"), (query_parts[1], "any"),
            (key_parts[0], "any"), (key_parts[1], "any"),
            (value_parts[0], "any"), (value_parts[1], "any"),
        ],
        [(row_shape, F32, "rows"), (row_shape, BF16, "rows")],
        [wide_scratch] * 4 + [dma((4, members))],
        steps, 4 * square_flops,
    )
    key_y, value_x, near_rows = tie(key_y, value_x, near_rows)
    down_y = swap(down_g[1], y_mask)
    key_g, value_g = fold(key_keep, key_y), fold(value_keep, value_x)
    key_x, value_z = swap(key_g[quad:], x_mask), swap(value_g[quad:], z_near)
    qmo_g = jnp.concatenate(
        [fold(query_g[:quad], query_x), fold(output_g[:quad], output_y)], axis=1
    )
    qmo_z = swap(qmo_g[near:], z_near)
    key_x, value_z, down_y, qmo_z, gl_far = tie(key_x, value_z, down_y, qmo_z, gl_far)
    gate_lift = final(gl_g[0], gl_far)
    key_g, value_g = fold(key_g[:quad], key_x), fold(value_g[:quad], value_z)
    key_z, value_far = swap(key_g[near:], z_near), far_pairs(value_g)
    qmo_g = far_folds(fold(qmo_g[:near], qmo_z))[0]
    key_gradient = far_folds(fold(key_g[:near], key_z))[0][0]
    value_y = swap(value_far[1], y_mask)
    value_gradient = final(value_far[0], value_y)[0]
    query_gradient, modulate_gradient, output_gradient = qmo_g
    down_gradient = final(down_g[0], down_y).T
    gate_gradient, lift_gradient = gate_lift[0].T, gate_lift[1].T
    input_gradient = middle_grad + norm_backward(input_rows, core_sum(near_rows, far_rows))
    return (
        layer_output,
        input_gradient,
        query_gradient,
        key_gradient,
        value_gradient,
        modulate_gradient,
        output_gradient,
        gate_gradient,
        lift_gradient,
        down_gradient,
    )


def solution(mesh):
    placed = (
        P(None, ("wide", "narrow"), None),
        P("wide", "narrow"),
        P("wide", "narrow"),
        P("wide", "narrow"),
        P("wide", "narrow"),
        P("wide", "narrow"),
        P(None, ("wide", "narrow")),
        P(None, ("wide", "narrow")),
        P(None, ("wide", "narrow")),
        P("narrow"),
        P(),
        P(None, ("wide", "narrow"), None),
    )
    return jax.shard_map(
        on_device,
        mesh=mesh,
        in_specs=placed,
        out_specs=(
            P(None, ("wide", "narrow"), None),
            P(None, ("wide", "narrow"), None),
            P("wide", "narrow"),
            P("wide", "narrow"),
            P("wide", "narrow"),
            P("wide", "narrow"),
            P("wide", "narrow"),
            P(None, ("wide", "narrow")),
            P(None, ("wide", "narrow")),
            P(None, ("wide", "narrow")),
        ),
        check_vma=False,
    )
```

```python
import functools
import math

import jax
import jax.numpy as jnp
from jax import lax
from jax.experimental import pallas as pl
from jax.experimental.pallas import tpu as pltpu
from jax.sharding import PartitionSpec as P

EPS = 1e-06
AXES = ("wide", "narrow")
BF16 = jnp.bfloat16
F32 = jnp.float32


def simple_norm(values):
    return values * lax.rsqrt(jnp.mean(values * values, axis=-1, keepdims=True) + EPS)


def norm_backward(values, cotangent):
    scale = lax.rsqrt(jnp.mean(values * values, axis=-1, keepdims=True) + EPS)
    inner = jnp.mean(values * cotangent, axis=-1, keepdims=True)
    return scale * cotangent - values * (scale * scale * scale * inner)


def apply_swish(values):
    return values * jax.nn.sigmoid(values)


def swish_slope(values):
    sigmoid_value = jax.nn.sigmoid(values)
    return sigmoid_value + values * sigmoid_value * (1.0 - sigmoid_value)


def exchange(x, mask):
    count = lax.axis_size(AXES)
    return lax.ppermute(x, AXES, [(i, i ^ mask) for i in range(count)])


def after(x, *others):
    return lax.optimization_barrier((x, *others))[0]


def shift_z(x, step, reverse):
    count, unit = lax.axis_size(AXES), 2 * lax.axis_size("narrow")
    pairs = [(i, i + step * unit) for i in range(count - step * unit)]
    if reverse:
        pairs = [(b, a) for a, b in pairs]
    return lax.ppermute(x, AXES, pairs)


def gather_plane(x, masks):
    return gather_more(x[None], masks)


def gather_more(held, masks):
    for mask in masks:
        held = jnp.concatenate([held, exchange(held, mask)], axis=0)
    return held


def gather_hidden(x, masks, swapped):
    held = gather_plane(x, masks)
    if swapped:
        held = jnp.swapaxes(held.reshape(2, 2, -1, *x.shape), 0, 1)
    return held.reshape(-1, x.shape[-1])


def scatter_plane(x, masks):
    for mask in reversed(masks):
        half = x.shape[0] // 2
        got = exchange(x[half:], mask)
        total = x[:half].astype(F32) + got.astype(F32)
        x = total.astype(BF16) if half > 1 else total
    return x[0]


def fold(mine, got, dtype=BF16):
    return (mine.astype(F32) + got.astype(F32)).astype(dtype)


def final(mine, got):
    return fold(mine, got, F32)


def relative(masks, index):
    out = 0
    for k, mask in enumerate(masks):
        out ^= mask * ((index >> k) & 1)
    return out


NT = (((1,), (1,)), ((), ()))
NN = (((1,), (0,)), ((), ()))
TN = (((0,), (0,)), ((), ()))


def mm(a, b, dims=NN):
    return lax.dot_general(a, b, dims, preferred_element_type=F32)


def turn(v, cosine, sine):
    return v * cosine + pltpu.roll(v, v.shape[-1] // 2, 1) * sine


def block_spots(masks):
    own = lax.axis_index(AXES)
    narrow_count = lax.axis_size("narrow")
    ids = jnp.array([relative(masks, i) for i in range(1 << len(masks))], jnp.int32) ^ own
    return jnp.stack([ids // narrow_count, (ids % narrow_count) // 2], axis=1)


def block_copy(spots, which, i, rows, cols, whole, part, sem, out):
    at = (
        pl.ds(pl.multiple_of(spots[which, i, 0] * rows, rows), rows),
        pl.ds(pl.multiple_of(spots[which, i, 1] * cols, cols), cols),
    )
    if out:
        return pltpu.make_async_copy(whole.at[at], part, sem)
    return pltpu.make_async_copy(part, whole.at[at], sem)


def each_block(spots, jobs, out=False):
    def go(method):
        for order, k, near, far, whole, sems in jobs:
            half, _, rows, cols = near.shape

            def step(i, _):
                for at, part in enumerate((near, far)):
                    copy = block_copy(
                        spots, order, i + at * half, rows, cols, whole, part.at[i, k],
                        sems.at[i + at * half], out,
                    )
                    getattr(copy, method)()
                return 0

            lax.fori_loop(0, half, step, 0)

    go("start")
    go("wait")


def both(near, far):
    rows = near.shape[0] * near.shape[1]
    return jnp.concatenate([near.reshape(rows, -1), far.reshape(rows, -1)], axis=0)


def slot_rows(x, s, size, count):
    return jnp.concatenate(
        [x[s * size : (s + 1) * size], x[(count + s) * size : (count + s + 1) * size]], axis=0
    )


def slot_back(parts, size):
    return jnp.concatenate([p[:size] for p in parts] + [p[size:] for p in parts], axis=0)


def put(ref, lanes, value):
    two, count, size, _ = ref.shape
    ref[:, :, :, lanes] = value.reshape(two, count, size, -1).astype(ref.dtype)


def get(ref, lanes=slice(None)):
    two, count, size, width = ref.shape
    x = ref[:, :, :, lanes]
    return x.reshape(two * count * size, x.shape[-1])


def key_value_kernel(
    spots, near, far, mask, cosine, sine, key_decay, kw0, kw1, vw0, vw1,
    key_pre, keys, values, state, wk, wv, sems
):
    @pl.when(pl.program_id(0) == 0)
    def _():
        each_block(spots, [(0, 0, kw0, kw1, wk, sems.at[0]), (2, 0, vw0, vw1, wv, sems.at[1])])

    count, size = near.shape[0], near.shape[1]
    x = both(near[...], far[...])
    valid = get(mask).astype(F32)
    head = cosine.shape[-1]
    pre = mm(x, wk[...])
    val_pre = mm(x, wv[...])
    for h in range(pre.shape[-1] // head):
        lanes = slice(h * head, (h + 1) * head)
        kp = pre[:, lanes]
        put(key_pre, lanes, kp)
        key = (valid * turn(kp * jax.nn.sigmoid(kp), cosine[...], sine[...])).astype(BF16)
        val = (valid * val_pre[:, lanes]).astype(BF16)
        put(keys, lanes, key)
        put(values, lanes, val)
        scaled = (key.astype(F32) * key_decay[:, lanes]).astype(BF16)
        for s in range(count):
            state[s, h] = mm(
                slot_rows(scaled, s, size, count), slot_rows(val, s, size, count), TN
            ).astype(BF16)


def query_kernel(
    spots, near, far, mask, cosine, sine, grid, keys, values, w0, w1,
    query_pre, queries, modulate, intra, wq, wm, sems
):
    @pl.when(pl.program_id(0) == 0)
    def _():
        each_block(spots, [(0, 0, w0, w1, wq, sems.at[0]), (0, 1, w0, w1, wm, sems.at[1])])

    count, size = near.shape[0], near.shape[1]
    x = both(near[...], far[...])
    valid = get(mask).astype(F32)
    head = cosine.shape[-1]
    pre = mm(x, wq[...])
    mod = mm(x, wm[...])
    for h in range(pre.shape[-1] // head):
        lanes = slice(h * head, (h + 1) * head)
        qp = pre[:, lanes]
        put(query_pre, lanes, qp)
        put(modulate, lanes, mod[:, lanes] * valid)
        q = turn(qp * jax.nn.sigmoid(qp), cosine[...], sine[...]).astype(BF16)
        put(queries, lanes, q)
        k, v = get(keys, lanes), get(values, lanes)
        scores = (mm(q, k, NT) * grid[h]).astype(BF16)
        put(intra, lanes, mm(scores, v))


def load_states(spots, pieces, held, sems):
    member = spots[3, 0, 0]
    copies = [
        pltpu.make_async_copy(p, held.at[member ^ k], sems.at[k]) for k, p in enumerate(pieces)
    ]
    for c in copies:
        c.start()
    for c in copies:
        c.wait()


def mixed_kernel(
    spots, queries, intra, modulate, query_decay, s0, s1, s2, s3, w0, w1,
    mixed, gated, near_out, far_out, wo, held, sems, state_sems
):
    @pl.when(pl.program_id(0) == 0)
    def _():
        load_states(spots, (s0, s1, s2, s3), held, state_sems)
        each_block(spots, [(1, 0, w0, w1, wo, sems)])

    step = pl.program_id(0)
    _, count, size, width = queries.shape
    heads = held.shape[2]
    head = width // heads
    gates = []
    for h in range(heads):
        lanes = slice(h * head, (h + 1) * head)
        q = (get(queries, lanes).astype(F32) * query_decay[:, lanes]).astype(BF16)
        parts = [mm(slot_rows(q, s, size, count), held[step, s, h]) for s in range(count)]
        mix = get(intra, lanes).astype(F32) + slot_back(parts, size)
        put(mixed, lanes, mix)
        scale = lax.rsqrt(jnp.mean(mix * mix, axis=-1, keepdims=True) + EPS)
        gates.append((mix * scale * get(modulate, lanes).astype(F32)).astype(BF16))
    gate = jnp.concatenate(gates, axis=1)
    put(gated, slice(None), gate)
    out = mm(gate, wo[...], NT)
    near_out[...] = out[: count * size].reshape(near_out.shape)
    far_out[...] = out[count * size :].astype(BF16).reshape(far_out.shape)


def mixed_back_kernel(
    spots, near, far, mixed, modulate, queries, query_pre, keys, values, mask, cosine, sine,
    query_decay, grid, grid_t, s0, s1, s2, s3, w0, w1,
    modulate_grad, query_grad, key_grad, value_grad, state_grad, wo, held, sems, state_sems
):
    @pl.when(pl.program_id(0) == 0)
    def _():
        load_states(spots, (s0, s1, s2, s3), held, state_sems)
        each_block(spots, [(1, 0, w0, w1, wo, sems)])

    step = pl.program_id(0)
    _, count, size, width = queries.shape
    heads = held.shape[2]
    head = width // heads
    gate_grad = mm(both(near[...], far[...]), wo[...])
    valid = get(mask).astype(F32)
    for h in range(heads):
        lanes = slice(h * head, (h + 1) * head)
        mix = get(mixed, lanes).astype(F32)
        scale = lax.rsqrt(jnp.mean(mix * mix, axis=-1, keepdims=True) + EPS)
        gg = gate_grad[:, lanes]
        put(modulate_grad, lanes, gg * valid * (mix * scale))
        cot = gg * get(modulate, lanes).astype(F32)
        inner = jnp.mean(mix * cot, axis=-1, keepdims=True)
        gm = (scale * cot - mix * (scale * scale * scale * inner)).astype(BF16)
        q, k, v = get(queries, lanes), get(keys, lanes), get(values, lanes)
        qs = (q.astype(F32) * query_decay[:, lanes]).astype(BF16)
        gst = (mm(v, gm, NT) * grid_t[h]).astype(BF16)
        gs = (mm(gm, v, NT) * grid[h]).astype(BF16)
        sct = (mm(k, q, NT) * grid_t[h]).astype(BF16)
        put(value_grad, lanes, mm(sct, gm))
        put(key_grad, lanes, mm(gst, q))
        gq = []
        for s in range(count):
            pick = lambda x: slot_rows(x, s, size, count)
            gms = pick(gm)
            gq.append(mm(gms, held[step, s, h], NT))
            state_grad[s, h] = mm(pick(qs), gms, TN).astype(BF16)
        gq = mm(gs, k) + slot_back(gq, size) * query_decay[:, lanes]
        qp = get(query_pre, lanes).astype(F32)
        sg = jax.nn.sigmoid(qp)
        slope = sg + qp * sg * (1.0 - sg)
        put(query_grad, lanes, turn(gq, cosine[...], -sine[...]) * slope)


def rows_kernel(
    spots, query_grad, modulate_grad, key_grad, value_grad, w0, w1, kw0, kw1, vw0, vw1,
    near_out, far_out, wq, wm, wk, wv, sems
):
    @pl.when(pl.program_id(0) == 0)
    def _():
        each_block(
            spots,
            [
                (0, 0, w0, w1, wq, sems.at[0]), (0, 1, w0, w1, wm, sems.at[1]),
                (0, 0, kw0, kw1, wk, sems.at[2]), (2, 0, vw0, vw1, wv, sems.at[3]),
            ],
        )

    out = mm(get(query_grad), wq[...], NT) + mm(get(modulate_grad), wm[...], NT)
    out = out + mm(get(key_grad), wk[...], NT) + mm(get(value_grad), wv[...], NT)
    half = out.shape[0] // 2
    near_out[...] = out[:half].reshape(near_out.shape)
    far_out[...] = out[half:].astype(BF16).reshape(far_out.shape)


def key_back_kernel(
    spots, key_grad, value_grad, keys, values, key_pre, mask, cosine, sine, key_decay,
    g0, g1, g2, g3, key_out, value_out, held, state_sems
):
    @pl.when(pl.program_id(0) == 0)
    def _():
        load_states(spots, (g0, g1, g2, g3), held, state_sems)

    step = pl.program_id(0)
    _, count, size, width = keys.shape
    heads = held.shape[2]
    head = width // heads
    valid = get(mask).astype(F32)
    for h in range(heads):
        lanes = slice(h * head, (h + 1) * head)
        decay = key_decay[:, lanes]
        k, v = get(keys, lanes), get(values, lanes)
        scaled = (k.astype(F32) * decay).astype(BF16)
        pk = [mm(slot_rows(v, s, size, count), held[step, s, h], NT) for s in range(count)]
        pv = [mm(slot_rows(scaled, s, size, count), held[step, s, h]) for s in range(count)]
        gk = get(key_grad, lanes).astype(F32) + slot_back(pk, size) * decay
        gv = get(value_grad, lanes).astype(F32) + slot_back(pv, size)
        kp = get(key_pre, lanes).astype(F32)
        sg = jax.nn.sigmoid(kp)
        slope = sg + kp * sg * (1.0 - sg)
        put(key_out, lanes, turn(gk * valid, cosine[...], -sine[...]) * slope)
        put(value_out, lanes, gv * valid)


def hidden_kernel(
    spots, n0, n1, n2, n3, b0, b1, b2, b3, mask, gate_w, lift_w, down_w,
    inner_out, gate_out, lift_out, keep, send, branch_keep, branch_send
):
    flat = lambda refs: jnp.concatenate([r[...].reshape(-1, r.shape[-1]) for r in refs], axis=0)
    x, b = flat((n0, n1, n2, n3)), flat((b0, b1, b2, b3))
    valid = get(mask)[:, :1].astype(F32)
    gate, lift, down = gate_w[...], lift_w[...], down_w[...]
    parts = []
    for r in range(0, x.shape[0], 256):
        rows = slice(r, r + 256)
        gate_pre = mm(x[rows], gate, NT)
        lift_pre = mm(x[rows], lift, NT)
        inner_grad = mm(b[rows], down, NT) * valid[rows]
        q = jax.nn.sigmoid(gate_pre)
        act = gate_pre * q
        gate_grad = (inner_grad * lift_pre * (q + act * (1.0 - q))).astype(BF16)
        lift_grad = (inner_grad * act).astype(BF16)
        inner = (act * lift_pre).astype(BF16)
        total = (mm(gate_grad, gate) + mm(lift_grad, lift)).astype(BF16)
        parts.append((inner, gate_grad, lift_grad, total, mm(inner, down).astype(BF16)))
    inner, gate_grad, lift_grad, total, branch = (jnp.concatenate(p, axis=0) for p in zip(*parts))
    put(inner_out, slice(None), inner)
    put(gate_out, slice(None), gate_grad)
    put(lift_out, slice(None), lift_grad)
    half = total.shape[0] // 2
    for near, far, value in ((keep, send, total), (branch_keep, branch_send, branch)):
        near[...] = value[:half].reshape(near.shape)
        far[...] = value[half:].reshape(far.shape)


def outer_kernel(order, spots, near, far, *refs):
    count = (len(refs) - 4) // 1
    grads, (keep, send, whole, sems) = refs[:count], refs[count:]
    rows = near.shape[0] * near.shape[1]
    width = near.shape[2]
    tile = 256
    for c in range(0, width, tile):
        a = near[:, :, c : c + tile].reshape(rows, tile)
        b = far[:, :, c : c + tile].reshape(rows, tile)
        for k, g in enumerate(grads):
            g0 = g[0].reshape(rows, -1)
            g1 = g[1].reshape(rows, -1)
            whole[k, c : c + tile, :] = (mm(a, g0, TN) + mm(b, g1, TN)).astype(BF16)
    each_block(
        spots, [(order, k, keep, send, whole.at[k], sems.at[k]) for k in range(count)], out=True
    )


ANY = pl.BlockSpec(memory_space=pltpu.HBM)
VMEM = pl.BlockSpec(memory_space=pltpu.VMEM)


def run(kernel, name, spots, inputs, outputs, scratch, steps, flops):
    def spec(shape, kind):
        if kind == "any":
            return ANY
        if kind == "rows":
            size = shape[0] // steps
            return pl.BlockSpec((size, *shape[1:]), lambda i, _: (i,) + (0,) * (len(shape) - 1))
        if kind == "pair":
            size = shape[1] // steps
            return pl.BlockSpec(
                (shape[0], size, *shape[2:]), lambda i, _: (0, i) + (0,) * (len(shape) - 2)
            )
        return pl.BlockSpec(shape, lambda i, _: (0,) * len(shape))

    moved = sum(a.size * a.dtype.itemsize for a, _ in inputs)
    moved += sum(math.prod(s) * jnp.dtype(d).itemsize for s, d, _ in outputs)
    return pl.pallas_call(
        kernel,
        out_shape=[jax.ShapeDtypeStruct(s, d) for s, d, _ in outputs],
        grid_spec=pltpu.PrefetchScalarGridSpec(
            num_scalar_prefetch=1,
            grid=(steps,),
            in_specs=[spec(a.shape, kind) for a, kind in inputs],
            out_specs=[spec(s, kind) for s, _, kind in outputs],
            scratch_shapes=scratch,
        ),
        compiler_params=pltpu.CompilerParams(vmem_limit_bytes=40 * 2**20),
        cost_estimate=pl.CostEstimate(flops=int(flops * 2.4), bytes_accessed=int(moved * 2.4), transcendentals=0),
        name=name,
    )(spots, *[a for a, _ in inputs])


class Carry:
    def __init__(self, local, block_decay, reverse):
        self.local, self.reverse = local, reverse
        narrow_count = lax.axis_size("narrow")
        self.member = 2 * (lax.axis_index("wide") % 2) + lax.axis_index("narrow") // 2
        self.masks = [0, 2, narrow_count, narrow_count + 2]
        ranks = [self.member ^ k for k in range(4)]
        self.ranks = [3 - r if reverse else r for r in ranks]
        self.log_decay = jnp.log(block_decay)

    def power(self, e):
        return jnp.exp(e * self.log_decay)[None, :, None, None]

    def spread(self):
        share = self.local.shape[0] // 4
        parts = [
            lax.dynamic_slice_in_dim(self.local, (self.member ^ k) * share, share, 0)
            for k in range(4)
        ]
        self.got = [parts[0]] + [exchange(parts[k], self.masks[k]) for k in range(1, 4)]

    def along(self, between=lambda step, got: got):
        self.held = [h.astype(F32) for h in self.got]
        span = sum(self.power((3 - self.ranks[k]).astype(F32)) * self.held[k] for k in range(4))
        before, step = 0.0, 1
        while step < lax.axis_size("wide") // 2:
            got = between(step, shift_z(span.astype(BF16), step, self.reverse)).astype(F32)
            before = before + self.power(4.0 * (step - 1)) * got
            span = span + self.power(4.0 * step) * got
            step *= 2
        self.before = before

    def back(self):
        sent = []
        for k in range(4):
            state = self.power(self.ranks[k].astype(F32)) * self.before
            for j in range(4):
                gap = (self.ranks[k] - 1 - self.ranks[j]).astype(F32)
                scale = jnp.where(gap >= 0, self.power(jnp.maximum(gap, 0.0)), 0.0)
                state = state + scale * self.held[j]
            sent.append(state.astype(BF16))
        return [sent[0]] + [exchange(sent[k], self.masks[k]) for k in range(1, 4)]


def on_device(
    layer_input,
    query_weight,
    key_weight,
    value_weight,
    modulate_weight,
    output_weight,
    gate_matrix,
    lift_matrix,
    down_matrix,
    decay_factor,
    valid_lengths,
    output_cotangent,
):
    narrow_count, wide_count = lax.axis_size("narrow"), lax.axis_size("wide")
    wide_index, narrow_index = lax.axis_index("wide"), lax.axis_index("narrow")
    core, side = narrow_index % 2, narrow_index // 2
    slots, quarter, width = layer_input.shape
    block = 2 * quarter
    rows, cols = query_weight.shape
    heads = 2 * decay_factor.shape[0]
    head_size = cols // decay_factor.shape[0]
    x_mask = 2
    wide_masks = []
    bit = narrow_count
    while bit < narrow_count * wide_count:
        wide_masks.append(bit)
        bit *= 2
    y_mask, z_masks = wide_masks[0], wide_masks[:0:-1]
    order_yx = z_masks + [y_mask, x_mask]
    order_xy = z_masks + [x_mask, y_mask]
    order_v = [y_mask] + z_masks + [x_mask]
    members = 1 << len(order_yx)
    half = members // 2

    base = wide_index * (quarter * narrow_count) + side * block
    offsets = jnp.stack(
        [core * quarter + jnp.arange(quarter), (1 - core) * quarter + jnp.arange(quarter)]
    ).astype(jnp.int32)
    mask = ((base + offsets)[:, None, :] < valid_lengths[None, :, None]).astype(F32)
    mask_rows = mask[0][:, :, None]
    mask_wide = jnp.broadcast_to(mask[..., None], (2, slots, quarter, head_size)).astype(BF16)
    member = 2 * (wide_index % 2) + side
    spots = jnp.concatenate(
        [
            block_spots(order_xy)[None],
            block_spots(order_yx)[None],
            block_spots(order_v)[None],
            jnp.broadcast_to(member, (1, members, 2)).astype(jnp.int32),
        ]
    )

    def core_sum(near, far):
        return near + exchange(far, 1).astype(F32)

    other_decay = exchange(decay_factor, x_mask)
    decay = jnp.concatenate(
        [jnp.where(side == 0, decay_factor, other_decay), jnp.where(side == 0, other_decay, decay_factor)]
    )
    log_decay = jnp.log(decay)
    block_decay = jnp.exp(block * log_decay)
    steps = 4
    count = slots // steps

    def table(values):
        lanes = values.shape[-1]
        return jnp.broadcast_to(values[:, None], (2, count, quarter, lanes)).reshape(-1, lanes)

    half_head = head_size // 2
    frequency = jnp.exp(-math.log(10000.0) * jnp.arange(half_head, dtype=F32) / half_head)
    phase = (base + offsets).astype(F32)[..., None] * frequency
    cosine, sine = jnp.cos(phase), jnp.sin(phase)
    cosine = table(jnp.concatenate([cosine, cosine], axis=-1))
    sine = table(jnp.concatenate([-sine, sine], axis=-1))
    spot = offsets.astype(F32)
    log_lanes = jnp.repeat(log_decay, head_size)
    query_decay = table(jnp.exp((spot[..., None] + 1.0) * log_lanes))
    key_decay = table(jnp.exp((block - 1.0 - spot[..., None]) * log_lanes))
    flat = jnp.broadcast_to(spot[:, None], (2, count, quarter)).reshape(-1)
    slot_of = jnp.broadcast_to(jnp.arange(count)[None, :, None], (2, count, quarter)).reshape(-1)
    gap = flat[:, None] - flat[None, :]
    seen = (gap >= 0.0) & (slot_of[:, None] == slot_of[None, :])
    decay_grid = jnp.where(
        seen[None], jnp.exp(jnp.maximum(gap, 0.0)[None] * log_decay[:, None, None]), 0.0
    )
    decay_grid_t = jnp.swapaxes(decay_grid, 1, 2)

    def join(*parts):
        return jnp.concatenate(parts, axis=0)

    z_far, z_near = z_masks[:-1], z_masks[-1]
    swap = exchange

    def tie(*arrays):
        return lax.optimization_barrier(arrays)

    def far_open(x):
        for m in z_far[:-1]:
            x = join(x, swap(x, m))
        return x, swap(x, z_far[-1])

    key_w, value_w = key_weight[None, None], value_weight[None, None]
    dn = down_matrix.T[None]
    gl = jnp.stack([gate_matrix.T, lift_matrix.T])[None]
    qmo = jnp.stack([query_weight, modulate_weight, output_weight])[None]
    input_rows = layer_input.astype(F32)
    normed = simple_norm(input_rows).astype(BF16)
    cotangent = output_cotangent.astype(F32)
    cotangent_x = [swap(output_cotangent[: slots // 2], x_mask)]
    key_w, k_got = far_open(key_w)
    k_got, v_got = tie(k_got, swap(value_w, y_mask))
    key_w, value_w = join(key_w, k_got), join(value_w, v_got)
    value_w, v_got = far_open(value_w)
    k_got, v_got, dn_y, cotangent_x[0] = tie(
        swap(key_w, z_near), v_got, swap(dn, y_mask), cotangent_x[0]
    )
    key_w, value_w, dn = join(key_w, k_got), join(value_w, v_got), join(dn, dn_y)
    normed_pair = (normed, swap(normed, 1))
    k_got, v_got = tie(swap(key_w, x_mask), swap(value_w, z_near))
    key_w, value_w, qmo = join(key_w, k_got), join(value_w, v_got), tie(qmo, k_got)[0]
    qmo, q_got = far_open(qmo)
    k_got, v_got, q_got = tie(swap(key_w, y_mask), swap(value_w, x_mask), q_got)
    key_parts, value_parts = (key_w, k_got), (value_w, v_got)
    qmo = join(qmo, q_got)
    qmo_z = swap(qmo, z_near)
    inner_width = heads * head_size
    chip_shape = (2, slots, quarter, inner_width)
    row_shape = (slots, quarter, width)
    state_shape = (slots, heads, head_size, head_size)
    square_flops = 2 * 2 * slots * quarter * width * inner_width
    wide_scratch = pltpu.VMEM((width, inner_width), BF16)
    held_scratch = pltpu.VMEM((4, slots // 4, heads, head_size, head_size), BF16)
    dma = pltpu.SemaphoreType.DMA

    key_pre, keys, values, local_state = run(
        key_value_kernel, "key_value", spots,
        [
            (normed_pair[0], "rows"), (normed_pair[1], "rows"), (mask_wide, "pair"),
            (cosine, "whole"), (sine, "whole"), (key_decay, "whole"),
            (key_parts[0], "any"), (key_parts[1], "any"),
            (value_parts[0], "any"), (value_parts[1], "any"),
        ],
        [
            (chip_shape, BF16, "pair"), (chip_shape, BF16, "pair"), (chip_shape, BF16, "pair"),
            (state_shape, BF16, "rows"),
        ],
        [wide_scratch, wide_scratch, dma((2, members))],
        steps, 2 * square_flops,
    )
    local_state, qmo_z = tie(local_state, qmo_z)
    qmo = join(qmo, qmo_z)
    qm, out_w = qmo[:, :2], qmo[:, 2:]
    scan = Carry(local_state, block_decay, False)
    scan.spread()
    gl, gl_got = far_open(tie(gl, qmo_z)[0])
    scan.got[1], scan.got[2], scan.got[3], qm, out_w = tie(*scan.got[1:], qm, out_w)
    qm_x, o_y = swap(qm, x_mask), swap(out_w, y_mask)
    held = {}

    def forward_step(step, got):
        if step == 1:
            got, qx, oy, held["gl"] = tie(got, qm_x, o_y, gl_got)
            held["qm"], held["out"] = join(qm, qx), join(out_w, oy)
            held["gl"] = join(gl, held["gl"])
            held["more"] = [
                swap(held["qm"], y_mask), swap(held["out"], x_mask), swap(held["gl"], z_near),
                swap(tie(output_cotangent[slots // 2 :], oy)[0], x_mask),
            ]
        if step == 2:
            got, *held["more"] = tie(got, *held["more"])
        return got

    scan.along(forward_step)
    qm_y, o_x, gl_z, more_x = held["more"]
    cotangent_x.append(more_x)
    gl = join(held["gl"], gl_z)
    query_parts, output_parts = (held["qm"], qm_y), (held["out"], o_x)
    dn, dn_got = far_open(tie(dn, gl_z)[0])
    state_parts = scan.back()
    query_pre, queries, modulate, intra = run(
        query_kernel, "query", spots,
        [
            (normed_pair[0], "rows"), (normed_pair[1], "rows"), (mask_wide, "pair"),
            (cosine, "whole"), (sine, "whole"), (decay_grid, "whole"),
            (keys, "pair"), (values, "pair"), (query_parts[0], "any"), (query_parts[1], "any"),
        ],
        [
            (chip_shape, BF16, "pair"), (chip_shape, BF16, "pair"), (chip_shape, BF16, "pair"),
            (chip_shape, BF16, "pair"),
        ],
        [wide_scratch, wide_scratch, dma((2, members))],
        steps, 2 * square_flops,
    )
    *state_parts, queries, dn_got = tie(*state_parts, queries, dn_got)
    dn = join(dn, dn_got)
    state_inputs = [(p, "any") for p in state_parts]
    output_inputs = [(p, "any") for p in output_parts]
    mixed, gated, near_att, far_att = run(
        mixed_kernel, "mixed", spots,
        [
            (queries, "pair"), (intra, "pair"), (modulate, "pair"), (query_decay, "whole"),
            *state_inputs, *output_inputs,
        ],
        [
            (chip_shape, BF16, "pair"), (chip_shape, BF16, "pair"), (row_shape, F32, "rows"),
            (row_shape, BF16, "rows"),
        ],
        [wide_scratch, held_scratch, dma((members,)), dma((4,))],
        steps, square_flops,
    )
    middle = input_rows + core_sum(near_att, far_att)
    two = simple_norm(middle).astype(BF16)
    two_x, gl_y = tie(swap(two, x_mask), swap(gl, y_mask))
    dn_z = swap(dn, z_near)

    def quarters(mine, got_x):
        return [mine, got_x, swap(mine, 1), swap(got_x, 1)]

    def core_part(keep, send):
        got = swap(send, 1)
        return fold(keep[0], got[0], F32), fold(keep[1], got[1])

    two_pieces = quarters(two, two_x)
    normed_two = jnp.stack(two_pieces)
    row_starts = (narrow_index ^ jnp.array([0, x_mask, 1, 1 + x_mask], jnp.int32)) * quarter
    row_spots = wide_index * (quarter * narrow_count) + row_starts[:, None] + jnp.arange(quarter)
    row_mask = (row_spots[:, None, :] < valid_lengths[None, :, None]).astype(F32)[..., None]
    branch_pieces = quarters(output_cotangent, jnp.concatenate(cotangent_x))
    row_mask_wide = jnp.broadcast_to(row_mask, (4, slots, quarter, head_size)).astype(BF16)
    gate_t = join(gl[:, 0], gl_y[:, 0]).reshape(-1, width)
    lift_t = join(gl[:, 1], gl_y[:, 1]).reshape(-1, width)
    bulk = half // 2
    down_t = jnp.swapaxes(join(dn, dn_z).reshape(bulk, 2, -1, width), 0, 1).reshape(-1, width)

    def outer(a, b):
        return jnp.einsum("pblf,pbld->fd", a, b, preferred_element_type=F32).astype(BF16)

    hidden_shape = (4, slots, quarter, gate_t.shape[0])
    sum_shape = (2, slots, quarter, width)
    hidden_flops = 2 * 4 * slots * quarter * width * gate_t.shape[0]
    inner, gate_grad, lift_grad, row_keep, row_send, branch_keep, branch_send = run(
        hidden_kernel, "hidden", spots,
        [
            *[(p, "rows") for p in two_pieces], *[(p, "rows") for p in branch_pieces],
            (row_mask_wide, "pair"), (gate_t, "whole"),
            (lift_t, "whole"), (down_t, "whole"),
        ],
        [(hidden_shape, BF16, "pair")] * 3 + [(sum_shape, BF16, "pair")] * 4,
        [], steps, 6 * hidden_flops,
    )
    row_mine, row_send = core_part(row_keep, row_send)
    row_got = swap(row_send, x_mask)
    branch_rows = jnp.stack(branch_pieces).astype(F32)
    branch_rows = (tie(row_mask, row_send)[0] * branch_rows).astype(BF16)
    gate_grad, lift_grad, inner, row_send = tie(gate_grad, lift_grad, inner, row_send)
    gate_g = outer(gate_grad, normed_two).reshape(2, bulk, -1, width)
    gate_y = swap(gate_g[1], y_mask)
    lift_grad, inner, gate_g = tie(lift_grad, inner, gate_g)
    lift_g = outer(lift_grad, normed_two).reshape(2, bulk, -1, width)
    down_g = outer(inner, branch_rows).reshape(2, 2, bulk // 2, -1, width)
    branch_mine, branch_send = core_part(branch_keep, branch_send)
    row_got, gate_y, lift_g, down_z_send, branch_send = tie(
        row_got, gate_y, lift_g, down_g[:, 1], branch_send
    )
    lift_y = swap(lift_g[1], y_mask)
    branch_got = swap(branch_send, x_mask)
    down_z = swap(down_z_send, z_near)
    middle_grad = cotangent + norm_backward(middle, row_mine + row_got.astype(F32))

    attended_grad = middle_grad.astype(BF16)
    attended_pair = (attended_grad, exchange(attended_grad, 1))
    modulate_grad, query_grad, key_grad, value_grad, state_grad = run(
        mixed_back_kernel, "mixed_back", spots,
        [
            (attended_pair[0], "rows"), (attended_pair[1], "rows"), (mixed, "pair"),
            (modulate, "pair"), (queries, "pair"), (query_pre, "pair"), (keys, "pair"),
            (values, "pair"), (mask_wide, "pair"), (cosine, "whole"), (sine, "whole"),
            (query_decay, "whole"), (decay_grid, "whole"), (decay_grid_t, "whole"),
            *state_inputs, *output_inputs,
        ],
        [
            (chip_shape, BF16, "pair"), (chip_shape, BF16, "pair"), (chip_shape, BF16, "pair"),
            (chip_shape, BF16, "pair"), (state_shape, BF16, "rows"),
        ],
        [wide_scratch, held_scratch, dma((members,)), dma((4,))],
        steps, 2 * square_flops,
    )
    state_grad, lift_y, gated = tie(state_grad, lift_y, gated)
    near = bulk // 2
    scan = Carry(state_grad, block_decay, True)
    scan.spread()

    def square(name, order, a, *grads):
        shape = (half, len(grads), rows, cols)
        return run(
            functools.partial(outer_kernel, order), name, spots,
            [(a[0], "whole"), (a[1], "whole"), *[(g, "whole") for g in grads]],
            [(shape, BF16, "any"), (shape, BF16, "any")],
            [pltpu.VMEM((len(grads), width, inner_width), BF16), dma((len(grads), members))],
            1, len(grads) * square_flops,
        )

    output_keep, output_send = square("output_outer", 1, attended_pair, gated)
    query_keep, query_send = square("query_outer", 0, normed_pair, query_grad, modulate_grad)
    *scan.got, down_z, branch_got, query_keep, query_send, output_keep, output_send = tie(
        *scan.got, down_z, branch_got, query_keep, query_send, output_keep, output_send
    )
    layer_output = (middle + mask_rows * (branch_mine + branch_got.astype(F32))).astype(BF16)
    down_g = jnp.moveaxis(fold(down_g[:, 0], down_z), 1, 0)
    for m in z_far[:0:-1]:
        size = down_g.shape[0] // 2
        down_g = fold(down_g[:size], swap(down_g[size:], m))
    gl_g = jnp.stack([fold(gate_g[0], gate_y), fold(lift_g[0], lift_y)], axis=1)

    query_y, output_x = swap(query_send[:, :1], y_mask), swap(output_send, x_mask)

    def backward_step(step, got):
        if step == 1:
            got, held["y"], mod_send = tie(got, query_y, query_send[:, 1:])
            held["more"] = swap(mod_send, y_mask)
        if step == 2:
            got, held["more"], held["x"] = tie(got, held["more"], output_x)
        return got

    scan.along(backward_step)
    query_y = jnp.concatenate([held["y"], held["more"]], axis=1)
    scan.before, down_g, gl_g = tie(scan.before, down_g, gl_g)
    down_far = swap(down_g[1], z_far[0])
    gl_z = swap(gl_g[near:], z_near)
    later_parts = list(tie(*scan.back()))
    query_keep, output_keep = tie(query_keep, output_keep, *later_parts)[:2]
    query_g, output_g = fold(query_keep, query_y), fold(output_keep, held["x"])
    quad = half // 2
    query_x, output_y = swap(query_g[quad:], x_mask), swap(output_g[quad:], y_mask)
    later_inputs = [(p, "any") for p in later_parts]
    quad = half // 2
    def far_folds(x):
        for m in reversed(z_far):
            size = x.shape[0] // 2
            x = (fold if size > 1 else final)(x[:size], swap(x[size:], m))
        return x

    key_out, value_out = run(
        key_back_kernel, "key_back", spots,
        [
            (key_grad, "pair"), (value_grad, "pair"), (keys, "pair"), (values, "pair"),
            (key_pre, "pair"), (mask_wide, "pair"), (cosine, "whole"), (sine, "whole"),
            (key_decay, "whole"), *later_inputs,
        ],
        [(chip_shape, BF16, "pair"), (chip_shape, BF16, "pair")],
        [held_scratch, dma((4,))],
        steps, square_flops // 2,
    )
    key_keep, key_send = square("key_outer", 0, normed_pair, key_out)
    value_keep, value_send = square("value_outer", 1, normed_pair, value_out)
    key_send, value_send, gl_z, down_far, query_x, output_y = tie(
        key_send, value_send, gl_z, down_far, query_x, output_y
    )
    down_g = fold(down_g[0], down_far)
    gl_g = fold(gl_g[:near], gl_z)
    for m in z_far[:0:-1]:
        size = gl_g.shape[0] // 2
        gl_g = fold(gl_g[:size], swap(gl_g[size:], m))
    gl_far = swap(gl_g[1], z_far[0])
    key_y, value_x = swap(key_send, y_mask), swap(value_send, x_mask)
    key_out, value_out = tie(key_out, value_out, key_send, value_send)[:2]
    near_rows, far_rows = run(
        rows_kernel, "rows", spots,
        [
            (query_grad, "pair"), (modulate_grad, "pair"), (key_out, "pair"),
            (value_out, "pair"), (query_parts[0], "any"), (query_parts[1], "any"),
            (key_parts[0], "any"), (key_parts[1], "any"),
            (value_parts[0], "any"), (value_parts[1], "any"),
        ],
        [(row_shape, F32, "rows"), (row_shape, BF16, "rows")],
        [wide_scratch] * 4 + [dma((4, members))],
        steps, 4 * square_flops,
    )
    qmo_g = jnp.concatenate(
        [fold(query_g[:quad], query_x), fold(output_g[:quad], output_y)], axis=1
    )
    qmo_z = swap(qmo_g[near:], z_near)
    key_y, value_x, near_rows = tie(key_y, value_x, near_rows)
    down_y = swap(down_g[1], y_mask)
    key_g, value_g = fold(key_keep, key_y), fold(value_keep, value_x)
    key_x, value_y = swap(key_g[quad:], x_mask), swap(value_g[quad:], y_mask)
    key_x, value_y, down_y, qmo_z, gl_far = tie(key_x, value_y, down_y, qmo_z, gl_far)
    gate_lift = final(gl_g[0], gl_far)
    kv_g = jnp.concatenate([fold(key_g[:quad], key_x), fold(value_g[:quad], value_y)], axis=1)
    kv_z = swap(kv_g[near:], z_near)
    qmo_g = far_folds(fold(qmo_g[:near], qmo_z))[0]
    key_gradient, value_gradient = far_folds(fold(kv_g[:near], kv_z))[0]
    query_gradient, modulate_gradient, output_gradient = qmo_g
    down_gradient = final(down_g[0], down_y).T
    gate_gradient, lift_gradient = gate_lift[0].T, gate_lift[1].T
    input_gradient = middle_grad + norm_backward(input_rows, core_sum(near_rows, far_rows))
    return (
        layer_output,
        input_gradient,
        query_gradient,
        key_gradient,
        value_gradient,
        modulate_gradient,
        output_gradient,
        gate_gradient,
        lift_gradient,
        down_gradient,
    )


def solution(mesh):
    placed = (
        P(None, ("wide", "narrow"), None),
        P("wide", "narrow"),
        P("wide", "narrow"),
        P("wide", "narrow"),
        P("wide", "narrow"),
        P("wide", "narrow"),
        P(None, ("wide", "narrow")),
        P(None, ("wide", "narrow")),
        P(None, ("wide", "narrow")),
        P("narrow"),
        P(),
        P(None, ("wide", "narrow"), None),
    )
    return jax.shard_map(
        on_device,
        mesh=mesh,
        in_specs=placed,
        out_specs=(
            P(None, ("wide", "narrow"), None),
            P(None, ("wide", "narrow"), None),
            P("wide", "narrow"),
            P("wide", "narrow"),
            P("wide", "narrow"),
            P("wide", "narrow"),
            P("wide", "narrow"),
            P(None, ("wide", "narrow")),
            P(None, ("wide", "narrow")),
            P(None, ("wide", "narrow")),
        ),
        check_vma=False,
    )
```

```python
import functools
import math

import jax
import jax.numpy as jnp
from jax import lax
from jax.experimental import pallas as pl
from jax.experimental.pallas import tpu as pltpu
from jax.sharding import PartitionSpec as P

EPS = 1e-06
AXES = ("wide", "narrow")
BF16 = jnp.bfloat16
F32 = jnp.float32


def simple_norm(values):
    return values * lax.rsqrt(jnp.mean(values * values, axis=-1, keepdims=True) + EPS)


def norm_backward(values, cotangent):
    scale = lax.rsqrt(jnp.mean(values * values, axis=-1, keepdims=True) + EPS)
    inner = jnp.mean(values * cotangent, axis=-1, keepdims=True)
    return scale * cotangent - values * (scale * scale * scale * inner)


def apply_swish(values):
    return values * jax.nn.sigmoid(values)


def swish_slope(values):
    sigmoid_value = jax.nn.sigmoid(values)
    return sigmoid_value + values * sigmoid_value * (1.0 - sigmoid_value)


def exchange(x, mask):
    count = lax.axis_size(AXES)
    return lax.ppermute(x, AXES, [(i, i ^ mask) for i in range(count)])


def after(x, *others):
    return lax.optimization_barrier((x, *others))[0]


def shift_z(x, step, reverse):
    count, unit = lax.axis_size(AXES), 2 * lax.axis_size("narrow")
    pairs = [(i, i + step * unit) for i in range(count - step * unit)]
    if reverse:
        pairs = [(b, a) for a, b in pairs]
    return lax.ppermute(x, AXES, pairs)


def gather_plane(x, masks):
    return gather_more(x[None], masks)


def gather_more(held, masks):
    for mask in masks:
        held = jnp.concatenate([held, exchange(held, mask)], axis=0)
    return held


def gather_hidden(x, masks, swapped):
    held = gather_plane(x, masks)
    if swapped:
        held = jnp.swapaxes(held.reshape(2, 2, -1, *x.shape), 0, 1)
    return held.reshape(-1, x.shape[-1])


def scatter_plane(x, masks):
    for mask in reversed(masks):
        half = x.shape[0] // 2
        got = exchange(x[half:], mask)
        total = x[:half].astype(F32) + got.astype(F32)
        x = total.astype(BF16) if half > 1 else total
    return x[0]


def fold(mine, got, dtype=BF16):
    return (mine.astype(F32) + got.astype(F32)).astype(dtype)


def final(mine, got):
    return fold(mine, got, F32)


def relative(masks, index):
    out = 0
    for k, mask in enumerate(masks):
        out ^= mask * ((index >> k) & 1)
    return out


NT = (((1,), (1,)), ((), ()))
NN = (((1,), (0,)), ((), ()))
TN = (((0,), (0,)), ((), ()))


def mm(a, b, dims=NN):
    return lax.dot_general(a, b, dims, preferred_element_type=F32)


def turn(v, cosine, sine):
    return v * cosine + pltpu.roll(v, v.shape[-1] // 2, 1) * sine


def block_spots(masks):
    own = lax.axis_index(AXES)
    narrow_count = lax.axis_size("narrow")
    ids = jnp.array([relative(masks, i) for i in range(1 << len(masks))], jnp.int32) ^ own
    return jnp.stack([ids // narrow_count, (ids % narrow_count) // 2], axis=1)


def block_copy(spots, which, i, rows, cols, whole, part, sem, out):
    at = (
        pl.ds(pl.multiple_of(spots[which, i, 0] * rows, rows), rows),
        pl.ds(pl.multiple_of(spots[which, i, 1] * cols, cols), cols),
    )
    if out:
        return pltpu.make_async_copy(whole.at[at], part, sem)
    return pltpu.make_async_copy(part, whole.at[at], sem)


def each_block(spots, jobs, out=False):
    def go(method):
        for order, k, near, far, whole, sems in jobs:
            half, _, rows, cols = near.shape

            def step(i, _):
                for at, part in enumerate((near, far)):
                    copy = block_copy(
                        spots, order, i + at * half, rows, cols, whole, part.at[i, k],
                        sems.at[i + at * half], out,
                    )
                    getattr(copy, method)()
                return 0

            lax.fori_loop(0, half, step, 0)

    go("start")
    go("wait")


def both(near, far):
    rows = near.shape[0] * near.shape[1]
    return jnp.concatenate([near.reshape(rows, -1), far.reshape(rows, -1)], axis=0)


def slot_rows(x, s, size, count):
    return jnp.concatenate(
        [x[s * size : (s + 1) * size], x[(count + s) * size : (count + s + 1) * size]], axis=0
    )


def slot_back(parts, size):
    return jnp.concatenate([p[:size] for p in parts] + [p[size:] for p in parts], axis=0)


def put(ref, lanes, value):
    two, count, size, _ = ref.shape
    ref[:, :, :, lanes] = value.reshape(two, count, size, -1).astype(ref.dtype)


def get(ref, lanes=slice(None)):
    two, count, size, width = ref.shape
    x = ref[:, :, :, lanes]
    return x.reshape(two * count * size, x.shape[-1])


def key_value_kernel(
    spots, near, far, mask, cosine, sine, key_decay, kw0, kw1, vw0, vw1,
    key_pre, keys, values, state, wk, wv, sems
):
    @pl.when(pl.program_id(0) == 0)
    def _():
        each_block(spots, [(0, 0, kw0, kw1, wk, sems.at[0]), (2, 0, vw0, vw1, wv, sems.at[1])])

    count, size = near.shape[0], near.shape[1]
    x = both(near[...], far[...])
    valid = get(mask).astype(F32)
    head = cosine.shape[-1]
    pre = mm(x, wk[...])
    val_pre = mm(x, wv[...])
    for h in range(pre.shape[-1] // head):
        lanes = slice(h * head, (h + 1) * head)
        kp = pre[:, lanes]
        put(key_pre, lanes, kp)
        key = (valid * turn(kp * jax.nn.sigmoid(kp), cosine[...], sine[...])).astype(BF16)
        val = (valid * val_pre[:, lanes]).astype(BF16)
        put(keys, lanes, key)
        put(values, lanes, val)
        scaled = (key.astype(F32) * key_decay[:, lanes]).astype(BF16)
        for s in range(count):
            state[s, h] = mm(
                slot_rows(scaled, s, size, count), slot_rows(val, s, size, count), TN
            ).astype(BF16)


def query_kernel(
    spots, near, far, mask, cosine, sine, grid, keys, values, w0, w1,
    query_pre, queries, modulate, intra, wq, wm, sems
):
    @pl.when(pl.program_id(0) == 0)
    def _():
        each_block(spots, [(0, 0, w0, w1, wq, sems.at[0]), (0, 1, w0, w1, wm, sems.at[1])])

    count, size = near.shape[0], near.shape[1]
    x = both(near[...], far[...])
    valid = get(mask).astype(F32)
    head = cosine.shape[-1]
    pre = mm(x, wq[...])
    mod = mm(x, wm[...])
    for h in range(pre.shape[-1] // head):
        lanes = slice(h * head, (h + 1) * head)
        qp = pre[:, lanes]
        put(query_pre, lanes, qp)
        put(modulate, lanes, mod[:, lanes] * valid)
        q = turn(qp * jax.nn.sigmoid(qp), cosine[...], sine[...]).astype(BF16)
        put(queries, lanes, q)
        k, v = get(keys, lanes), get(values, lanes)
        scores = (mm(q, k, NT) * grid[h]).astype(BF16)
        put(intra, lanes, mm(scores, v))


def load_states(spots, pieces, held, sems):
    member = spots[3, 0, 0]
    copies = [
        pltpu.make_async_copy(p, held.at[member ^ k], sems.at[k]) for k, p in enumerate(pieces)
    ]
    for c in copies:
        c.start()
    for c in copies:
        c.wait()


def mixed_kernel(
    spots, queries, intra, modulate, query_decay, s0, s1, s2, s3, w0, w1,
    mixed, gated, near_out, far_out, wo, held, sems, state_sems
):
    @pl.when(pl.program_id(0) == 0)
    def _():
        load_states(spots, (s0, s1, s2, s3), held, state_sems)
        each_block(spots, [(1, 0, w0, w1, wo, sems)])

    step = pl.program_id(0)
    _, count, size, width = queries.shape
    heads = held.shape[2]
    head = width // heads
    gates = []
    for h in range(heads):
        lanes = slice(h * head, (h + 1) * head)
        q = (get(queries, lanes).astype(F32) * query_decay[:, lanes]).astype(BF16)
        parts = [mm(slot_rows(q, s, size, count), held[step, s, h]) for s in range(count)]
        mix = get(intra, lanes).astype(F32) + slot_back(parts, size)
        put(mixed, lanes, mix)
        scale = lax.rsqrt(jnp.mean(mix * mix, axis=-1, keepdims=True) + EPS)
        gates.append((mix * scale * get(modulate, lanes).astype(F32)).astype(BF16))
    gate = jnp.concatenate(gates, axis=1)
    put(gated, slice(None), gate)
    out = mm(gate, wo[...], NT)
    near_out[...] = out[: count * size].reshape(near_out.shape)
    far_out[...] = out[count * size :].astype(BF16).reshape(far_out.shape)


def mixed_back_kernel(
    spots, near, far, mixed, modulate, queries, query_pre, keys, values, mask, cosine, sine,
    query_decay, grid, grid_t, s0, s1, s2, s3, w0, w1,
    modulate_grad, query_grad, key_grad, value_grad, state_grad, wo, held, sems, state_sems
):
    @pl.when(pl.program_id(0) == 0)
    def _():
        load_states(spots, (s0, s1, s2, s3), held, state_sems)
        each_block(spots, [(1, 0, w0, w1, wo, sems)])

    step = pl.program_id(0)
    _, count, size, width = queries.shape
    heads = held.shape[2]
    head = width // heads
    gate_grad = mm(both(near[...], far[...]), wo[...])
    valid = get(mask).astype(F32)
    for h in range(heads):
        lanes = slice(h * head, (h + 1) * head)
        mix = get(mixed, lanes).astype(F32)
        scale = lax.rsqrt(jnp.mean(mix * mix, axis=-1, keepdims=True) + EPS)
        gg = gate_grad[:, lanes]
        put(modulate_grad, lanes, gg * valid * (mix * scale))
        cot = gg * get(modulate, lanes).astype(F32)
        inner = jnp.mean(mix * cot, axis=-1, keepdims=True)
        gm = (scale * cot - mix * (scale * scale * scale * inner)).astype(BF16)
        q, k, v = get(queries, lanes), get(keys, lanes), get(values, lanes)
        qs = (q.astype(F32) * query_decay[:, lanes]).astype(BF16)
        gst = (mm(v, gm, NT) * grid_t[h]).astype(BF16)
        gs = (mm(gm, v, NT) * grid[h]).astype(BF16)
        sct = (mm(k, q, NT) * grid_t[h]).astype(BF16)
        put(value_grad, lanes, mm(sct, gm))
        put(key_grad, lanes, mm(gst, q))
        gq = []
        for s in range(count):
            pick = lambda x: slot_rows(x, s, size, count)
            gms = pick(gm)
            gq.append(mm(gms, held[step, s, h], NT))
            state_grad[s, h] = mm(pick(qs), gms, TN).astype(BF16)
        gq = mm(gs, k) + slot_back(gq, size) * query_decay[:, lanes]
        qp = get(query_pre, lanes).astype(F32)
        sg = jax.nn.sigmoid(qp)
        slope = sg + qp * sg * (1.0 - sg)
        put(query_grad, lanes, turn(gq, cosine[...], -sine[...]) * slope)


def rows_kernel(
    spots, query_grad, modulate_grad, key_grad, value_grad, w0, w1, kw0, kw1, vw0, vw1,
    near_out, far_out, wq, wm, wk, wv, sems
):
    @pl.when(pl.program_id(0) == 0)
    def _():
        each_block(
            spots,
            [
                (0, 0, w0, w1, wq, sems.at[0]), (0, 1, w0, w1, wm, sems.at[1]),
                (0, 0, kw0, kw1, wk, sems.at[2]), (2, 0, vw0, vw1, wv, sems.at[3]),
            ],
        )

    out = mm(get(query_grad), wq[...], NT) + mm(get(modulate_grad), wm[...], NT)
    out = out + mm(get(key_grad), wk[...], NT) + mm(get(value_grad), wv[...], NT)
    half = out.shape[0] // 2
    near_out[...] = out[:half].reshape(near_out.shape)
    far_out[...] = out[half:].astype(BF16).reshape(far_out.shape)


def key_back_kernel(
    spots, key_grad, value_grad, keys, values, key_pre, mask, cosine, sine, key_decay,
    g0, g1, g2, g3, key_out, value_out, held, state_sems
):
    @pl.when(pl.program_id(0) == 0)
    def _():
        load_states(spots, (g0, g1, g2, g3), held, state_sems)

    step = pl.program_id(0)
    _, count, size, width = keys.shape
    heads = held.shape[2]
    head = width // heads
    valid = get(mask).astype(F32)
    for h in range(heads):
        lanes = slice(h * head, (h + 1) * head)
        decay = key_decay[:, lanes]
        k, v = get(keys, lanes), get(values, lanes)
        scaled = (k.astype(F32) * decay).astype(BF16)
        pk = [mm(slot_rows(v, s, size, count), held[step, s, h], NT) for s in range(count)]
        pv = [mm(slot_rows(scaled, s, size, count), held[step, s, h]) for s in range(count)]
        gk = get(key_grad, lanes).astype(F32) + slot_back(pk, size) * decay
        gv = get(value_grad, lanes).astype(F32) + slot_back(pv, size)
        kp = get(key_pre, lanes).astype(F32)
        sg = jax.nn.sigmoid(kp)
        slope = sg + kp * sg * (1.0 - sg)
        put(key_out, lanes, turn(gk * valid, cosine[...], -sine[...]) * slope)
        put(value_out, lanes, gv * valid)


def hidden_kernel(
    spots, n0, n1, n2, n3, b0, b1, b2, b3, mask, gate_w, lift_w, down_w,
    inner_out, gate_out, lift_out, keep, send, branch_keep, branch_send
):
    flat = lambda refs: jnp.concatenate([r[...].reshape(-1, r.shape[-1]) for r in refs], axis=0)
    x, b = flat((n0, n1, n2, n3)), flat((b0, b1, b2, b3))
    valid = get(mask)[:, :1].astype(F32)
    gate, lift, down = gate_w[...], lift_w[...], down_w[...]
    parts = []
    for r in range(0, x.shape[0], 256):
        rows = slice(r, r + 256)
        gate_pre = mm(x[rows], gate, NT)
        lift_pre = mm(x[rows], lift, NT)
        inner_grad = mm(b[rows], down, NT) * valid[rows]
        q = jax.nn.sigmoid(gate_pre)
        act = gate_pre * q
        gate_grad = (inner_grad * lift_pre * (q + act * (1.0 - q))).astype(BF16)
        lift_grad = (inner_grad * act).astype(BF16)
        inner = (act * lift_pre).astype(BF16)
        total = (mm(gate_grad, gate) + mm(lift_grad, lift)).astype(BF16)
        parts.append((inner, gate_grad, lift_grad, total, mm(inner, down).astype(BF16)))
    inner, gate_grad, lift_grad, total, branch = (jnp.concatenate(p, axis=0) for p in zip(*parts))
    put(inner_out, slice(None), inner)
    put(gate_out, slice(None), gate_grad)
    put(lift_out, slice(None), lift_grad)
    half = total.shape[0] // 2
    for near, far, value in ((keep, send, total), (branch_keep, branch_send, branch)):
        near[...] = value[:half].reshape(near.shape)
        far[...] = value[half:].reshape(far.shape)


def outer_kernel(order, spots, near, far, *refs):
    count = (len(refs) - 4) // 1
    grads, (keep, send, whole, sems) = refs[:count], refs[count:]
    rows = near.shape[0] * near.shape[1]
    width = near.shape[2]
    tile = 256
    for c in range(0, width, tile):
        a = near[:, :, c : c + tile].reshape(rows, tile)
        b = far[:, :, c : c + tile].reshape(rows, tile)
        for k, g in enumerate(grads):
            g0 = g[0].reshape(rows, -1)
            g1 = g[1].reshape(rows, -1)
            whole[k, c : c + tile, :] = (mm(a, g0, TN) + mm(b, g1, TN)).astype(BF16)
    each_block(
        spots, [(order, k, keep, send, whole.at[k], sems.at[k]) for k in range(count)], out=True
    )


ANY = pl.BlockSpec(memory_space=pltpu.HBM)
VMEM = pl.BlockSpec(memory_space=pltpu.VMEM)


def run(kernel, name, spots, inputs, outputs, scratch, steps, flops):
    def spec(shape, kind):
        if kind == "any":
            return ANY
        if kind == "rows":
            size = shape[0] // steps
            return pl.BlockSpec((size, *shape[1:]), lambda i, _: (i,) + (0,) * (len(shape) - 1))
        if kind == "pair":
            size = shape[1] // steps
            return pl.BlockSpec(
                (shape[0], size, *shape[2:]), lambda i, _: (0, i) + (0,) * (len(shape) - 2)
            )
        return pl.BlockSpec(shape, lambda i, _: (0,) * len(shape))

    moved = sum(a.size * a.dtype.itemsize for a, _ in inputs)
    moved += sum(math.prod(s) * jnp.dtype(d).itemsize for s, d, _ in outputs)
    return pl.pallas_call(
        kernel,
        out_shape=[jax.ShapeDtypeStruct(s, d) for s, d, _ in outputs],
        grid_spec=pltpu.PrefetchScalarGridSpec(
            num_scalar_prefetch=1,
            grid=(steps,),
            in_specs=[spec(a.shape, kind) for a, kind in inputs],
            out_specs=[spec(s, kind) for s, _, kind in outputs],
            scratch_shapes=scratch,
        ),
        compiler_params=pltpu.CompilerParams(vmem_limit_bytes=(48 if name == "mixed_back" else 40) * 2**20),
        cost_estimate=pl.CostEstimate(flops=int(flops * 2.4), bytes_accessed=int(moved * 2.4), transcendentals=0),
        name=name,
    )(spots, *[a for a, _ in inputs])


class Carry:
    def __init__(self, local, block_decay, reverse):
        self.local, self.reverse = local, reverse
        narrow_count = lax.axis_size("narrow")
        self.member = 2 * (lax.axis_index("wide") % 2) + lax.axis_index("narrow") // 2
        self.masks = [0, 2, narrow_count, narrow_count + 2]
        ranks = [self.member ^ k for k in range(4)]
        self.ranks = [3 - r if reverse else r for r in ranks]
        self.log_decay = jnp.log(block_decay)

    def power(self, e):
        return jnp.exp(e * self.log_decay)[None, :, None, None]

    def spread(self):
        share = self.local.shape[0] // 4
        parts = [
            lax.dynamic_slice_in_dim(self.local, (self.member ^ k) * share, share, 0)
            for k in range(4)
        ]
        self.got = [parts[0]] + [exchange(parts[k], self.masks[k]) for k in range(1, 4)]

    def along(self, between=lambda step, got: got):
        self.held = [h.astype(F32) for h in self.got]
        span = sum(self.power((3 - self.ranks[k]).astype(F32)) * self.held[k] for k in range(4))
        before, step = 0.0, 1
        while step < lax.axis_size("wide") // 2:
            got = between(step, shift_z(span.astype(BF16), step, self.reverse)).astype(F32)
            before = before + self.power(4.0 * (step - 1)) * got
            span = span + self.power(4.0 * step) * got
            step *= 2
        self.before = before

    def back(self):
        sent = []
        for k in range(4):
            state = self.power(self.ranks[k].astype(F32)) * self.before
            for j in range(4):
                gap = (self.ranks[k] - 1 - self.ranks[j]).astype(F32)
                scale = jnp.where(gap >= 0, self.power(jnp.maximum(gap, 0.0)), 0.0)
                state = state + scale * self.held[j]
            sent.append(state.astype(BF16))
        return [sent[0]] + [exchange(sent[k], self.masks[k]) for k in range(1, 4)]


def on_device(
    layer_input,
    query_weight,
    key_weight,
    value_weight,
    modulate_weight,
    output_weight,
    gate_matrix,
    lift_matrix,
    down_matrix,
    decay_factor,
    valid_lengths,
    output_cotangent,
):
    narrow_count, wide_count = lax.axis_size("narrow"), lax.axis_size("wide")
    wide_index, narrow_index = lax.axis_index("wide"), lax.axis_index("narrow")
    core, side = narrow_index % 2, narrow_index // 2
    slots, quarter, width = layer_input.shape
    block = 2 * quarter
    rows, cols = query_weight.shape
    heads = 2 * decay_factor.shape[0]
    head_size = cols // decay_factor.shape[0]
    x_mask = 2
    wide_masks = []
    bit = narrow_count
    while bit < narrow_count * wide_count:
        wide_masks.append(bit)
        bit *= 2
    y_mask, z_masks = wide_masks[0], wide_masks[:0:-1]
    order_yx = z_masks + [y_mask, x_mask]
    order_xy = z_masks + [x_mask, y_mask]
    order_v = [y_mask] + z_masks + [x_mask]
    members = 1 << len(order_yx)
    half = members // 2

    base = wide_index * (quarter * narrow_count) + side * block
    offsets = jnp.stack(
        [core * quarter + jnp.arange(quarter), (1 - core) * quarter + jnp.arange(quarter)]
    ).astype(jnp.int32)
    mask = ((base + offsets)[:, None, :] < valid_lengths[None, :, None]).astype(F32)
    mask_rows = mask[0][:, :, None]
    mask_wide = jnp.broadcast_to(mask[..., None], (2, slots, quarter, head_size)).astype(BF16)
    member = 2 * (wide_index % 2) + side
    spots = jnp.concatenate(
        [
            block_spots(order_xy)[None],
            block_spots(order_yx)[None],
            block_spots(order_v)[None],
            jnp.broadcast_to(member, (1, members, 2)).astype(jnp.int32),
        ]
    )

    def core_sum(near, far):
        return near + exchange(far, 1).astype(F32)

    other_decay = exchange(decay_factor, x_mask)
    decay = jnp.concatenate(
        [jnp.where(side == 0, decay_factor, other_decay), jnp.where(side == 0, other_decay, decay_factor)]
    )
    log_decay = jnp.log(decay)
    block_decay = jnp.exp(block * log_decay)
    steps = 4
    count = slots // steps

    def table(values):
        lanes = values.shape[-1]
        return jnp.broadcast_to(values[:, None], (2, count, quarter, lanes)).reshape(-1, lanes)

    half_head = head_size // 2
    frequency = jnp.exp(-math.log(10000.0) * jnp.arange(half_head, dtype=F32) / half_head)
    phase = (base + offsets).astype(F32)[..., None] * frequency
    cosine, sine = jnp.cos(phase), jnp.sin(phase)
    cosine = table(jnp.concatenate([cosine, cosine], axis=-1))
    sine = table(jnp.concatenate([-sine, sine], axis=-1))
    spot = offsets.astype(F32)
    log_lanes = jnp.repeat(log_decay, head_size)
    query_decay = table(jnp.exp((spot[..., None] + 1.0) * log_lanes))
    key_decay = table(jnp.exp((block - 1.0 - spot[..., None]) * log_lanes))
    flat = jnp.broadcast_to(spot[:, None], (2, count, quarter)).reshape(-1)
    slot_of = jnp.broadcast_to(jnp.arange(count)[None, :, None], (2, count, quarter)).reshape(-1)
    gap = flat[:, None] - flat[None, :]
    seen = (gap >= 0.0) & (slot_of[:, None] == slot_of[None, :])
    decay_grid = jnp.where(
        seen[None], jnp.exp(jnp.maximum(gap, 0.0)[None] * log_decay[:, None, None]), 0.0
    )
    decay_grid_t = jnp.swapaxes(decay_grid, 1, 2)

    def join(*parts):
        return jnp.concatenate(parts, axis=0)

    z_far, z_near = z_masks[:-1], z_masks[-1]
    swap = exchange

    def tie(*arrays):
        return lax.optimization_barrier(arrays)

    def far_open(x):
        for m in z_far[:-1]:
            x = join(x, swap(x, m))
        return x, swap(x, z_far[-1])

    key_w, value_w = key_weight[None, None], value_weight[None, None]
    dn = down_matrix.T[None]
    gl = jnp.stack([gate_matrix.T, lift_matrix.T])[None]
    qmo = jnp.stack([query_weight, modulate_weight, output_weight])[None]
    input_rows = layer_input.astype(F32)
    normed = simple_norm(input_rows).astype(BF16)
    cotangent = output_cotangent.astype(F32)
    cotangent_x = [swap(output_cotangent[: slots // 2], x_mask)]
    key_w, k_got = far_open(key_w)
    k_got, v_got = tie(k_got, swap(value_w, y_mask))
    key_w, value_w = join(key_w, k_got), join(value_w, v_got)
    value_w, v_got = far_open(value_w)
    k_got, v_got, dn_y, cotangent_x[0] = tie(
        swap(key_w, z_near), v_got, swap(dn, y_mask), cotangent_x[0]
    )
    key_w, value_w, dn = join(key_w, k_got), join(value_w, v_got), join(dn, dn_y)
    normed_pair = (normed, swap(normed, 1))
    k_got, v_got = tie(swap(key_w, x_mask), swap(value_w, z_near))
    key_w, value_w, qmo = join(key_w, k_got), join(value_w, v_got), tie(qmo, k_got)[0]
    qmo, q_got = far_open(qmo)
    k_got, v_got, q_got = tie(swap(key_w, y_mask), swap(value_w, x_mask), q_got)
    key_parts, value_parts = (key_w, k_got), (value_w, v_got)
    qmo = join(qmo, q_got)
    qmo_z = swap(qmo, z_near)
    inner_width = heads * head_size
    chip_shape = (2, slots, quarter, inner_width)
    row_shape = (slots, quarter, width)
    state_shape = (slots, heads, head_size, head_size)
    square_flops = 2 * 2 * slots * quarter * width * inner_width
    wide_scratch = pltpu.VMEM((width, inner_width), BF16)
    held_scratch = pltpu.VMEM((4, slots // 4, heads, head_size, head_size), BF16)
    dma = pltpu.SemaphoreType.DMA

    key_pre, keys, values, local_state = run(
        key_value_kernel, "key_value", spots,
        [
            (normed_pair[0], "rows"), (normed_pair[1], "rows"), (mask_wide, "pair"),
            (cosine, "whole"), (sine, "whole"), (key_decay, "whole"),
            (key_parts[0], "any"), (key_parts[1], "any"),
            (value_parts[0], "any"), (value_parts[1], "any"),
        ],
        [
            (chip_shape, BF16, "pair"), (chip_shape, BF16, "pair"), (chip_shape, BF16, "pair"),
            (state_shape, BF16, "rows"),
        ],
        [wide_scratch, wide_scratch, dma((2, members))],
        steps, 2 * square_flops,
    )
    local_state, qmo_z = tie(local_state, qmo_z)
    qmo = join(qmo, qmo_z)
    qm, out_w = qmo[:, :2], qmo[:, 2:]
    scan = Carry(local_state, block_decay, False)
    scan.spread()
    gl, gl_got = far_open(tie(gl, qmo_z)[0])
    scan.got[1], scan.got[2], scan.got[3], qm, out_w = tie(*scan.got[1:], qm, out_w)
    qm_x, o_y = swap(qm, x_mask), swap(out_w, y_mask)
    held = {}

    def forward_step(step, got):
        if step == 1:
            got, qx, oy, held["gl"] = tie(got, qm_x, o_y, gl_got)
            held["qm"], held["out"] = join(qm, qx), join(out_w, oy)
            held["gl"] = join(gl, held["gl"])
            held["more"] = [
                swap(held["qm"], y_mask), swap(held["out"], x_mask), swap(held["gl"], z_near),
                swap(tie(output_cotangent[slots // 2 :], oy)[0], x_mask),
            ]
        if step == 2:
            got, *held["more"] = tie(got, *held["more"])
        return got

    scan.along(forward_step)
    qm_y, o_x, gl_z, more_x = held["more"]
    cotangent_x.append(more_x)
    gl = join(held["gl"], gl_z)
    query_parts, output_parts = (held["qm"], qm_y), (held["out"], o_x)
    dn, dn_got = far_open(tie(dn, gl_z)[0])
    state_parts = scan.back()
    query_pre, queries, modulate, intra = run(
        query_kernel, "query", spots,
        [
            (normed_pair[0], "rows"), (normed_pair[1], "rows"), (mask_wide, "pair"),
            (cosine, "whole"), (sine, "whole"), (decay_grid, "whole"),
            (keys, "pair"), (values, "pair"), (query_parts[0], "any"), (query_parts[1], "any"),
        ],
        [
            (chip_shape, BF16, "pair"), (chip_shape, BF16, "pair"), (chip_shape, BF16, "pair"),
            (chip_shape, BF16, "pair"),
        ],
        [wide_scratch, wide_scratch, dma((2, members))],
        steps, 2 * square_flops,
    )
    *state_parts, queries, dn_got = tie(*state_parts, queries, dn_got)
    dn = join(dn, dn_got)
    state_inputs = [(p, "any") for p in state_parts]
    output_inputs = [(p, "any") for p in output_parts]
    mixed, gated, near_att, far_att = run(
        mixed_kernel, "mixed", spots,
        [
            (queries, "pair"), (intra, "pair"), (modulate, "pair"), (query_decay, "whole"),
            *state_inputs, *output_inputs,
        ],
        [
            (chip_shape, BF16, "pair"), (chip_shape, BF16, "pair"), (row_shape, F32, "rows"),
            (row_shape, BF16, "rows"),
        ],
        [wide_scratch, held_scratch, dma((members,)), dma((4,))],
        steps, square_flops,
    )
    middle = input_rows + core_sum(near_att, far_att)
    two = simple_norm(middle).astype(BF16)
    two_x, gl_y = tie(swap(two, x_mask), swap(gl, y_mask))
    dn_z = swap(dn, z_near)

    def quarters(mine, got_x):
        return [mine, got_x, swap(mine, 1), swap(got_x, 1)]

    def core_part(keep, send):
        got = swap(send, 1)
        return fold(keep[0], got[0], F32), fold(keep[1], got[1])

    two_pieces = quarters(two, two_x)
    normed_two = jnp.stack(two_pieces)
    row_starts = (narrow_index ^ jnp.array([0, x_mask, 1, 1 + x_mask], jnp.int32)) * quarter
    row_spots = wide_index * (quarter * narrow_count) + row_starts[:, None] + jnp.arange(quarter)
    row_mask = (row_spots[:, None, :] < valid_lengths[None, :, None]).astype(F32)[..., None]
    branch_pieces = quarters(output_cotangent, jnp.concatenate(cotangent_x))
    row_mask_wide = jnp.broadcast_to(row_mask, (4, slots, quarter, head_size)).astype(BF16)
    gate_t = join(gl[:, 0], gl_y[:, 0]).reshape(-1, width)
    lift_t = join(gl[:, 1], gl_y[:, 1]).reshape(-1, width)
    bulk = half // 2
    down_t = jnp.swapaxes(join(dn, dn_z).reshape(bulk, 2, -1, width), 0, 1).reshape(-1, width)

    def outer(a, b):
        return jnp.einsum("pblf,pbld->fd", a, b, preferred_element_type=F32).astype(BF16)

    hidden_shape = (4, slots, quarter, gate_t.shape[0])
    sum_shape = (2, slots, quarter, width)
    hidden_flops = 2 * 4 * slots * quarter * width * gate_t.shape[0]
    inner, gate_grad, lift_grad, row_keep, row_send, branch_keep, branch_send = run(
        hidden_kernel, "hidden", spots,
        [
            *[(p, "rows") for p in two_pieces], *[(p, "rows") for p in branch_pieces],
            (row_mask_wide, "pair"), (gate_t, "whole"),
            (lift_t, "whole"), (down_t, "whole"),
        ],
        [(hidden_shape, BF16, "pair")] * 3 + [(sum_shape, BF16, "pair")] * 4,
        [], steps, 6 * hidden_flops,
    )
    row_mine, row_send = core_part(row_keep, row_send)
    row_got = swap(row_send, x_mask)
    branch_rows = jnp.stack(branch_pieces).astype(F32)
    branch_rows = (tie(row_mask, row_send)[0] * branch_rows).astype(BF16)
    gate_grad, lift_grad, inner, row_send = tie(gate_grad, lift_grad, inner, row_send)
    gate_g = outer(gate_grad, normed_two).reshape(2, bulk, -1, width)
    gate_y = swap(gate_g[1], y_mask)
    lift_grad, inner, gate_g = tie(lift_grad, inner, gate_g)
    lift_g = outer(lift_grad, normed_two).reshape(2, bulk, -1, width)
    down_g = outer(inner, branch_rows).reshape(2, 2, bulk // 2, -1, width)
    branch_mine, branch_send = core_part(branch_keep, branch_send)
    row_got, gate_y, lift_send, down_z_send, branch_send = tie(
        row_got, gate_y, lift_g[1], down_g[:, 1], branch_send
    )
    lift_y = swap(lift_send, y_mask)
    branch_got = swap(branch_send, x_mask)
    down_z = swap(down_z_send, z_near)
    middle_grad = cotangent + norm_backward(middle, row_mine + row_got.astype(F32))

    attended_grad = middle_grad.astype(BF16)
    attended_pair = (attended_grad, exchange(attended_grad, 1))
    modulate_grad, query_grad, key_grad, value_grad, state_grad = run(
        mixed_back_kernel, "mixed_back", spots,
        [
            (attended_pair[0], "rows"), (attended_pair[1], "rows"), (mixed, "pair"),
            (modulate, "pair"), (queries, "pair"), (query_pre, "pair"), (keys, "pair"),
            (values, "pair"), (mask_wide, "pair"), (cosine, "whole"), (sine, "whole"),
            (query_decay, "whole"), (decay_grid, "whole"), (decay_grid_t, "whole"),
            *state_inputs, *output_inputs,
        ],
        [
            (chip_shape, BF16, "pair"), (chip_shape, BF16, "pair"), (chip_shape, BF16, "pair"),
            (chip_shape, BF16, "pair"), (state_shape, BF16, "rows"),
        ],
        [wide_scratch, held_scratch, dma((members,)), dma((4,))],
        steps, 2 * square_flops,
    )
    state_grad, lift_y, gated = tie(state_grad, lift_y, gated)
    near = bulk // 2
    scan = Carry(state_grad, block_decay, True)
    scan.spread()

    def square(name, order, a, *grads):
        shape = (half, len(grads), rows, cols)
        return run(
            functools.partial(outer_kernel, order), name, spots,
            [(a[0], "whole"), (a[1], "whole"), *[(g, "whole") for g in grads]],
            [(shape, BF16, "any"), (shape, BF16, "any")],
            [pltpu.VMEM((len(grads), width, inner_width), BF16), dma((len(grads), members))],
            1, len(grads) * square_flops,
        )

    output_keep, output_send = square("output_outer", 1, attended_pair, gated)
    query_keep, query_send = square("query_outer", 0, normed_pair, query_grad, modulate_grad)
    *scan.got, gate_y, down_z, branch_got, query_keep, query_send, output_keep, output_send = tie(
        *scan.got, gate_y, down_z, branch_got, query_keep, query_send, output_keep, output_send
    )
    layer_output = (middle + mask_rows * (branch_mine + branch_got.astype(F32))).astype(BF16)
    down_g = jnp.moveaxis(fold(down_g[:, 0], down_z), 1, 0)
    for m in z_far[:0:-1]:
        size = down_g.shape[0] // 2
        down_g = fold(down_g[:size], swap(down_g[size:], m))
    gl_g = jnp.stack([fold(gate_g[0], gate_y), fold(lift_g[0], lift_y)], axis=1)

    query_y, output_x = swap(query_send[:, :1], y_mask), swap(output_send, x_mask)

    def backward_step(step, got):
        if step == 1:
            got, held["y"], mod_send = tie(got, query_y, query_send[:, 1:])
            held["more"] = swap(mod_send, y_mask)
        if step == 2:
            got, held["more"], held["x"] = tie(got, held["more"], output_x)
        return got

    scan.along(backward_step)
    query_y = jnp.concatenate([held["y"], held["more"]], axis=1)
    scan.before, down_g, gl_g = tie(scan.before, down_g, gl_g)
    down_far = swap(down_g[1], z_far[0])
    gl_z = swap(gl_g[near:], z_near)
    later_parts = list(tie(*scan.back()))
    query_keep, output_keep = tie(query_keep, output_keep, *later_parts)[:2]
    query_g, output_g = fold(query_keep, query_y), fold(output_keep, held["x"])
    quad = half // 2
    query_x, output_y = swap(query_g[quad:], x_mask), swap(output_g[quad:], y_mask)
    later_inputs = [(p, "any") for p in later_parts]
    quad = half // 2
    def far_folds(x):
        for m in reversed(z_far):
            size = x.shape[0] // 2
            x = (fold if size > 1 else final)(x[:size], swap(x[size:], m))
        return x

    key_out, value_out = run(
        key_back_kernel, "key_back", spots,
        [
            (key_grad, "pair"), (value_grad, "pair"), (keys, "pair"), (values, "pair"),
            (key_pre, "pair"), (mask_wide, "pair"), (cosine, "whole"), (sine, "whole"),
            (key_decay, "whole"), *later_inputs,
        ],
        [(chip_shape, BF16, "pair"), (chip_shape, BF16, "pair")],
        [held_scratch, dma((4,))],
        steps, square_flops // 2,
    )
    key_keep, key_send = square("key_outer", 0, normed_pair, key_out)
    value_keep, value_send = square("value_outer", 1, normed_pair, value_out)
    key_send, value_send, gl_z, down_far, query_x, output_y = tie(
        key_send, value_send, gl_z, down_far, query_x, output_y
    )
    down_g = fold(down_g[0], down_far)
    gl_g = fold(gl_g[:near], gl_z)
    for m in z_far[:0:-1]:
        size = gl_g.shape[0] // 2
        gl_g = fold(gl_g[:size], swap(gl_g[size:], m))
    gl_far = swap(gl_g[1], z_far[0])
    key_y, value_x = swap(key_send, y_mask), swap(value_send, x_mask)
    key_out, value_out = tie(key_out, value_out, key_send, value_send)[:2]
    near_rows, far_rows = run(
        rows_kernel, "rows", spots,
        [
            (query_grad, "pair"), (modulate_grad, "pair"), (key_out, "pair"),
            (value_out, "pair"), (query_parts[0], "any"), (query_parts[1], "any"),
            (key_parts[0], "any"), (key_parts[1], "any"),
            (value_parts[0], "any"), (value_parts[1], "any"),
        ],
        [(row_shape, F32, "rows"), (row_shape, BF16, "rows")],
        [wide_scratch] * 4 + [dma((4, members))],
        steps, 4 * square_flops,
    )
    qmo_g = jnp.concatenate(
        [fold(query_g[:quad], query_x), fold(output_g[:quad], output_y)], axis=1
    )
    qmo_z = swap(qmo_g[near:], z_near)
    key_y, value_x, near_rows = tie(key_y, value_x, near_rows)
    down_y = swap(down_g[1], y_mask)
    key_g, value_g = fold(key_keep, key_y), fold(value_keep, value_x)
    key_x, value_y = swap(key_g[quad:], x_mask), swap(value_g[quad:], y_mask)
    key_x, value_y, down_y, qmo_z, gl_far = tie(key_x, value_y, down_y, qmo_z, gl_far)
    gate_lift = final(gl_g[0], gl_far)
    kv_g = jnp.concatenate([fold(key_g[:quad], key_x), fold(value_g[:quad], value_y)], axis=1)
    kv_z = swap(kv_g[near:], z_near)
    qmo_g = far_folds(fold(qmo_g[:near], qmo_z))[0]
    key_gradient, value_gradient = far_folds(fold(kv_g[:near], kv_z))[0]
    query_gradient, modulate_gradient, output_gradient = qmo_g
    down_gradient = final(down_g[0], down_y).T
    gate_gradient, lift_gradient = gate_lift[0].T, gate_lift[1].T
    input_gradient = middle_grad + norm_backward(input_rows, core_sum(near_rows, far_rows))
    return (
        layer_output,
        input_gradient,
        query_gradient,
        key_gradient,
        value_gradient,
        modulate_gradient,
        output_gradient,
        gate_gradient,
        lift_gradient,
        down_gradient,
    )


def solution(mesh):
    placed = (
        P(None, ("wide", "narrow"), None),
        P("wide", "narrow"),
        P("wide", "narrow"),
        P("wide", "narrow"),
        P("wide", "narrow"),
        P("wide", "narrow"),
        P(None, ("wide", "narrow")),
        P(None, ("wide", "narrow")),
        P(None, ("wide", "narrow")),
        P("narrow"),
        P(),
        P(None, ("wide", "narrow"), None),
    )
    return jax.shard_map(
        on_device,
        mesh=mesh,
        in_specs=placed,
        out_specs=(
            P(None, ("wide", "narrow"), None),
            P(None, ("wide", "narrow"), None),
            P("wide", "narrow"),
            P("wide", "narrow"),
            P("wide", "narrow"),
            P("wide", "narrow"),
            P("wide", "narrow"),
            P(None, ("wide", "narrow")),
            P(None, ("wide", "narrow")),
            P(None, ("wide", "narrow")),
        ),
        check_vma=False,
    )
```

```python
import functools
import math

import jax
import jax.numpy as jnp
from jax import lax
from jax.experimental import pallas as pl
from jax.experimental.pallas import tpu as pltpu
from jax.sharding import PartitionSpec as P

EPS = 1e-06
AXES = ("wide", "narrow")
BF16 = jnp.bfloat16
F32 = jnp.float32


def simple_norm(values):
    return values * lax.rsqrt(jnp.mean(values * values, axis=-1, keepdims=True) + EPS)


def norm_backward(values, cotangent):
    scale = lax.rsqrt(jnp.mean(values * values, axis=-1, keepdims=True) + EPS)
    inner = jnp.mean(values * cotangent, axis=-1, keepdims=True)
    return scale * cotangent - values * (scale * scale * scale * inner)


def apply_swish(values):
    return values * jax.nn.sigmoid(values)


def swish_slope(values):
    sigmoid_value = jax.nn.sigmoid(values)
    return sigmoid_value + values * sigmoid_value * (1.0 - sigmoid_value)


def exchange(x, mask):
    count = lax.axis_size(AXES)
    return lax.ppermute(x, AXES, [(i, i ^ mask) for i in range(count)])


def after(x, *others):
    return lax.optimization_barrier((x, *others))[0]


def shift_z(x, step, reverse):
    count, unit = lax.axis_size(AXES), 2 * lax.axis_size("narrow")
    pairs = [(i, i + step * unit) for i in range(count - step * unit)]
    if reverse:
        pairs = [(b, a) for a, b in pairs]
    return lax.ppermute(x, AXES, pairs)


def gather_plane(x, masks):
    return gather_more(x[None], masks)


def gather_more(held, masks):
    for mask in masks:
        held = jnp.concatenate([held, exchange(held, mask)], axis=0)
    return held


def gather_hidden(x, masks, swapped):
    held = gather_plane(x, masks)
    if swapped:
        held = jnp.swapaxes(held.reshape(2, 2, -1, *x.shape), 0, 1)
    return held.reshape(-1, x.shape[-1])


def scatter_plane(x, masks):
    for mask in reversed(masks):
        half = x.shape[0] // 2
        got = exchange(x[half:], mask)
        total = x[:half].astype(F32) + got.astype(F32)
        x = total.astype(BF16) if half > 1 else total
    return x[0]


def fold(mine, got, dtype=BF16):
    return (mine.astype(F32) + got.astype(F32)).astype(dtype)


def final(mine, got):
    return fold(mine, got, F32)


def relative(masks, index):
    out = 0
    for k, mask in enumerate(masks):
        out ^= mask * ((index >> k) & 1)
    return out


NT = (((1,), (1,)), ((), ()))
NN = (((1,), (0,)), ((), ()))
TN = (((0,), (0,)), ((), ()))


def mm(a, b, dims=NN):
    return lax.dot_general(a, b, dims, preferred_element_type=F32)


def turn(v, cosine, sine):
    return v * cosine + pltpu.roll(v, v.shape[-1] // 2, 1) * sine


def block_spots(masks):
    own = lax.axis_index(AXES)
    narrow_count = lax.axis_size("narrow")
    ids = jnp.array([relative(masks, i) for i in range(1 << len(masks))], jnp.int32) ^ own
    return jnp.stack([ids // narrow_count, (ids % narrow_count) // 2], axis=1)


def block_copy(spots, which, i, rows, cols, whole, part, sem, out):
    at = (
        pl.ds(pl.multiple_of(spots[which, i, 0] * rows, rows), rows),
        pl.ds(pl.multiple_of(spots[which, i, 1] * cols, cols), cols),
    )
    if out:
        return pltpu.make_async_copy(whole.at[at], part, sem)
    return pltpu.make_async_copy(part, whole.at[at], sem)


def each_block(spots, jobs, out=False):
    def go(method):
        for order, k, near, far, whole, sems in jobs:
            half, _, rows, cols = near.shape

            def step(i, _):
                for at, part in enumerate((near, far)):
                    copy = block_copy(
                        spots, order, i + at * half, rows, cols, whole, part.at[i, k],
                        sems.at[i + at * half], out,
                    )
                    getattr(copy, method)()
                return 0

            lax.fori_loop(0, half, step, 0)

    go("start")
    go("wait")


def both(near, far):
    rows = near.shape[0] * near.shape[1]
    return jnp.concatenate([near.reshape(rows, -1), far.reshape(rows, -1)], axis=0)


def slot_rows(x, s, size, count):
    return jnp.concatenate(
        [x[s * size : (s + 1) * size], x[(count + s) * size : (count + s + 1) * size]], axis=0
    )


def slot_back(parts, size):
    return jnp.concatenate([p[:size] for p in parts] + [p[size:] for p in parts], axis=0)


def put(ref, lanes, value):
    two, count, size, _ = ref.shape
    ref[:, :, :, lanes] = value.reshape(two, count, size, -1).astype(ref.dtype)


def get(ref, lanes=slice(None)):
    two, count, size, width = ref.shape
    x = ref[:, :, :, lanes]
    return x.reshape(two * count * size, x.shape[-1])


def key_value_kernel(
    spots, near, far, mask, cosine, sine, key_decay, kw0, kw1, vw0, vw1,
    key_pre, keys, values, state, wk, wv, sems
):
    @pl.when(pl.program_id(0) == 0)
    def _():
        each_block(spots, [(0, 0, kw0, kw1, wk, sems.at[0]), (2, 0, vw0, vw1, wv, sems.at[1])])

    count, size = near.shape[0], near.shape[1]
    x = both(near[...], far[...])
    valid = get(mask).astype(F32)
    head = cosine.shape[-1]
    pre = mm(x, wk[...])
    val_pre = mm(x, wv[...])
    for h in range(pre.shape[-1] // head):
        lanes = slice(h * head, (h + 1) * head)
        kp = pre[:, lanes]
        put(key_pre, lanes, kp)
        key = (valid * turn(kp * jax.nn.sigmoid(kp), cosine[...], sine[...])).astype(BF16)
        val = (valid * val_pre[:, lanes]).astype(BF16)
        put(keys, lanes, key)
        put(values, lanes, val)
        scaled = (key.astype(F32) * key_decay[:, lanes]).astype(BF16)
        for s in range(count):
            state[s, h] = mm(
                slot_rows(scaled, s, size, count), slot_rows(val, s, size, count), TN
            ).astype(BF16)


def query_kernel(
    spots, near, far, mask, cosine, sine, grid, keys, values, w0, w1,
    query_pre, queries, modulate, intra, wq, wm, sems
):
    @pl.when(pl.program_id(0) == 0)
    def _():
        each_block(spots, [(0, 0, w0, w1, wq, sems.at[0]), (0, 1, w0, w1, wm, sems.at[1])])

    count, size = near.shape[0], near.shape[1]
    x = both(near[...], far[...])
    valid = get(mask).astype(F32)
    head = cosine.shape[-1]
    pre = mm(x, wq[...])
    mod = mm(x, wm[...])
    for h in range(pre.shape[-1] // head):
        lanes = slice(h * head, (h + 1) * head)
        qp = pre[:, lanes]
        put(query_pre, lanes, qp)
        put(modulate, lanes, mod[:, lanes] * valid)
        q = turn(qp * jax.nn.sigmoid(qp), cosine[...], sine[...]).astype(BF16)
        put(queries, lanes, q)
        k, v = get(keys, lanes), get(values, lanes)
        scores = (mm(q, k, NT) * grid[h]).astype(BF16)
        put(intra, lanes, mm(scores, v))


def load_states(spots, pieces, held, sems):
    member = spots[3, 0, 0]
    copies = [
        pltpu.make_async_copy(p, held.at[member ^ k], sems.at[k]) for k, p in enumerate(pieces)
    ]
    for c in copies:
        c.start()
    for c in copies:
        c.wait()


def mixed_kernel(
    spots, queries, intra, modulate, query_decay, s0, s1, s2, s3, w0, w1,
    mixed, gated, near_out, far_out, wo, held, sems, state_sems
):
    @pl.when(pl.program_id(0) == 0)
    def _():
        load_states(spots, (s0, s1, s2, s3), held, state_sems)
        each_block(spots, [(1, 0, w0, w1, wo, sems)])

    step = pl.program_id(0)
    _, count, size, width = queries.shape
    heads = held.shape[2]
    head = width // heads
    gates = []
    for h in range(heads):
        lanes = slice(h * head, (h + 1) * head)
        q = (get(queries, lanes).astype(F32) * query_decay[:, lanes]).astype(BF16)
        parts = [mm(slot_rows(q, s, size, count), held[step, s, h]) for s in range(count)]
        mix = get(intra, lanes).astype(F32) + slot_back(parts, size)
        put(mixed, lanes, mix)
        scale = lax.rsqrt(jnp.mean(mix * mix, axis=-1, keepdims=True) + EPS)
        gates.append((mix * scale * get(modulate, lanes).astype(F32)).astype(BF16))
    gate = jnp.concatenate(gates, axis=1)
    put(gated, slice(None), gate)
    out = mm(gate, wo[...], NT)
    near_out[...] = out[: count * size].reshape(near_out.shape)
    far_out[...] = out[count * size :].astype(BF16).reshape(far_out.shape)


def mixed_back_kernel(
    spots, near, far, mixed, modulate, queries, query_pre, keys, values, mask, cosine, sine,
    query_decay, grid, grid_t, s0, s1, s2, s3, w0, w1,
    modulate_grad, query_grad, key_grad, value_grad, state_grad, wo, held, sems, state_sems
):
    @pl.when(pl.program_id(0) == 0)
    def _():
        load_states(spots, (s0, s1, s2, s3), held, state_sems)
        each_block(spots, [(1, 0, w0, w1, wo, sems)])

    step = pl.program_id(0)
    _, count, size, width = queries.shape
    heads = held.shape[2]
    head = width // heads
    gate_grad = mm(both(near[...], far[...]), wo[...])
    valid = get(mask).astype(F32)
    for h in range(heads):
        lanes = slice(h * head, (h + 1) * head)
        mix = get(mixed, lanes).astype(F32)
        scale = lax.rsqrt(jnp.mean(mix * mix, axis=-1, keepdims=True) + EPS)
        gg = gate_grad[:, lanes]
        put(modulate_grad, lanes, gg * valid * (mix * scale))
        cot = gg * get(modulate, lanes).astype(F32)
        inner = jnp.mean(mix * cot, axis=-1, keepdims=True)
        gm = (scale * cot - mix * (scale * scale * scale * inner)).astype(BF16)
        q, k, v = get(queries, lanes), get(keys, lanes), get(values, lanes)
        qs = (q.astype(F32) * query_decay[:, lanes]).astype(BF16)
        gst = (mm(v, gm, NT) * grid_t[h]).astype(BF16)
        gs = (mm(gm, v, NT) * grid[h]).astype(BF16)
        sct = (mm(k, q, NT) * grid_t[h]).astype(BF16)
        put(value_grad, lanes, mm(sct, gm))
        put(key_grad, lanes, mm(gst, q))
        gq = []
        for s in range(count):
            pick = lambda x: slot_rows(x, s, size, count)
            gms = pick(gm)
            gq.append(mm(gms, held[step, s, h], NT))
            state_grad[s, h] = mm(pick(qs), gms, TN).astype(BF16)
        gq = mm(gs, k) + slot_back(gq, size) * query_decay[:, lanes]
        qp = get(query_pre, lanes).astype(F32)
        sg = jax.nn.sigmoid(qp)
        slope = sg + qp * sg * (1.0 - sg)
        put(query_grad, lanes, turn(gq, cosine[...], -sine[...]) * slope)


def rows_kernel(
    spots, query_grad, modulate_grad, key_grad, value_grad, w0, w1, kw0, kw1, vw0, vw1,
    near_out, far_out, wq, wm, wk, wv, sems
):
    @pl.when(pl.program_id(0) == 0)
    def _():
        each_block(
            spots,
            [
                (0, 0, w0, w1, wq, sems.at[0]), (0, 1, w0, w1, wm, sems.at[1]),
                (0, 0, kw0, kw1, wk, sems.at[2]), (2, 0, vw0, vw1, wv, sems.at[3]),
            ],
        )

    out = mm(get(query_grad), wq[...], NT) + mm(get(modulate_grad), wm[...], NT)
    out = out + mm(get(key_grad), wk[...], NT) + mm(get(value_grad), wv[...], NT)
    half = out.shape[0] // 2
    near_out[...] = out[:half].reshape(near_out.shape)
    far_out[...] = out[half:].astype(BF16).reshape(far_out.shape)


def key_back_kernel(
    spots, key_grad, value_grad, keys, values, key_pre, mask, cosine, sine, key_decay,
    g0, g1, g2, g3, key_out, value_out, held, state_sems
):
    @pl.when(pl.program_id(0) == 0)
    def _():
        load_states(spots, (g0, g1, g2, g3), held, state_sems)

    step = pl.program_id(0)
    _, count, size, width = keys.shape
    heads = held.shape[2]
    head = width // heads
    valid = get(mask).astype(F32)
    for h in range(heads):
        lanes = slice(h * head, (h + 1) * head)
        decay = key_decay[:, lanes]
        k, v = get(keys, lanes), get(values, lanes)
        scaled = (k.astype(F32) * decay).astype(BF16)
        pk = [mm(slot_rows(v, s, size, count), held[step, s, h], NT) for s in range(count)]
        pv = [mm(slot_rows(scaled, s, size, count), held[step, s, h]) for s in range(count)]
        gk = get(key_grad, lanes).astype(F32) + slot_back(pk, size) * decay
        gv = get(value_grad, lanes).astype(F32) + slot_back(pv, size)
        kp = get(key_pre, lanes).astype(F32)
        sg = jax.nn.sigmoid(kp)
        slope = sg + kp * sg * (1.0 - sg)
        put(key_out, lanes, turn(gk * valid, cosine[...], -sine[...]) * slope)
        put(value_out, lanes, gv * valid)


def hidden_kernel(
    spots, n0, n1, n2, n3, b0, b1, b2, b3, mask, gate_w, lift_w, down_w,
    inner_out, gate_out, lift_out, keep, send, branch_keep, branch_send
):
    flat = lambda refs: jnp.concatenate([r[...].reshape(-1, r.shape[-1]) for r in refs], axis=0)
    x, b = flat((n0, n1, n2, n3)), flat((b0, b1, b2, b3))
    valid = get(mask)[:, :1].astype(F32)
    gate, lift, down = gate_w[...], lift_w[...], down_w[...]
    parts = []
    for r in range(0, x.shape[0], 256):
        rows = slice(r, r + 256)
        gate_pre = mm(x[rows], gate, NT)
        lift_pre = mm(x[rows], lift, NT)
        inner_grad = mm(b[rows], down, NT) * valid[rows]
        q = jax.nn.sigmoid(gate_pre)
        act = gate_pre * q
        gate_grad = (inner_grad * lift_pre * (q + act * (1.0 - q))).astype(BF16)
        lift_grad = (inner_grad * act).astype(BF16)
        inner = (act * lift_pre).astype(BF16)
        total = (mm(gate_grad, gate) + mm(lift_grad, lift)).astype(BF16)
        parts.append((inner, gate_grad, lift_grad, total, mm(inner, down).astype(BF16)))
    inner, gate_grad, lift_grad, total, branch = (jnp.concatenate(p, axis=0) for p in zip(*parts))
    put(inner_out, slice(None), inner)
    put(gate_out, slice(None), gate_grad)
    put(lift_out, slice(None), lift_grad)
    half = total.shape[0] // 2
    for near, far, value in ((keep, send, total), (branch_keep, branch_send, branch)):
        near[...] = value[:half].reshape(near.shape)
        far[...] = value[half:].reshape(far.shape)


def outer_kernel(order, spots, near, far, *refs):
    count = (len(refs) - 4) // 1
    grads, (keep, send, whole, sems) = refs[:count], refs[count:]
    rows = near.shape[0] * near.shape[1]
    width = near.shape[2]
    tile = 256
    for c in range(0, width, tile):
        a = near[:, :, c : c + tile].reshape(rows, tile)
        b = far[:, :, c : c + tile].reshape(rows, tile)
        for k, g in enumerate(grads):
            g0 = g[0].reshape(rows, -1)
            g1 = g[1].reshape(rows, -1)
            whole[k, c : c + tile, :] = (mm(a, g0, TN) + mm(b, g1, TN)).astype(BF16)
    each_block(
        spots, [(order, k, keep, send, whole.at[k], sems.at[k]) for k in range(count)], out=True
    )


def outer_pair_kernel(
    orders, spots, near, far, g0, g1, keep0, send0, keep1, send1, whole, sems
):
    rows = near.shape[0] * near.shape[1]
    width = near.shape[2]
    tile = 256
    for c in range(0, width, tile):
        a = near[:, :, c : c + tile].reshape(rows, tile)
        b = far[:, :, c : c + tile].reshape(rows, tile)
        for k, g in enumerate((g0, g1)):
            first, second = g[0].reshape(rows, -1), g[1].reshape(rows, -1)
            whole[k, c : c + tile, :] = (mm(a, first, TN) + mm(b, second, TN)).astype(BF16)
    each_block(
        spots,
        [
            (orders[0], 0, keep0, send0, whole.at[0], sems.at[0]),
            (orders[1], 0, keep1, send1, whole.at[1], sems.at[1]),
        ],
        out=True,
    )


ANY = pl.BlockSpec(memory_space=pltpu.HBM)
VMEM = pl.BlockSpec(memory_space=pltpu.VMEM)


def run(kernel, name, spots, inputs, outputs, scratch, steps, flops):
    def spec(shape, kind):
        if kind == "any":
            return ANY
        if kind == "rows":
            size = shape[0] // steps
            return pl.BlockSpec((size, *shape[1:]), lambda i, _: (i,) + (0,) * (len(shape) - 1))
        if kind == "pair":
            size = shape[1] // steps
            return pl.BlockSpec(
                (shape[0], size, *shape[2:]), lambda i, _: (0, i) + (0,) * (len(shape) - 2)
            )
        return pl.BlockSpec(shape, lambda i, _: (0,) * len(shape))

    moved = sum(a.size * a.dtype.itemsize for a, _ in inputs)
    moved += sum(math.prod(s) * jnp.dtype(d).itemsize for s, d, _ in outputs)
    return pl.pallas_call(
        kernel,
        out_shape=[jax.ShapeDtypeStruct(s, d) for s, d, _ in outputs],
        grid_spec=pltpu.PrefetchScalarGridSpec(
            num_scalar_prefetch=1,
            grid=(steps,),
            in_specs=[spec(a.shape, kind) for a, kind in inputs],
            out_specs=[spec(s, kind) for s, _, kind in outputs],
            scratch_shapes=scratch,
        ),
        compiler_params=pltpu.CompilerParams(vmem_limit_bytes=(46 if name == "mixed_back" else 40) * 2**20),
        cost_estimate=pl.CostEstimate(flops=int(flops * 2.4), bytes_accessed=int(moved * 2.4), transcendentals=0),
        name=name,
    )(spots, *[a for a, _ in inputs])


class Carry:
    def __init__(self, local, block_decay, reverse):
        self.local, self.reverse = local, reverse
        narrow_count = lax.axis_size("narrow")
        self.member = 2 * (lax.axis_index("wide") % 2) + lax.axis_index("narrow") // 2
        self.masks = [0, 2, narrow_count, narrow_count + 2]
        ranks = [self.member ^ k for k in range(4)]
        self.ranks = [3 - r if reverse else r for r in ranks]
        self.log_decay = jnp.log(block_decay)

    def power(self, e):
        return jnp.exp(e * self.log_decay)[None, :, None, None]

    def spread(self):
        share = self.local.shape[0] // 4
        parts = [
            lax.dynamic_slice_in_dim(self.local, (self.member ^ k) * share, share, 0)
            for k in range(4)
        ]
        self.got = [parts[0]] + [exchange(parts[k], self.masks[k]) for k in range(1, 4)]

    def along(self, between=lambda step, got: got):
        self.held = [h.astype(F32) for h in self.got]
        span = sum(self.power((3 - self.ranks[k]).astype(F32)) * self.held[k] for k in range(4))
        before, step = 0.0, 1
        while step < lax.axis_size("wide") // 2:
            got = between(step, shift_z(span.astype(BF16), step, self.reverse)).astype(F32)
            before = before + self.power(4.0 * (step - 1)) * got
            span = span + self.power(4.0 * step) * got
            step *= 2
        self.before = before

    def back(self):
        sent = []
        for k in range(4):
            state = self.power(self.ranks[k].astype(F32)) * self.before
            for j in range(4):
                gap = (self.ranks[k] - 1 - self.ranks[j]).astype(F32)
                scale = jnp.where(gap >= 0, self.power(jnp.maximum(gap, 0.0)), 0.0)
                state = state + scale * self.held[j]
            sent.append(state.astype(BF16))
        return [sent[0]] + [exchange(sent[k], self.masks[k]) for k in range(1, 4)]


def on_device(
    layer_input,
    query_weight,
    key_weight,
    value_weight,
    modulate_weight,
    output_weight,
    gate_matrix,
    lift_matrix,
    down_matrix,
    decay_factor,
    valid_lengths,
    output_cotangent,
):
    narrow_count, wide_count = lax.axis_size("narrow"), lax.axis_size("wide")
    wide_index, narrow_index = lax.axis_index("wide"), lax.axis_index("narrow")
    core, side = narrow_index % 2, narrow_index // 2
    slots, quarter, width = layer_input.shape
    block = 2 * quarter
    rows, cols = query_weight.shape
    heads = 2 * decay_factor.shape[0]
    head_size = cols // decay_factor.shape[0]
    x_mask = 2
    wide_masks = []
    bit = narrow_count
    while bit < narrow_count * wide_count:
        wide_masks.append(bit)
        bit *= 2
    y_mask, z_masks = wide_masks[0], wide_masks[:0:-1]
    order_yx = z_masks + [y_mask, x_mask]
    order_xy = z_masks + [x_mask, y_mask]
    order_v = [y_mask] + z_masks + [x_mask]
    members = 1 << len(order_yx)
    half = members // 2

    base = wide_index * (quarter * narrow_count) + side * block
    offsets = jnp.stack(
        [core * quarter + jnp.arange(quarter), (1 - core) * quarter + jnp.arange(quarter)]
    ).astype(jnp.int32)
    mask = ((base + offsets)[:, None, :] < valid_lengths[None, :, None]).astype(F32)
    mask_rows = mask[0][:, :, None]
    mask_wide = jnp.broadcast_to(mask[..., None], (2, slots, quarter, head_size)).astype(BF16)
    member = 2 * (wide_index % 2) + side
    spots = jnp.concatenate(
        [
            block_spots(order_xy)[None],
            block_spots(order_yx)[None],
            block_spots(order_v)[None],
            jnp.broadcast_to(member, (1, members, 2)).astype(jnp.int32),
        ]
    )

    def core_sum(near, far):
        return near + exchange(far, 1).astype(F32)

    other_decay = exchange(decay_factor, x_mask)
    decay = jnp.concatenate(
        [jnp.where(side == 0, decay_factor, other_decay), jnp.where(side == 0, other_decay, decay_factor)]
    )
    log_decay = jnp.log(decay)
    block_decay = jnp.exp(block * log_decay)
    steps = 4
    count = slots // steps

    def table(values):
        lanes = values.shape[-1]
        return jnp.broadcast_to(values[:, None], (2, count, quarter, lanes)).reshape(-1, lanes)

    half_head = head_size // 2
    frequency = jnp.exp(-math.log(10000.0) * jnp.arange(half_head, dtype=F32) / half_head)
    phase = (base + offsets).astype(F32)[..., None] * frequency
    cosine, sine = jnp.cos(phase), jnp.sin(phase)
    cosine = table(jnp.concatenate([cosine, cosine], axis=-1))
    sine = table(jnp.concatenate([-sine, sine], axis=-1))
    spot = offsets.astype(F32)
    log_lanes = jnp.repeat(log_decay, head_size)
    query_decay = table(jnp.exp((spot[..., None] + 1.0) * log_lanes))
    key_decay = table(jnp.exp((block - 1.0 - spot[..., None]) * log_lanes))
    flat = jnp.broadcast_to(spot[:, None], (2, count, quarter)).reshape(-1)
    slot_of = jnp.broadcast_to(jnp.arange(count)[None, :, None], (2, count, quarter)).reshape(-1)
    gap = flat[:, None] - flat[None, :]
    seen = (gap >= 0.0) & (slot_of[:, None] == slot_of[None, :])
    decay_grid = jnp.where(
        seen[None], jnp.exp(jnp.maximum(gap, 0.0)[None] * log_decay[:, None, None]), 0.0
    )
    decay_grid_t = jnp.swapaxes(decay_grid, 1, 2)

    def join(*parts):
        return jnp.concatenate(parts, axis=0)

    z_far, z_near = z_masks[:-1], z_masks[-1]
    swap = exchange

    def tie(*arrays):
        return lax.optimization_barrier(arrays)

    def far_open(x):
        for m in z_far[:-1]:
            x = join(x, swap(x, m))
        return x, swap(x, z_far[-1])

    key_w, value_w = key_weight[None, None], value_weight[None, None]
    dn = down_matrix.T[None]
    gl = jnp.stack([gate_matrix.T, lift_matrix.T])[None]
    qmo = jnp.stack([query_weight, modulate_weight, output_weight])[None]
    input_rows = layer_input.astype(F32)
    normed = simple_norm(input_rows).astype(BF16)
    cotangent = output_cotangent.astype(F32)
    cotangent_x = [swap(output_cotangent[: slots // 2], x_mask)]
    key_w, k_got = far_open(key_w)
    k_got, v_got = tie(k_got, swap(value_w, y_mask))
    key_w, value_w = join(key_w, k_got), join(value_w, v_got)
    value_w, v_got = far_open(value_w)
    k_got, v_got, dn_y, cotangent_x[0] = tie(
        swap(key_w, z_near), v_got, swap(dn, y_mask), cotangent_x[0]
    )
    key_w, value_w, dn = join(key_w, k_got), join(value_w, v_got), join(dn, dn_y)
    normed_pair = (normed, swap(normed, 1))
    k_got, v_got = tie(swap(key_w, x_mask), swap(value_w, z_near))
    key_w, value_w, qmo = join(key_w, k_got), join(value_w, v_got), tie(qmo, k_got)[0]
    qmo, q_got = far_open(qmo)
    k_got, v_got, q_got = tie(swap(key_w, y_mask), swap(value_w, x_mask), q_got)
    key_parts, value_parts = (key_w, k_got), (value_w, v_got)
    qmo = join(qmo, q_got)
    qmo_z = swap(qmo, z_near)
    inner_width = heads * head_size
    chip_shape = (2, slots, quarter, inner_width)
    row_shape = (slots, quarter, width)
    state_shape = (slots, heads, head_size, head_size)
    square_flops = 2 * 2 * slots * quarter * width * inner_width
    wide_scratch = pltpu.VMEM((width, inner_width), BF16)
    held_scratch = pltpu.VMEM((4, slots // 4, heads, head_size, head_size), BF16)
    dma = pltpu.SemaphoreType.DMA

    key_pre, keys, values, local_state = run(
        key_value_kernel, "key_value", spots,
        [
            (normed_pair[0], "rows"), (normed_pair[1], "rows"), (mask_wide, "pair"),
            (cosine, "whole"), (sine, "whole"), (key_decay, "whole"),
            (key_parts[0], "any"), (key_parts[1], "any"),
            (value_parts[0], "any"), (value_parts[1], "any"),
        ],
        [
            (chip_shape, BF16, "pair"), (chip_shape, BF16, "pair"), (chip_shape, BF16, "pair"),
            (state_shape, BF16, "rows"),
        ],
        [wide_scratch, wide_scratch, dma((2, members))],
        steps, 2 * square_flops,
    )
    local_state, qmo_z = tie(local_state, qmo_z)
    qmo = join(qmo, qmo_z)
    qm, out_w = qmo[:, :2], qmo[:, 2:]
    scan = Carry(local_state, block_decay, False)
    scan.spread()
    gl, gl_got = far_open(tie(gl, qmo_z)[0])
    scan.got[1], scan.got[2], scan.got[3], qm, out_w = tie(*scan.got[1:], qm, out_w)
    qm_x, o_y = swap(qm, x_mask), swap(out_w, y_mask)
    held = {}

    def forward_step(step, got):
        if step == 1:
            got, qx, oy, held["gl"] = tie(got, qm_x, o_y, gl_got)
            held["qm"], held["out"] = join(qm, qx), join(out_w, oy)
            held["gl"] = join(gl, held["gl"])
            held["more"] = [
                swap(held["qm"], y_mask), swap(held["out"], x_mask), swap(held["gl"], z_near),
                swap(tie(output_cotangent[slots // 2 :], oy)[0], x_mask),
            ]
        if step == 2:
            got, *held["more"] = tie(got, *held["more"])
        return got

    scan.along(forward_step)
    qm_y, o_x, gl_z, more_x = held["more"]
    cotangent_x.append(more_x)
    gl = join(held["gl"], gl_z)
    query_parts, output_parts = (held["qm"], qm_y), (held["out"], o_x)
    dn, dn_got = far_open(tie(dn, gl_z)[0])
    state_parts = scan.back()
    query_pre, queries, modulate, intra = run(
        query_kernel, "query", spots,
        [
            (normed_pair[0], "rows"), (normed_pair[1], "rows"), (mask_wide, "pair"),
            (cosine, "whole"), (sine, "whole"), (decay_grid, "whole"),
            (keys, "pair"), (values, "pair"), (query_parts[0], "any"), (query_parts[1], "any"),
        ],
        [
            (chip_shape, BF16, "pair"), (chip_shape, BF16, "pair"), (chip_shape, BF16, "pair"),
            (chip_shape, BF16, "pair"),
        ],
        [wide_scratch, wide_scratch, dma((2, members))],
        steps, 2 * square_flops,
    )
    *state_parts, queries, dn_got = tie(*state_parts, queries, dn_got)
    dn = join(dn, dn_got)
    state_inputs = [(p, "any") for p in state_parts]
    output_inputs = [(p, "any") for p in output_parts]
    mixed, gated, near_att, far_att = run(
        mixed_kernel, "mixed", spots,
        [
            (queries, "pair"), (intra, "pair"), (modulate, "pair"), (query_decay, "whole"),
            *state_inputs, *output_inputs,
        ],
        [
            (chip_shape, BF16, "pair"), (chip_shape, BF16, "pair"), (row_shape, F32, "rows"),
            (row_shape, BF16, "rows"),
        ],
        [wide_scratch, held_scratch, dma((members,)), dma((4,))],
        steps, square_flops,
    )
    middle = input_rows + core_sum(near_att, far_att)
    two = simple_norm(middle).astype(BF16)
    two_x, gl_y = tie(swap(two, x_mask), swap(gl, y_mask))
    dn_z = swap(dn, z_near)

    def quarters(mine, got_x):
        return [mine, got_x, swap(mine, 1), swap(got_x, 1)]

    def core_part(keep, send):
        got = swap(send, 1)
        return fold(keep[0], got[0], F32), fold(keep[1], got[1])

    two_pieces = quarters(two, two_x)
    normed_two = jnp.stack(two_pieces)
    row_starts = (narrow_index ^ jnp.array([0, x_mask, 1, 1 + x_mask], jnp.int32)) * quarter
    row_spots = wide_index * (quarter * narrow_count) + row_starts[:, None] + jnp.arange(quarter)
    row_mask = (row_spots[:, None, :] < valid_lengths[None, :, None]).astype(F32)[..., None]
    branch_pieces = quarters(output_cotangent, jnp.concatenate(cotangent_x))
    row_mask_wide = jnp.broadcast_to(row_mask, (4, slots, quarter, head_size)).astype(BF16)
    gate_t = join(gl[:, 0], gl_y[:, 0]).reshape(-1, width)
    lift_t = join(gl[:, 1], gl_y[:, 1]).reshape(-1, width)
    bulk = half // 2
    down_t = jnp.swapaxes(join(dn, dn_z).reshape(bulk, 2, -1, width), 0, 1).reshape(-1, width)

    def outer(a, b):
        return jnp.einsum("pblf,pbld->fd", a, b, preferred_element_type=F32).astype(BF16)

    hidden_shape = (4, slots, quarter, gate_t.shape[0])
    sum_shape = (2, slots, quarter, width)
    hidden_flops = 2 * 4 * slots * quarter * width * gate_t.shape[0]
    inner, gate_grad, lift_grad, row_keep, row_send, branch_keep, branch_send = run(
        hidden_kernel, "hidden", spots,
        [
            *[(p, "rows") for p in two_pieces], *[(p, "rows") for p in branch_pieces],
            (row_mask_wide, "pair"), (gate_t, "whole"),
            (lift_t, "whole"), (down_t, "whole"),
        ],
        [(hidden_shape, BF16, "pair")] * 3 + [(sum_shape, BF16, "pair")] * 4,
        [], steps, 6 * hidden_flops,
    )
    row_mine, row_send = core_part(row_keep, row_send)
    row_got = swap(row_send, x_mask)
    branch_rows = jnp.stack(branch_pieces).astype(F32)
    branch_rows = (tie(row_mask, row_send)[0] * branch_rows).astype(BF16)
    gate_grad, lift_grad, inner, row_send = tie(gate_grad, lift_grad, inner, row_send)
    gate_g = outer(gate_grad, normed_two).reshape(2, bulk, -1, width)
    gate_y = swap(gate_g[1], y_mask)
    lift_grad, inner, gate_g = tie(lift_grad, inner, gate_g)
    lift_g = outer(lift_grad, normed_two).reshape(2, bulk, -1, width)
    down_g = outer(inner, branch_rows).reshape(2, 2, bulk // 2, -1, width)
    branch_mine, branch_send = core_part(branch_keep, branch_send)
    row_got, gate_y, lift_send, down_z_send, branch_send = tie(
        row_got, gate_y, lift_g[1], down_g[:, 1], branch_send
    )
    lift_y = swap(lift_send, y_mask)
    branch_got = swap(branch_send, x_mask)
    down_z = swap(down_z_send, z_near)
    middle_grad = cotangent + norm_backward(middle, row_mine + row_got.astype(F32))

    attended_grad = middle_grad.astype(BF16)
    attended_pair = (attended_grad, exchange(attended_grad, 1))
    modulate_grad, query_grad, key_grad, value_grad, state_grad = run(
        mixed_back_kernel, "mixed_back", spots,
        [
            (attended_pair[0], "rows"), (attended_pair[1], "rows"), (mixed, "pair"),
            (modulate, "pair"), (queries, "pair"), (query_pre, "pair"), (keys, "pair"),
            (values, "pair"), (mask_wide, "pair"), (cosine, "whole"), (sine, "whole"),
            (query_decay, "whole"), (decay_grid, "whole"), (decay_grid_t, "whole"),
            *state_inputs, *output_inputs,
        ],
        [
            (chip_shape, BF16, "pair"), (chip_shape, BF16, "pair"), (chip_shape, BF16, "pair"),
            (chip_shape, BF16, "pair"), (state_shape, BF16, "rows"),
        ],
        [wide_scratch, held_scratch, dma((members,)), dma((4,))],
        steps, 2 * square_flops,
    )
    state_grad, lift_y, gated = tie(state_grad, lift_y, gated)
    near = bulk // 2
    scan = Carry(state_grad, block_decay, True)
    scan.spread()

    def square(name, order, a, *grads):
        shape = (half, len(grads), rows, cols)
        return run(
            functools.partial(outer_kernel, order), name, spots,
            [(a[0], "whole"), (a[1], "whole"), *[(g, "whole") for g in grads]],
            [(shape, BF16, "any"), (shape, BF16, "any")],
            [pltpu.VMEM((len(grads), width, inner_width), BF16), dma((len(grads), members))],
            1, len(grads) * square_flops,
        )

    output_keep, output_send = square("output_outer", 1, attended_pair, gated)
    query_keep, query_send = square("query_outer", 0, normed_pair, query_grad, modulate_grad)
    *scan.got, gate_y, down_z, branch_got, query_keep, query_send, output_keep, output_send = tie(
        *scan.got, gate_y, down_z, branch_got, query_keep, query_send, output_keep, output_send
    )
    layer_output = (middle + mask_rows * (branch_mine + branch_got.astype(F32))).astype(BF16)
    down_g = jnp.moveaxis(fold(down_g[:, 0], down_z), 1, 0)
    for m in z_far[:0:-1]:
        size = down_g.shape[0] // 2
        down_g = fold(down_g[:size], swap(down_g[size:], m))
    gl_g = jnp.stack([fold(gate_g[0], gate_y), fold(lift_g[0], lift_y)], axis=1)

    query_y, output_x = swap(query_send[:, :1], y_mask), swap(output_send, x_mask)

    def backward_step(step, got):
        if step == 1:
            got, mod_send = tie(got, query_send[:, 1:])
            held["more"] = swap(mod_send, y_mask)
        if step == 2:
            got, held["y"], held["more"], held["x"] = tie(got, query_y, held["more"], output_x)
        return got

    scan.along(backward_step)
    query_y = jnp.concatenate([held["y"], held["more"]], axis=1)
    scan.before, down_g, gl_g = tie(scan.before, down_g, gl_g)
    down_far = swap(down_g[1], z_far[0])
    gl_z = swap(gl_g[near:], z_near)
    later_parts = list(tie(*scan.back()))
    query_keep, output_keep = tie(query_keep, output_keep, *later_parts)[:2]
    query_g, output_g = fold(query_keep, query_y), fold(output_keep, held["x"])
    quad = half // 2
    query_x, output_y = swap(query_g[quad:], x_mask), swap(output_g[quad:], y_mask)
    later_inputs = [(p, "any") for p in later_parts]
    quad = half // 2
    def far_folds(x):
        for m in reversed(z_far):
            size = x.shape[0] // 2
            x = (fold if size > 1 else final)(x[:size], swap(x[size:], m))
        return x

    key_out, value_out = run(
        key_back_kernel, "key_back", spots,
        [
            (key_grad, "pair"), (value_grad, "pair"), (keys, "pair"), (values, "pair"),
            (key_pre, "pair"), (mask_wide, "pair"), (cosine, "whole"), (sine, "whole"),
            (key_decay, "whole"), *later_inputs,
        ],
        [(chip_shape, BF16, "pair"), (chip_shape, BF16, "pair")],
        [held_scratch, dma((4,))],
        steps, square_flops // 2,
    )
    part_shape = (half, 1, rows, cols)
    key_keep, key_send, value_keep, value_send = run(
        functools.partial(outer_pair_kernel, (0, 1)), "key_value_outer", spots,
        [
            (normed_pair[0], "whole"), (normed_pair[1], "whole"), (key_out, "whole"),
            (value_out, "whole"),
        ],
        [(part_shape, BF16, "any")] * 4,
        [pltpu.VMEM((2, width, inner_width), BF16), dma((2, members))],
        1, 2 * square_flops,
    )
    key_send, value_send, gl_z, down_far, query_x, output_y = tie(
        key_send, value_send, gl_z, down_far, query_x, output_y
    )
    down_g = fold(down_g[0], down_far)
    gl_g = fold(gl_g[:near], gl_z)
    for m in z_far[:0:-1]:
        size = gl_g.shape[0] // 2
        gl_g = fold(gl_g[:size], swap(gl_g[size:], m))
    gl_far = swap(gl_g[1], z_far[0])
    key_y, value_x = swap(key_send, y_mask), swap(value_send, x_mask)
    key_out, value_out = tie(key_out, value_out, key_send, value_send)[:2]
    near_rows, far_rows = run(
        rows_kernel, "rows", spots,
        [
            (query_grad, "pair"), (modulate_grad, "pair"), (key_out, "pair"),
            (value_out, "pair"), (query_parts[0], "any"), (query_parts[1], "any"),
            (key_parts[0], "any"), (key_parts[1], "any"),
            (value_parts[0], "any"), (value_parts[1], "any"),
        ],
        [(row_shape, F32, "rows"), (row_shape, BF16, "rows")],
        [wide_scratch] * 4 + [dma((4, members))],
        steps, 4 * square_flops,
    )
    qmo_g = jnp.concatenate(
        [fold(query_g[:quad], query_x), fold(output_g[:quad], output_y)], axis=1
    )
    qmo_z = swap(qmo_g[near:], z_near)
    key_y, value_x, near_rows = tie(key_y, value_x, near_rows)
    down_y = swap(down_g[1], y_mask)
    key_g, value_g = fold(key_keep, key_y), fold(value_keep, value_x)
    key_x, value_y = swap(key_g[quad:], x_mask), swap(value_g[quad:], y_mask)
    key_x, value_y, down_y, qmo_z, gl_far = tie(key_x, value_y, down_y, qmo_z, gl_far)
    gate_lift = final(gl_g[0], gl_far)
    kv_g = jnp.concatenate([fold(key_g[:quad], key_x), fold(value_g[:quad], value_y)], axis=1)
    kv_z = swap(kv_g[near:], z_near)
    qmo_g = far_folds(fold(qmo_g[:near], qmo_z))[0]
    key_gradient, value_gradient = far_folds(fold(kv_g[:near], kv_z))[0]
    query_gradient, modulate_gradient, output_gradient = qmo_g
    down_gradient = final(down_g[0], down_y).T
    gate_gradient, lift_gradient = gate_lift[0].T, gate_lift[1].T
    input_gradient = middle_grad + norm_backward(input_rows, core_sum(near_rows, far_rows))
    return (
        layer_output,
        input_gradient,
        query_gradient,
        key_gradient,
        value_gradient,
        modulate_gradient,
        output_gradient,
        gate_gradient,
        lift_gradient,
        down_gradient,
    )


def solution(mesh):
    placed = (
        P(None, ("wide", "narrow"), None),
        P("wide", "narrow"),
        P("wide", "narrow"),
        P("wide", "narrow"),
        P("wide", "narrow"),
        P("wide", "narrow"),
        P(None, ("wide", "narrow")),
        P(None, ("wide", "narrow")),
        P(None, ("wide", "narrow")),
        P("narrow"),
        P(),
        P(None, ("wide", "narrow"), None),
    )
    return jax.shard_map(
        on_device,
        mesh=mesh,
        in_specs=placed,
        out_specs=(
            P(None, ("wide", "narrow"), None),
            P(None, ("wide", "narrow"), None),
            P("wide", "narrow"),
            P("wide", "narrow"),
            P("wide", "narrow"),
            P("wide", "narrow"),
            P("wide", "narrow"),
            P(None, ("wide", "narrow")),
            P(None, ("wide", "narrow")),
            P(None, ("wide", "narrow")),
        ),
        check_vma=False,
    )
```
